32 devices in a mesh: section: 4 (over x, core), dp: 8 (over z, y).
Axes of the slice: x: 2, y: 2, z: 4, core: 2. Of those that a mesh axis runs over, the one named last changes fastest.
Arguments:
- tokens: bfloat16 [16384, 512], P('dp'), may hold values from -6 to 6
- segment_ids: int32 [16, 1024], P('dp'), may hold values from 0 to 3, never falling along the last dimension, each value on 1 to 512 neighbouring positions
- live_mask: int32 [16, 1024], P('dp'), may hold values from 0 to 1, as said below
- cotangent: bfloat16 [16384, 512], P('dp'), may hold values from -6 to 6
- project_in: bfloat16 [2, 512, 1536], replicated, may hold values from -0.25 to 0.25
- project_out: bfloat16 [2, 512, 512], replicated, may hold values from -1 to 1
- up_weight: bfloat16 [2, 512, 2048], replicated, may hold values from -0.25 to 0.25
- up_bias: float32 [2, 2048], replicated, may hold values from -2 to 2
- down_weight: bfloat16 [2, 2048, 512], replicated, may hold values from -0.125 to 0.125
- down_bias: float32 [2, 512], replicated, may hold values from -2 to 2
- norm_gain: float32 [2, 2, 512], replicated, may hold values from 0.1 to 1.9
- norm_shift: float32 [2, 2, 512], replicated, may hold values from -2 to 2
Outputs:
- mixed_out: bfloat16 [16384, 512], P('dp', 'section')
- grad_tokens: bfloat16 [16384, 512], P('dp', 'section')
- grad_project_in: float32 [2, 512, 1536], P(None, 'dp')
- grad_project_out: float32 [2, 512, 512], P(None, 'dp')
- grad_up_weight: float32 [2, 512, 2048], P(None, 'dp')
- grad_up_bias: float32 [2, 2048], P(None, 'dp')
- grad_down_weight: float32 [2, 2048, 512], P(None, 'dp')
- grad_down_bias: float32 [2, 512], P(None, 'dp')
- grad_norm_gain: float32 [2, 2, 512], P(None, None, 'dp')
- grad_norm_shift: float32 [2, 2, 512], P(None, None, 'dp')
The draws below stay inside these ranges and needn't reach their ends.
Inputs may be any that keep to these rules, and one draw needn't show every extreme that they name: `segment_ids`: never falls along a row. `live_mask`: padding stands only at the end of a row.
All inputs are finite; a program needn't handle non-finite values.
Results may differ from the reference program's by a relative error of at most 0.019.
Values may be sent and summed in bfloat16 or wider, within the bound.
No kernel may reach another device: no remote copies, remote signals or barrier semaphores. Data moves between devices by JAX's collectives and lax.ppermute only.
A program may use at most 384 MiB of HBM per device.

```python
import math
import jax
import jax.numpy as jnp
import numpy as np
from jax import lax

D = 512
H = 8
FF = 2048
SEQ = 1024
TOKENS = 16384
ROWS = 16
N_SECTION = 4
N_DP = 8


def draw_live_mask(key, part):
    key = jax.random.fold_in(key, 7)
    padding = jax.random.randint(key, (ROWS, 1), 0, SEQ // 8 + 1)
    places = jnp.arange(SEQ)[None, :]
    return (places < SEQ - padding).astype(jnp.int32)


def levels(rng, shape, shards, low, top_value):
    loudness = 1.0
    for dim, parts in shards:
        heights = jax.random.uniform(jax.random.fold_in(jax.random.fold_in(rng, 6), dim), (parts,), jnp.float32, low / len(shards), top_value / len(shards))
        loudness = loudness * jnp.repeat(jnp.exp(heights), shape[dim] // parts).reshape((-1,) + (1,) * (len(shape) - 1 - dim))
    return loudness


def split_up(amount, total, reach, skew):
    weights = [(1 << 20) // math.isqrt(rank ** skew) + 1 for rank in range(2, amount + 1)]
    spare, given = total - reach - (amount - 1), [1] * (amount - 1)
    while spare > 0:
        movable = [i for i in range(amount - 1) if given[i] < reach]
        mass, budget = sum([weights[i] for i in movable]), spare
        for i in movable:
            extra = min(reach - given[i], max(1, budget * weights[i] // mass), spare)
            given[i] = given[i] + extra
            spare = spare - extra
    return np.array([reach] + given)


def uneven_parts(own_key, amount, total, most, skew):
    if amount == 2:
        one = jax.random.randint(own_key, (), max(1, total - most), min(most, total - 1) + 1)
        return jnp.stack([one, total - one])
    sizes = jnp.asarray(split_up(amount, total, most, skew), jnp.int32)
    twos = (amount - 1) // 2
    source_of, receiver = sizes[1:1 + 2 * twos:2], sizes[2:2 + 2 * twos:2]
    margin = jnp.minimum(source_of - 1, most - receiver)
    shifted = jax.random.randint(jax.random.fold_in(own_key, 1), (twos,), 0, 1 << 20) % (margin + 1)
    sizes = sizes.at[1:1 + 2 * twos:2].set(source_of - shifted).at[2:2 + 2 * twos:2].set(receiver + shifted)
    return sizes[jax.random.permutation(jax.random.fold_in(own_key, 2), amount)]


def gaussian(own_key, extent, scale, most, pieces=(), kind=jnp.bfloat16):
    values = scale * jax.random.normal(own_key, extent, jnp.float32)
    if pieces:
        values = values * levels(own_key, extent, pieces, -0.22, 0.18)
    return jnp.clip(values, -most, most).astype(kind)


def setup_inputs(seed: int = 0) -> dict:
    splits = jax.random.split(jax.random.key(seed), 13)
    return {
        "tokens": gaussian(splits[0], (TOKENS, D), 1.0, 6.0, ((0, 8),)),
        "segment_ids": jax.vmap(lambda own: jnp.searchsorted(jnp.cumsum(uneven_parts(own, 4, SEQ, SEQ // 2, 0)), jnp.arange(SEQ), side="right"))(jax.random.split(splits[1], ROWS)).reshape((ROWS, SEQ)).astype(jnp.int32),
        "live_mask": draw_live_mask(jax.random.fold_in(splits[12], 71), 0),
        "cotangent": gaussian(splits[3], (TOKENS, D), 1.0, 6.0, ((0, 8),)),
        "project_in": gaussian(splits[4], (2, D, 3 * D), D ** -0.5, 0.25),
        "project_out": gaussian(splits[5], (2, D, D), (D // 16) ** -0.5, 1.0),
        "up_weight": gaussian(splits[6], (2, D, FF), D ** -0.5, 0.25),
        "up_bias": gaussian(splits[7], (2, FF), 0.3, 2.0, (), jnp.float32),
        "down_weight": gaussian(splits[8], (2, FF, D), FF ** -0.5, 0.125),
        "down_bias": gaussian(splits[9], (2, D), 0.3, 2.0, (), jnp.float32),
        "norm_gain": jnp.clip(1.0 + 0.18 * jax.random.normal(splits[10], (2, 2, D), jnp.float32), 0.1, 1.9),
        "norm_shift": gaussian(splits[11], (2, 2, D), 0.3, 2.0, (), jnp.float32),
    }


@jax.custom_vjp
def low(v):
    return lax.optimization_barrier(v.astype(jnp.bfloat16)).astype(jnp.float32)

@jax.custom_vjp
def low_back(v):
    return v

def low_keep(v):
    return (low(v), None)

def low_pass(kept, grad):
    return (grad,)

def back_keep(v):
    return (v, None)

def back_low(kept, grad):
    return (low(grad),)
low.defvjp(low_keep, low_pass)
low_back.defvjp(back_keep, back_low)
highest = lax.Precision.HIGHEST
masked_score = -1e+30

def product(first_operand, second_operand):
    return jnp.dot(first_operand, second_operand, precision=highest, preferred_element_type=jnp.float32)

def layer_norm(values, norm_scale, norm_bias):
    center = values - lax.optimization_barrier(jnp.mean(values, axis=-1, keepdims=True))
    spread = lax.optimization_barrier(jnp.mean(center * center, axis=-1, keepdims=True))
    return center * lax.rsqrt(spread + 1e-05) * norm_scale + norm_bias

def attend_row(packed):
    merged_row, segment_row, live_row = packed
    heads_all = merged_row.reshape(SEQ, 3, H, D // H)
    queries = heads_all[:, 0]
    keys_all = heads_all[:, 1]
    values_all = heads_all[:, 2]
    scores = jnp.einsum('qhd,khd->hqk', queries, keys_all, precision=highest, preferred_element_type=jnp.float32) * (D // H) ** (-0.5)
    places = jnp.arange(SEQ)
    allowed = (segment_row[:, None] == segment_row[None, :]) & ((live_row[None, :] == 1) | (places[:, None] == places[None, :]))
    scores = low_back(jnp.where(allowed[None], scores, masked_score))
    attn_low = low(jax.nn.softmax(scores, axis=-1))
    mixture = jnp.einsum('hqk,khd->qhd', attn_low, values_all, precision=highest, preferred_element_type=jnp.float32)
    return mixture.reshape(SEQ, D)

def layer(inputs, segment_rows, live_rows, weights_one):
    project_in, project_out, up_weight, up_bias, down_weight, down_bias, norm_gain, norm_shift = weights_one
    entry = low_back(inputs)
    merged_rows = low(low_back(product(entry, project_in)))
    rows_here = segment_rows.shape[0]
    mixture = lax.map(jax.checkpoint(attend_row), (merged_rows.reshape(rows_here, SEQ, 3 * D), segment_rows, live_rows))
    mixture = low(low_back(mixture.reshape(rows_here * SEQ, D)))
    summed = entry + low_back(product(mixture, project_out))
    normed = layer_norm(summed, norm_gain[0], norm_shift[0])
    hidden = low_back(product(low(normed), up_weight) + up_bias)
    active = low(jax.nn.gelu(hidden, approximate=True))
    branch = low_back(product(active, down_weight) + down_bias)
    return low(layer_norm(normed + branch, norm_gain[1], norm_shift[1]))

def reference(tokens, segment_ids, live_mask, cotangent, project_in, project_out, up_weight, up_bias, down_weight, down_bias, norm_gain, norm_shift):
    weights_all = tuple((element.astype(jnp.float32) for element in (project_in, project_out, up_weight, up_bias, down_weight, down_bias, norm_gain, norm_shift)))
    group = math.gcd(ROWS, 4)
    blocks = ROWS // group
    token_blocks = tokens.astype(jnp.float32).reshape(blocks, group * SEQ, D)
    grad_blocks = cotangent.astype(jnp.float32).reshape(blocks, group * SEQ, D)
    segment_blocks = segment_ids.reshape(blocks, group, SEQ)
    live_blocks = live_mask.reshape(blocks, group, SEQ)

    def accumulate(totals, block_data):
        inputs, grad_out, segment_rows, live_rows = block_data

        def forward(values, params):
            current = values
            for position in range(N_SECTION):
                chosen = tuple((element[position % 2] for element in params))
                current = layer(current, segment_rows, live_rows, chosen)
            return current
        result, pullback = jax.vjp(forward, inputs, weights_all)
        grad_input, grad_params = pullback(grad_out)
        totals = tuple((total + grad_part for total, grad_part in zip(totals, grad_params)))
        return (totals, (result, grad_input))
    zeros_all = tuple((jnp.zeros_like(element) for element in weights_all))
    totals, (results, grads_input) = lax.scan(accumulate, zeros_all, (token_blocks, grad_blocks, segment_blocks, live_blocks))
    scale_dp = 1.0 / N_DP
    mixed_out = results.reshape(TOKENS, D).astype(jnp.bfloat16)
    grad_tokens = grads_input.reshape(TOKENS, D).astype(jnp.bfloat16)
    return (mixed_out, grad_tokens, totals[0] * scale_dp, totals[1] * scale_dp, totals[2] * scale_dp, totals[3] * scale_dp, totals[4] * scale_dp, totals[5] * scale_dp, totals[6] * scale_dp, totals[7] * scale_dp)
```

```python
import jax
import jax.numpy as jnp
from jax import lax
from jax.experimental import pallas as pl
from jax.experimental.pallas import tpu as pltpu
from jax.sharding import PartitionSpec as P

H = 8
HD = 64
T = 512
SEGMENTS = 4
EVEN, MOST = 512, 768
SMALL = 16
EPS = 1e-05
MASKED = -1e30
SAFE = 2.0**60
ONES = 16
LOG2E = 1.4426950408889634
F32 = jnp.float32
BF16 = jnp.bfloat16
VMEM_BYTES = 60 * 1024 * 1024


def dot(a, b):
    return jnp.dot(a, b, preferred_element_type=F32)


def dot_nt(a, b):
    return lax.dot_general(a, b, (((1,), (1,)), ((), ())), preferred_element_type=F32)


def dot_tn(a, b):
    return lax.dot_general(a, b, (((0,), (0,)), ((), ())), preferred_element_type=F32)


def row_stats(values):
    center = values - jnp.mean(values, axis=-1, keepdims=True)
    spread = jnp.mean(center * center, axis=-1, keepdims=True)
    inverse = lax.rsqrt(spread + EPS)
    return center * inverse, inverse


def norm_back(grad, plain, inverse, gain):
    scaled = grad * gain
    return inverse * (
        scaled
        - jnp.mean(scaled, axis=-1, keepdims=True)
        - plain * jnp.mean(scaled * plain, axis=-1, keepdims=True)
    )


def column_sum(values):
    return jnp.sum(values, axis=0, keepdims=True)


def aligned(start, size):
    if isinstance(start, int):
        return pl.ds(start, size)
    return pl.ds(pl.multiple_of(start, size), size)


def head_mask(odd):
    lanes = lax.broadcasted_iota(jnp.int32, (1, 2 * HD), 1)
    low = jnp.where(lanes < HD, 1.0, 0.0)
    return (low * (1.0 - odd) + (1.0 - low) * odd).astype(BF16)


def staged(count, unrolled, first, rest):
    if unrolled:
        ready = first(0)
        for i in range(count):
            following = first(i + 1) if i + 1 < count else None
            rest(i, ready)
            ready = following
    else:

        @pl.loop(0, count)
        def _(i):
            rest(i, first(i))


WHOLE = pl.BlockSpec(memory_space=pltpu.VMEM)
AFAR = pl.BlockSpec(memory_space=pl.ANY)
SCALARS = pl.BlockSpec(memory_space=pltpu.SMEM)
PARAMS = pltpu.CompilerParams(vmem_limit_bytes=VMEM_BYTES)


def for_count(count, run):
    @pl.when(count <= EVEN)
    def _():
        run(EVEN)

    @pl.when(count > EVEN)
    def _():
        run(MOST)


def split_row(segments):
    length = segments.shape[-1]
    sizes = [jnp.sum((segments == v).astype(jnp.int32)) for v in range(SEGMENTS)]
    best_mask = jnp.int32(0)
    best_cost = jnp.int32(2 * length)
    for mask in range(1 << (SEGMENTS - 1)):
        with_first = sizes[0]
        for v in range(1, SEGMENTS):
            if mask >> (v - 1) & 1:
                with_first = with_first + sizes[v]
        cost = jnp.maximum(with_first, length - with_first)
        better = cost < best_cost
        best_mask = jnp.where(better, mask, best_mask)
        best_cost = jnp.where(better, cost, best_cost)
    return sizes, best_mask, best_cost


def group_targets(segments, half, sizes, mask):
    length = segments.shape[-1]
    start = jnp.int32(0)
    offset = jnp.int32(0)
    shift = jnp.full(segments.shape, 0, jnp.int32)
    for v in range(SEGMENTS):
        bit = jnp.int32(1) if v == 0 else lax.shift_right_logical(mask, v - 1) & 1
        inside = (bit == 1) == (half == 0)
        shift = jnp.where(segments == v, jnp.where(inside, offset - start, -4 * length), shift)
        start = start + sizes[v]
        offset = offset + jnp.where(inside, sizes[v], 0)
    return lax.broadcasted_iota(jnp.int32, segments.shape, 1) + shift


def one_hot(target, capacity):
    slots = lax.broadcasted_iota(jnp.int32, (capacity, target.shape[-1]), 0)
    return jnp.where(slots == target, 1.0, 0.0).astype(BF16)


def put_back(slots, values, core, own, other):
    half = own.shape[0]
    lanes = lax.broadcasted_iota(jnp.int32, (half, values.shape[0]), 1).astype(F32)
    for out, start in ((own, core * half), (other, (1 - core) * half)):
        column = slots[pl.ds(pl.multiple_of(start, half), half), 0:1]
        pick = jnp.where(column == lanes, 1.0, 0.0).astype(BF16)
        out[...] = dot(pick, values).astype(BF16)


BIG = ("w_in", "w_out", "w_up", "w_down")
KEPT = (
    ("x_kept", (MOST, T), BF16),
    ("qkv", (MOST, 3 * T), BF16),
    ("probs", (H, MOST, MOST), BF16),
    ("norms", (H, MOST), F32),
    ("mix_t", (T, MOST), BF16),
    ("s1", (MOST, T), F32),
    ("act", (MOST, 4 * T), BF16),
    ("gate", (MOST, 4 * T), BF16),
    ("s2", (MOST, T), F32),
)


def filled(ref, name, cap, *lead):
    if name == "probs":
        return ref.at[(*lead, slice(None), pl.ds(0, cap), pl.ds(0, cap))]
    if name in ("mix_t", "norms"):
        return ref.at[(*lead, slice(None), pl.ds(0, cap))]
    return ref.at[(*lead, pl.ds(0, cap), slice(None))]


def forward_kernel(positions, place, tokens, cotangent, segments, live, b_up, b_down, gain, shift, *refs):
    big = dict(zip(BIG, refs[:4]))
    names = [name for name, _, _ in KEPT]
    kept = dict(zip(names, refs[4:13]))
    own_last, other_last, g_first, counted, slots = refs[13:18]
    weights = dict(zip(BIG, refs[18:22]))
    held = dict(zip(names, refs[22:31]))
    row_x, row_g, allow, v_t, q_t, nrm, nlow, came, left, rows_came = refs[31:]
    row = place[0]
    half = place[1]
    length = segments.shape[1]
    own_rows = pl.ds(pl.multiple_of(row * length, length), length)
    load_x = pltpu.make_async_copy(tokens.at[own_rows], row_x, rows_came.at[0])
    load_g = pltpu.make_async_copy(cotangent.at[own_rows], row_g, rows_came.at[1])
    load_x.start()

    def weight_copy(i, layer):
        return pltpu.make_async_copy(big[BIG[i]].at[layer], weights[BIG[i]].at[layer], came.at[layer, i])

    for i in range(4):
        weight_copy(i, 0).start()
    load_g.start()
    for i in range(4):
        weight_copy(i, 1).start()

    seg = segments[pl.ds(row, 1), :]
    alive = live[pl.ds(row, 1), :]
    sizes, mask, cost = split_row(seg)
    target = group_targets(seg, half, sizes, mask)
    counted[0] = cost
    slots[...] = jnp.broadcast_to(target.astype(F32), (8, length)).T

    def run(cap):
        x_now, qkv, probs, norms, mix_t, s1, act, gate, s2 = (held[name] for name in names)

        def keep(name, position):
            i = names.index(name)
            return pltpu.make_async_copy(
                filled(held[name], name, cap), filled(kept[name], name, cap, position), left.at[i]
            )

        pick = one_hot(target, cap)
        load_x.wait()
        x_now[0:cap, :] = dot(pick, row_x[...]).astype(BF16)
        rows = lax.broadcasted_iota(jnp.int32, (8, length), 0)
        both = jnp.where(
            rows == 0, (seg + 1).astype(F32), jnp.where(rows == 1, alive.astype(F32), 0.0)
        ).astype(BF16)
        as_rows = dot_nt(both, pick)
        as_columns = dot_nt(pick, both)
        seg_row = as_rows[0:1, :]
        keys = lax.broadcasted_iota(jnp.int32, (cap, cap), 0)
        queries = lax.broadcasted_iota(jnp.int32, (cap, cap), 1)
        itself = keys == queries
        alive_key = (as_columns[:, 1:2] == 1.0) & (seg_row > 0.0)
        allowed = (seg_row == as_columns[:, 0:1]) & (alive_key | itself)
        allow[0:cap, 0:cap] = jnp.where(allowed, 1.0, 0.0).astype(BF16)
        load_g.wait()
        g_first[0:cap, :] = dot(pick, row_g[...]).astype(BF16)
        factor = HD**-0.5 * LOG2E
        tall = HD + ONES
        for i in range(H):
            v_t[i * tall + HD : (i + 1) * tall, 0:cap] = jnp.ones((ONES, cap), BF16)

        @pl.loop(0, positions)
        def _(position):
            layer = lax.rem(position, 2)

            def need(i):
                @pl.when(position < 2)
                def _():
                    weight_copy(i, layer).wait()

            def free(*which):
                @pl.when(position > 0)
                def _():
                    for name in which:
                        keep(name, position - 1).wait()

            keep("x_kept", position).start()
            need(0)
            free("qkv")

            for j in range(3):
                columns = slice(j * T, (j + 1) * T)
                merged = dot(x_now[0:cap, :], weights["w_in"][layer, :, columns])
                qkv[0:cap, columns] = (merged * factor if j == 0 else merged).astype(BF16)

            keep("qkv", position).start()
            values = qkv[0:cap, 2 * T : 3 * T].T
            for i in range(H):
                v_t[i * tall : i * tall + HD, 0:cap] = values[i * HD : (i + 1) * HD]
            q_t[:, 0:cap] = qkv[0:cap, 0:T].T
            free("probs", "norms", "mix_t")

            def score(i):
                at = i // 2 * (2 * HD) if isinstance(i, int) else lax.div(i, 2) * (2 * HD)
                keys = qkv[0:cap, aligned(T + at, 2 * HD)] * head_mask(i % 2)
                return dot(keys, q_t[aligned(at, 2 * HD), 0:cap])

            def mix(i, weight, sums):
                both = dot(v_t[aligned(i * tall, tall), 0:cap], weight)
                inverse = 1.0 / (both[HD : HD + 1] if sums is None else sums)
                mix_t[aligned(i * HD, HD), 0:cap] = (both[0:HD] * inverse).astype(BF16)
                return both[HD : HD + 1], inverse

            def plain_head(i, scores):
                weight = jnp.exp2(scores).astype(BF16) * allow[0:cap, 0:cap]
                probs[i, 0:cap, 0:cap] = weight
                sums, inverse = mix(i, weight, None)
                nrm[pl.ds(i, 1), 0:cap] = sums
                norms[pl.ds(i, 1), 0:cap] = inverse

            staged(H, cap == EVEN, score, plain_head)
            sums = nrm[0:H, 0:cap]
            outside = jnp.where((sums > 1.0 / SAFE) & (sums < SAFE), 0.0, 1.0)

            @pl.when(jnp.sum(outside) > 0.0)
            def _():
                @pl.loop(0, H)
                def _(i):
                    masked = jnp.where(allow[0:cap, 0:cap].astype(F32) > 0.0, score(i), MASKED)
                    weight = jnp.exp2(masked - jnp.max(masked, axis=0, keepdims=True))
                    probs[i, 0:cap, 0:cap] = weight.astype(BF16)
                    _, inverse = mix(i, weight.astype(BF16), column_sum(weight))
                    norms[pl.ds(i, 1), 0:cap] = inverse

            keep("probs", position).start()
            keep("norms", position).start()
            keep("mix_t", position).start()
            need(1)
            free("s1")
            summed = x_now[0:cap, :].astype(F32) + dot(mix_t[:, 0:cap].T, weights["w_out"][layer])
            s1[0:cap, :] = summed
            keep("s1", position).start()
            plain, _ = row_stats(summed)
            normed = plain * gain[layer, 0:1, :] + shift[layer, 0:1, :]
            nrm[0:cap, 0:T] = normed
            nlow[0:cap, :] = normed.astype(BF16)
            need(2)
            need(3)
            free("act", "gate")

            def raise_up(t):
                columns = aligned(t * T, T)
                return dot(nlow[0:cap, :], weights["w_up"][layer, :, columns])

            def activate(t, hidden):
                columns = aligned(t * T, T)
                v = hidden + b_up[pl.ds(layer, 1), columns]
                c0 = 0.7978845608028654
                c1 = c0 * 0.044715
                square = v * v
                half_one = 0.5 + 0.5 * jnp.tanh(v * (c0 + c1 * square))
                active = v * half_one
                act[0:cap, columns] = active.astype(BF16)
                slope = half_one + active * (1.0 - half_one) * (2.0 * c0 + 6.0 * c1 * square)
                gate[0:cap, columns] = slope.astype(BF16)

            staged(4, cap == EVEN, raise_up, activate)
            branch = dot(act[0:cap, :], weights["w_down"][layer])
            keep("act", position).start()
            keep("gate", position).start()
            free("s2")
            second = nrm[0:cap, 0:T] + (branch + b_down[pl.ds(layer, 1), :])
            s2[0:cap, :] = second
            keep("s2", position).start()
            plain2, _ = row_stats(second)
            keep("x_kept", position).wait()
            x_now[0:cap, :] = (plain2 * gain[layer, 1:2, :] + shift[layer, 1:2, :]).astype(BF16)

        put_back(slots, x_now[0:cap, :], half, own_last, other_last)
        for name in names[1:]:
            keep(name, positions - 1).wait()

    for_count(cost, run)


def forward(positions, place, tokens, cotangent, segments, live, weights):
    w_in, w_out, w_up, b_up, w_down, b_down, gain, shift = weights
    big = (w_in, w_out, w_up, w_down)
    length = segments.shape[1]

    def body(*refs):
        forward_kernel(positions, *refs)

    return pl.pallas_call(
        body,
        in_specs=[SCALARS, AFAR, AFAR] + [WHOLE] * 6 + [AFAR] * 4,
        out_specs=[AFAR] * len(KEPT) + [WHOLE, WHOLE, WHOLE, SCALARS, WHOLE],
        out_shape=[jax.ShapeDtypeStruct((positions,) + shape, kind) for _, shape, kind in KEPT]
        + [jax.ShapeDtypeStruct((length // 2, T), BF16)] * 2
        + [jax.ShapeDtypeStruct((MOST, T), BF16)]
        + [jax.ShapeDtypeStruct((1,), jnp.int32)]
        + [jax.ShapeDtypeStruct((length, 8), F32)],
        scratch_shapes=[pltpu.VMEM(w.shape, BF16) for w in big]
        + [pltpu.VMEM(shape, kind) for _, shape, kind in KEPT]
        + [
            pltpu.VMEM((length, T), BF16),
            pltpu.VMEM((length, T), BF16),
            pltpu.VMEM((MOST, MOST), BF16),
            pltpu.VMEM((H * (HD + ONES), MOST), BF16),
            pltpu.VMEM((T, MOST), BF16),
            pltpu.VMEM((MOST, max(T, MOST)), F32),
            pltpu.VMEM((MOST, T), BF16),
            pltpu.SemaphoreType.DMA((2, 4)),
            pltpu.SemaphoreType.DMA((len(KEPT),)),
            pltpu.SemaphoreType.DMA((2,)),
        ],
        compiler_params=PARAMS,
        cost_estimate=pl.CostEstimate(flops=60 * 10**9, bytes_accessed=1 << 20, transcendentals=0),
        name="forward",
    )(place, tokens, cotangent, segments, live, b_up, b_down, gain, shift, *big)


FFN_READ = ("s2", "s1", "w_down", "gate", "act", "w_up")
HEADS_READ = ("w_out", "mix_t", "norms", "qkv", "probs")
INPUT_READ = ("x_kept", "w_in")
READ = {
    "ffn": FFN_READ, "heads": HEADS_READ, "input": INPUT_READ, "attn": HEADS_READ + INPUT_READ,
}
FILLED = {"ffn": (0, 1), "heads": (3,), "input": (3, 2), "attn": (3, 2)}


def tile_parts(tile, ways):
    return tile.reshape(ways // 2, 2, T // ways, T)


def each(count, unrolled, body):
    if unrolled:
        for i in range(count):
            body(i)
    else:
        pl.loop(0, count)(body)


class Backward:
    def __init__(self, phases, ways, refs, cap):
        self.phases, self.ways, self.cap = phases, ways, cap
        self.__dict__.update(refs)
        self.wide = T // ways
        self.copies = {}
        self.waits = []
        self.filled_once = set()
        for layer in self.before:
            for which, (source, target) in self.before[layer].items():
                rows = pl.ds(0, source.shape[3])
                target = target.at[:, :, :, rows]
                copy = pltpu.make_async_copy(source, target, self.before_came.at[layer, which])
                self.copies["before", layer, which] = copy

    def start_reads(self, index):
        if index >= len(self.phases):
            return
        position, part = self.phases[index]
        names = list(READ[part])
        if part in ("attn", "heads") and (position, "ffn") not in self.phases:
            names = ["s1"] + names
        for name in names:
            sem = self.came.at[self.names.index(name)]
            source, target = self.sources[name], self.held[name]
            if name.startswith("w_"):
                source = source.at[position % 2]
            else:
                source = filled(source, name, self.cap, position)
                target = filled(target, name, self.cap)
            self.copies[name] = pltpu.make_async_copy(source, target, sem)
            self.copies[name].start()
        for i, (source, target) in enumerate(self.handed if part == "input" else ()):
            self.copies["handed", i] = pltpu.make_async_copy(source, target, self.hand.at[i])
            self.copies["handed", i].start()
        for which in FILLED[part]:
            if ("before", position % 2, which) in self.copies:
                self.copies["before", position % 2, which].start()

    def need(self, *names):
        for name in names:
            if name in self.copies:
                self.copies.pop(name).wait()

    def store(self, layer, which, index, value):
        if which in self.before.get(layer, {}) or (layer, which) in self.filled_once:
            value = value + self.grads[layer][which][index].astype(F32)
        self.grads[layer][which][index] = value.astype(BF16)

    def send(self, layer, which):
        source, sem = self.grads[layer][which], self.left.at[layer, which]
        self.filled_once.add((layer, which))
        if (layer, which) not in self.final:
            copy = pltpu.make_async_copy(source, self.results[layer, which], sem)
            copy.start()
        else:
            start = 0 if which < 2 or (layer, 0) not in self.keys else 2 * self.wide
            rows = pl.ds(start, source.shape[3])
            mine, other = (self.results[layer, role].at[:, :, :, rows] for role in ("mine", "other"))
            copy = pltpu.make_async_copy(source, mine, sem)
            other = pltpu.make_async_copy(source, other, sem)
            core = self.place[1]

            @pl.when(core == which % 2)
            def _():
                copy.start()

            @pl.when(core != which % 2)
            def _():
                other.start()

        self.waits.append(copy)

    def store_smalls(self):
        below = pl.ds(self.wide, self.extra)
        first, second = self.grads[0][2], self.grads[0][3]
        first[:, :, :, below, :] = jnp.zeros(first.shape[:3] + (self.extra, T), BF16)
        rows = lax.broadcasted_iota(jnp.int32, (self.extra, T), 0)
        for shard in range(self.ways):
            z, y = shard // 2, shard % 2
            lanes = shard * self.wide // 128 * 128
            ups = jnp.zeros((self.extra, T), F32)
            rest = jnp.zeros((self.extra, T), F32)
            for layer in range(2):
                start = shard * 4 * self.wide
                row = self.smalls[layer, start // T : start // T + 1, start % T : start % T + 4 * self.wide]
                row = jnp.concatenate([row, jnp.zeros((1, T - 4 * self.wide), F32)], axis=1)
                ups = jnp.where(rows == layer, row, ups)
                block = self.smalls[layer, :, lanes : lanes + 128]
                for i in range(5):
                    row = jnp.concatenate([block[4 + i : 5 + i], jnp.zeros((1, T - 128), F32)], axis=1)
                    rest = jnp.where(rows == 5 * layer + i, row, rest)
            second[y, 0, z, below, :] = ups.astype(BF16)
            second[y, 1, z, below, :] = rest.astype(BF16)

    def run(self):
        last_use = {}
        for index, (position, part) in enumerate(self.phases):
            last_use[position % 2, part] = index
        self.start_reads(0)
        self.start_reads(1)
        for index, (position, part) in enumerate(self.phases):
            getattr(self, part)(position)
            for which in FILLED[part]:
                if last_use[position % 2, part] == index:
                    self.send(position % 2, which)
                else:
                    self.filled_once.add((position % 2, which))
            self.start_reads(index + 2)
        for copy in self.waits:
            copy.wait()

    def ffn(self, position):
        cap, layer, wide, ways = self.cap, position % 2, self.wide, self.ways
        rows = slice(0, cap)
        smalls = self.smalls.at[layer]
        g = (self.entry if (position, "ffn") == self.phases[0] else self.g_now)[rows, :].astype(F32)
        self.need("s2")
        plain, inverse = row_stats(self.held["s2"][rows, :])
        smalls[6:7, :] += column_sum(g * plain)
        smalls[8:9, :] += column_sum(g)
        grad_f = norm_back(g, plain, inverse, self.gain[layer, 1:2, :])
        self.gf[rows, :] = grad_f
        grad_branch = grad_f.astype(BF16)
        self.gb[rows, :] = grad_branch
        smalls[4:5, :] += column_sum(grad_branch.astype(F32))
        self.need("s1")
        plain1, inverse1 = row_stats(self.held["s1"][rows, :])
        self.n1[rows, :] = plain1
        self.r1[rows, :] = inverse1
        low = (plain1 * self.gain[layer, 0:1, :] + self.shift[layer, 0:1, :]).astype(BF16)
        self.nl_t[:, rows] = low.T
        self.need("w_down", "gate", "act", "w_up", ("before", layer, 0), ("before", layer, 1))
        act, gate, w_down, w_up = (self.held[name] for name in ("act", "gate", "w_down", "w_up"))

        def lower(t):
            return dot_nt(self.gb[rows, :], w_down[aligned(t * T, T), :])

        def tile(t, da):
            columns = aligned(t * T, T)
            dh = (gate[rows, columns].astype(F32) * da).astype(BF16)
            gate[rows, columns] = dh
            smalls[pl.ds(t, 1), :] += column_sum(dh.astype(F32))
            parts = tile_parts(dot(self.nl_t[:, rows], dh), ways)
            few = ways // 8
            below = dot_tn(act[rows, columns], self.gb[rows, :]).reshape(few, 2, 2, 2 * wide, T)
            for y in range(2):
                self.store(layer, 0, (t // 2, y, slice(None), aligned(t % 2 * wide, wide)), parts[:, y])
                for x in range(2):
                    self.store(layer, 1, (y, x, pl.ds(t * few, few)), below[:, y, x])

        staged(4, cap == EVEN, lower, tile)
        self.gf[rows, :] = self.gf[rows, :] + dot_nt(gate[rows, :], w_up[...])
        if (position, "attn") not in self.phases:
            self.ends[0][rows, :] = self.gf[rows, :]

    def attn(self, position):
        self.heads(position)
        self.input(position)

    def heads(self, position):
        cap, layer, ways = self.cap, position % 2, self.ways
        rows = slice(0, cap)
        smalls = self.smalls.at[layer]
        if (position, "ffn") in self.phases:
            grad_normed = self.gf[rows, :]
            plain1, inverse1 = self.n1[rows, :], self.r1[rows, :]
        else:
            self.need("s1")
            grad_normed = self.entry[rows, :]
            plain1, inverse1 = row_stats(self.held["s1"][rows, :])
        smalls[5:6, :] += column_sum(grad_normed * plain1)
        smalls[7:8, :] += column_sum(grad_normed)
        grad_summed = norm_back(grad_normed, plain1, inverse1, self.gain[layer, 0:1, :])
        self.gf[rows, :] = grad_summed
        grad_attn = grad_summed.astype(BF16)
        self.need("w_out", "mix_t", ("before", layer, 3))
        mix_t, qkv, probs = (self.held[name] for name in ("mix_t", "qkv", "probs"))
        parts = tile_parts(dot(mix_t[:, rows], grad_attn), ways)
        for y in range(2):
            self.store(layer, 3, (y, 1, slice(None), pl.ds(0, self.wide)), parts[:, y])
        dmix_t, q_t, k_t, d_t = self.dmix_t, self.q_t, self.k_t, self.d_t
        self.need("norms")
        grad_mixture = dot_nt(self.held["w_out"][...], grad_attn)
        for i in range(H):
            own = slice(i * HD, (i + 1) * HD)
            dmix_t[own, rows] = (grad_mixture[own] * self.held["norms"][i : i + 1, rows]).astype(BF16)
        self.need("qkv")
        q_t[:, rows] = qkv[rows, 0:T].T
        k_t[:, rows] = qkv[rows, T : 2 * T].T
        self.need("probs")

        def grad_probs(i):
            at = i // 2 * (2 * HD) if isinstance(i, int) else lax.div(i, 2) * (2 * HD)
            values = qkv[rows, aligned(2 * T + at, 2 * HD)] * head_mask(i % 2)
            return dot(values, dmix_t[aligned(at, 2 * HD), rows])

        def head(i, dp):
            own = aligned(i * HD, HD)
            do = dmix_t[own, rows]
            delta = column_sum(do.astype(F32) * mix_t[own, rows].astype(F32))
            p = probs[i, rows, rows]
            ds = (p.astype(F32) * (dp - delta)).astype(BF16)
            d_t[own, rows] = (dot(k_t[own, rows], ds) * HD**-0.5).astype(BF16)
            own_k = aligned(T + i * HD, HD)
            d_t[own_k, rows] = (dot_nt(q_t[own, rows], ds) * (1.0 / LOG2E)).astype(BF16)
            own_v = aligned(2 * T + i * HD, HD)
            d_t[own_v, rows] = dot_nt(do, p).astype(BF16)

        staged(H, cap == EVEN, grad_probs, head)
        if self.phases[-1] == (position, "heads"):
            ends = ((self.gf.at[rows], self.ends[0].at[rows]), (d_t.at[:, rows], self.ends[1].at[:, rows]))
            for i, (source, target) in enumerate(ends):
                self.waits.append(pltpu.make_async_copy(source, target, self.hand.at[i]))
                self.waits[-1].start()

    def input(self, position):
        cap, layer, ways, d_t = self.cap, position % 2, self.ways, self.d_t
        rows = slice(0, cap)
        self.need("x_kept", "w_in", ("before", layer, 2), ("before", layer, 3))
        self.need(("handed", 0), ("handed", 1))
        x_t = self.held["x_kept"][rows, :].T
        for j in range(3):
            parts = tile_parts(dot_nt(x_t, d_t[j * T : (j + 1) * T, rows]), ways)
            for y in range(2):
                index = ((j, y) if j < 2 else (y, 0)) + (slice(None), pl.ds(0, self.wide))
                self.store(layer, 2 if j < 2 else 3, index, parts[:, y])
        if self.extra:
            self.store_smalls()
        g = (self.gf[rows, :] + dot(self.held["w_in"][...], d_t[:, rows]).T).astype(BF16)
        if self.last:
            put_back(self.slots[0], g, self.place[1], *(end.at[0] for end in self.ends))
            for end, earlier in zip(self.ends, self.slots[1:]):
                end[1] = earlier[...]
        else:
            self.g_now[rows, :] = g
            if (position, "attn") == self.phases[-1]:
                self.ends[0][rows, :] = g


def backward(phases, ways, place, count, entry, smalls, given, before, final, after=(), extra=0):
    parts = [part for _, part in phases]
    first_part, last_part = parts[0], parts[-1]
    names = ["s1"] if first_part in ("heads", "attn") else []
    for part in parts:
        names += [name for name in READ[part] if name not in names]
    shapes = {name: (shape, kind) for name, shape, kind in KEPT}
    for name in BIG:
        shapes[name] = (given[name].shape[1:], BF16)
    wide = T // ways
    packed = {}
    for position, part in phases:
        for which in sorted(FILLED[part]):
            packed[position % 2, which] = (2, 2, ways // 2, (2 if which < 2 else 1) * wide, T)
    olds = [(layer, which) for layer in before for which in before[layer]]
    n, keys = len(names), list(packed)
    extra_rows = extra
    if extra:
        for key in ((0, 2), (0, 3)):
            packed[key] = packed[key][:3] + (wide + extra, T)
    made = {}
    for layer, which in keys:
        if (layer, which) not in final:
            made[layer, which] = packed[layer, which]
        elif which in (0, 2):
            rows = packed[layer, which][3] + (made[layer, "mine"][3] if (layer, "mine") in made else 0)
            for role in ("mine", "other"):
                made[layer, role] = (2, 2, ways // 2, rows, T)
    last = phases[-1] in ((0, "input"), (0, "attn"))
    half = given["slots"][0].shape[0] // 2
    entries = [] if first_part == "input" else [entry]
    handed = list(entry) if first_part == "input" else []

    def body(place, count, gain, shift, *refs):
        refs = list(refs)

        def cut(amount):
            part = refs[:amount]
            del refs[:amount]
            return part

        entry_refs = cut(len(entries))
        smalls_in = cut(0 if smalls is None else 1)
        slots = cut(3 if last else 0)
        handed_refs = cut(len(handed))
        cut(len(after))

        def by_layer(keys, values):
            table = {}
            for (layer, which), value in zip(keys, values):
                table.setdefault(layer, {})[which] = value
            return table

        sources = dict(zip(names, cut(n)))
        olds_hbm = by_layer(olds, cut(len(olds)))
        results = dict(zip(made, cut(len(made))))
        smalls_out = cut(1)[0]
        end_refs = cut(len(ends))
        held = dict(zip(names, cut(n)))
        grads = by_layer(keys, cut(len(keys)))
        work = ("g_now", "gf", "gb", "n1", "r1", "nl_t", "dmix_t", "q_t", "k_t", "d_t")
        sems = ("came", "before_came", "left", "hand")
        table = dict(zip(work + sems, cut(len(work) + len(sems))))
        table.update(
            place=place, gain=gain, shift=shift, smalls=smalls_out, ends=end_refs,
            entry=entry_refs[0] if entry_refs else None, slots=slots, last=last, extra=extra_rows,
            handed=[],
            names=names, sources=sources, held=held, grads=grads, results=results, final=final, keys=keys,
            before={
                layer: {which: (ref, grads[layer][which]) for which, ref in olds_hbm[layer].items()}
                for layer in olds_hbm
            },
        )
        smalls_out[...] = smalls_in[0][...] if smalls_in else jnp.zeros(smalls_out.shape, F32)

        def run(cap):
            own = dict(table)
            if handed_refs:
                rows = pl.ds(0, cap)
                own["handed"] = [
                    (handed_refs[0].at[rows], table["gf"].at[rows]),
                    (handed_refs[1].at[:, rows], table["d_t"].at[:, rows]),
                ]
            Backward(phases, ways, own, cap).run()

        for_count(count[0], run)

    extras = ([] if smalls is None else [smalls]) + (list(given["slots"]) if last else [])
    end_spec = [WHOLE]
    if last:
        ends = [jax.ShapeDtypeStruct((2, half, T), BF16)] * 2
        end_spec = [WHOLE, WHOLE]
    elif last_part == "heads":
        ends = [jax.ShapeDtypeStruct((MOST, T), F32), jax.ShapeDtypeStruct((3 * T, MOST), BF16)]
        end_spec = [AFAR, AFAR]
    else:
        ends = [jax.ShapeDtypeStruct((MOST, T), F32 if last_part == "ffn" else BF16)]
    costs = {"attn": 14e9, "ffn": 10e9, "heads": 10e9, "input": 4e9}
    flops = sum(costs[part] for part in parts)
    outs = pl.pallas_call(
        body,
        in_specs=[SCALARS, SCALARS]
        + [WHOLE] * (2 + len(entries) + len(extras))
        + [AFAR] * (len(handed) + len(after) + n + len(olds)),
        out_specs=[AFAR] * len(made) + [WHOLE] + end_spec,
        out_shape=[jax.ShapeDtypeStruct(shape, BF16) for shape in made.values()]
        + [jax.ShapeDtypeStruct((2, SMALL, T), F32)]
        + ends,
        scratch_shapes=[pltpu.VMEM(*shapes[name]) for name in names]
        + [pltpu.VMEM(packed[key], BF16) for key in keys]
        + [
            pltpu.VMEM((MOST, T), BF16),
            pltpu.VMEM((MOST, T), F32),
            pltpu.VMEM((MOST, T), BF16),
            pltpu.VMEM((MOST, T), F32),
            pltpu.VMEM((MOST, 1), F32),
            pltpu.VMEM((T, MOST), BF16),
            pltpu.VMEM((T, MOST), BF16),
            pltpu.VMEM((T, MOST), BF16),
            pltpu.VMEM((T, MOST), BF16),
            pltpu.VMEM((3 * T, MOST), BF16),
            pltpu.SemaphoreType.DMA((n,)),
            pltpu.SemaphoreType.DMA((2, 4)),
            pltpu.SemaphoreType.DMA((2, 4)),
            pltpu.SemaphoreType.DMA((2,)),
        ],
        compiler_params=PARAMS,
        cost_estimate=pl.CostEstimate(flops=int(flops), bytes_accessed=1 << 20, transcendentals=0),
        name="backward_" + "_".join(f"{part}{position}" for position, part in phases),
    )(
        place, count, given["gain"], given["shift"], *entries, *extras, *handed, *after,
        *[given[name] for name in names], *[before[layer][which] for layer, which in olds],
    )
    table = dict(zip(made, outs))
    outs = outs[len(made) :]
    return table, outs[0], outs[1] if len(ends) == 1 else outs[1:]


def swap(block, pairs):
    return lax.ppermute(block, ("section", "dp"), pairs)


class Links:
    def __init__(self):
        self.sections = lax.axis_size("section")
        self.ways = lax.axis_size("dp")
        section = lax.axis_index("section")
        self.me = lax.axis_index("dp")
        self.core, self.x, y = section % 2, section // 2, self.me % 2
        self.bits = (self.ways // 2).bit_length() - 1
        one = jnp.where(self.core == 0, self.x, y)
        two = jnp.where(self.core == 0, y, self.x)
        low_first = [self.me // (2 << i) % 2 for i in range(self.bits)]
        self.halves = [one, two] + low_first
        self.token = None

    def pairs(self, partner):
        every = [(s, d) for s in range(self.sections) for d in range(self.ways)]
        return [
            (s * self.ways + d, partner(s, d)[0] * self.ways + partner(s, d)[1]) for s, d in every
        ]

    def in_dp(self, bits):
        return self.pairs(lambda s, d: (s, d ^ bits))

    def in_section(self, bits):
        return self.pairs(lambda s, d: (s ^ bits, d))

    def step(self, i):
        if i == 0:
            return self.pairs(lambda s, d: (s ^ 2, d) if s % 2 == 0 else (s, d ^ 1))
        if i == 1:
            return self.pairs(lambda s, d: (s, d ^ 1) if s % 2 == 0 else (s ^ 2, d))
        return self.in_dp(1 << (i - 1))

    def place(self, gives, steps_done, ndim):
        order = [0, 1] + list(range(self.bits + 1, 1, -1))
        return [gives[axis] if axis < len(gives) else None for axis in order if axis >= steps_done]

    def sum(self, terms):
        total = 0.0
        for array, index in terms:
            for dim in reversed(range(len(index))):
                if index[dim] is not None:
                    kind, axis = index[dim]
                    half = self.halves[axis]
                    at = half if kind == "keep" else 1 - half
                    array = lax.dynamic_index_in_dim(array, at, dim, keepdims=False)
            total = total + array.astype(F32)
        return total

    def ordered(self, total):
        if self.token is not None:
            row = lax.slice(self.token, (0,) * self.token.ndim, (1,) * (self.token.ndim - 1) + (T,))
            total = total + jnp.minimum(jnp.abs(row.reshape(T).astype(F32)), 0.0)
        self.token = total.astype(BF16)
        return self.token


class Group:
    def __init__(self, links, mine=None, other=None, groups=()):
        self.links, self.done = links, 0
        if groups:
            self.done = groups[0].done
            self.parts = [part for group in groups for part in group.parts]
        else:
            shape = (2, 2) + (2,) * links.bits + mine.shape[3:]
            came = swap(other, links.in_section(1))
            self.parts = [[(mine.reshape(shape), 0), (came.reshape(shape), 0)]]
        self.joint = []

    def sum(self, wanted):
        def of(have):
            return self.links.sum(
                [(array, self.links.place(wanted, done, array.ndim)) for array, done in have]
            )

        sums = [of(part) for part in self.parts]
        total = sums[0] if len(sums) == 1 else jnp.concatenate(sums, axis=-2)
        return total + of(self.joint) if self.joint else total

    def keeps(self):
        return [("keep", i) for i in range(self.done)]

    def give(self):
        give = self.links.ordered(self.sum(self.keeps() + [("give", self.done)]))
        came = swap(give, self.links.step(self.done))
        self.done += 1
        (self.joint if len(self.parts) > 1 else self.parts[0]).append((came, self.done))
        return give

    def finished(self):
        return self.done == 2 + self.links.bits

    def total(self):
        return self.sum(self.keeps())


def to_sections(links, total):
    over = swap(total, links.in_section(2))
    beside = swap(total, links.in_section(1))
    return [total, beside, over, swap(over, links.in_section(1))]


def spread(links, own, other):
    came = swap(other, links.in_section(1))
    rows, width = own.shape[1], own.shape[2] // links.sections
    after = [] if links.token is None else [links.token]
    section = (2 * links.x + links.core).reshape(1)

    def body(section, own, came, *refs):
        for bits, out in enumerate(refs[len(after) :]):
            at = aligned((section[0] ^ bits) * width, width)
            for i in range(2):
                out[i] = (own[i, :, at].astype(F32) + came[i, :, at].astype(F32)).astype(BF16)

    gives = pl.pallas_call(
        body,
        in_specs=[SCALARS, WHOLE, WHOLE] + [AFAR] * len(after),
        out_specs=[WHOLE] * 4,
        out_shape=[jax.ShapeDtypeStruct((2, rows, width), BF16)] * 4,
        compiler_params=PARAMS,
        name="spread",
    )(section, own, came, *after)
    return [gives[0]] + [swap(gives[bits], links.in_section(bits)) for bits in (1, 2, 3)]


def gather_kernel(ways, extra, place, sums, *refs):
    blocks, pieces = refs[:4], (refs[4:8], refs[8:12])
    mixed_out, tokens_out, ins, out_proj, ups, up_bias, downs, down_bias, gains, shifts = refs[12:]
    scale = 1.0 / ways
    wide = T // ways
    section = 2 * place[0] + place[1]
    me = place[2]
    half = blocks[0].shape[1]

    def small_rows(layer, row, rest):
        up_bias[layer : layer + 1, :] = row[0:1, 0 : 4 * wide]
        down_bias[layer : layer + 1, :] = rest[0:1, 0:wide]
        gains[layer] = rest[1:3, 0:wide]
        shifts[layer] = rest[3:5, 0:wide]

    for at in range(4):

        @pl.when(section == at)
        def _(at=at):
            for s in range(4):
                rows = pl.ds(s * half, half)
                tokens_out[rows, :] = blocks[s ^ at][0]
                mixed_out[rows, :] = blocks[s ^ at][1]
            for layer in range(2):
                of = [pieces[layer][s ^ at] for s in range(4)]
                own = pl.ds(2 * wide, wide)
                for x in range(2):
                    for i in range(2):
                        rows = pl.ds(i * wide, wide)
                        columns = pl.ds((2 * x + i) * T, T)
                        ups[layer, :, columns] = of[2 * x][rows, :].astype(F32) * scale
                    below = pl.ds(2 * x * wide, 2 * wide)
                    downs[layer, below, :] = of[2 * x + 1][0 : 2 * wide, :].astype(F32) * scale
                    ins[layer, :, pl.ds(x * T, T)] = of[2 * x][own, :].astype(F32) * scale
                ins[layer, :, pl.ds(2 * T, T)] = of[1][own, :].astype(F32) * scale
                out_proj[layer] = of[3][own, :].astype(F32) * scale
            if extra:
                below = pl.ds(3 * wide, extra)
                row = pieces[0][1 ^ at][below, :].astype(F32) * scale
                rest = pieces[0][3 ^ at][below, 0:128].astype(F32) * scale
                turn = lax.rem(me * wide, 128)
                rest = pltpu.roll(rest, lax.rem(128 - turn, 128), 1)
                for layer in range(2):
                    small_rows(layer, row[layer : layer + 1], rest[5 * layer : 5 * layer + 5])

    if not extra:
        for layer in range(2):
            start = me * (4 * wide)
            row = sums[layer, pl.ds(lax.div(start, T), 1), :] * scale
            row = jnp.broadcast_to(row, (8, T))
            row = pltpu.roll(row, lax.rem(T - lax.rem(start, T), T), 1)
            rest = pltpu.roll(sums[layer] * scale, lax.rem(T - me * wide, T), 1)
            small_rows(layer, row, rest[4:9])


def gather(place, sums, blocks, pieces, ways, extra):
    wide = T // ways
    _, half, width = blocks[0].shape

    def body(*refs):
        gather_kernel(ways, extra, *refs)

    shapes = [
        (2, wide, 3 * T), (2, wide, T), (2, wide, 4 * T), (2, 4 * wide), (2, 4 * wide, T),
        (2, wide), (2, 2, wide), (2, 2, wide),
    ]
    return pl.pallas_call(
        body,
        in_specs=[SCALARS] + [WHOLE] * 13,
        out_specs=[WHOLE] * 10,
        out_shape=[jax.ShapeDtypeStruct((4 * half, width), BF16)] * 2
        + [jax.ShapeDtypeStruct(shape, F32) for shape in shapes],
        compiler_params=PARAMS,
        name="gather",
    )(place, sums, *blocks, *pieces[0], *pieces[1])


def finer(block, kind, ways):
    made = 2 * block.shape[2]
    cut = ways // made
    if cut == 1:
        return block
    z, rows = block.shape[2:4]
    if kind == "down":
        block = block.transpose(2, 0, 1, 3, 4).reshape(z, 2, cut // 2, 2, 2, rows // cut, T)
        block = block.transpose(3, 4, 0, 1, 2, 5, 6)
    elif kind == "right":
        block = block.reshape(2, 2, z, cut // 2, 2, rows // cut, T).transpose(4, 1, 2, 0, 3, 5, 6)
    else:
        tiles = 2 if kind == "up" else 1
        block = block.reshape(2, 2, z, tiles, cut // 2, 2, rows // tiles // cut, T)
        block = block.transpose(0, 5, 2, 1, 4, 3, 6, 7)
    return block.reshape(2, 2, ways // 2, rows // cut, T)


def finer_pair(links, arrays, kinds):
    mine, other = arrays
    if 2 * mine.shape[2] == links.ways:
        return arrays
    wide = T // (2 * mine.shape[2])

    def cut(block, which):
        parts, start = [], 0
        for kind in kinds:
            rows = (2 if kind[0] == "up" else 1) * wide
            parts.append(finer(block[:, :, :, start : start + rows], kind[which], links.ways))
            start += rows
        return jnp.concatenate(parts, axis=3)

    return (
        jnp.where(links.core == 0, cut(mine, 0), cut(mine, 1)),
        jnp.where(links.core == 0, cut(other, 1), cut(other, 0)),
    )


def on_device(
    tokens, segment_ids, live_mask, cotangent,
    project_in, project_out, up_weight, up_bias, down_weight, down_bias, norm_gain, norm_shift,
):
    ways = lax.axis_size("dp")
    positions = lax.axis_size("section")
    made = min(ways, T // 32)
    links = Links()
    place = jnp.stack([links.x, links.core, links.me]).astype(jnp.int32)
    weights = (
        project_in, project_out, up_weight, up_bias, down_weight, down_bias, norm_gain, norm_shift,
    )
    *kept, own, other, g, count, slots = forward(
        positions, place, tokens, cotangent, segment_ids, live_mask, weights
    )
    given = dict(zip((name for name, _, _ in KEPT), kept))
    given.update(
        w_in=project_in, w_out=project_out, w_up=up_weight, w_down=down_weight,
        gain=norm_gain, shift=norm_shift, slots=(slots, own, other),
    )
    extra = SMALL if made == ways else 0
    of_ffn, of_attn = ("up", "down"), ("left", "right")

    def group(arrays, layer, kinds):
        return Group(links, *finer_pair(links, (arrays[layer, "mine"], arrays[layer, "other"]), kinds))

    def back(phases, entry, smalls, before, final=(), after=(), extra=0):
        return backward(
            phases, made, place, count, entry, smalls, given, before, final, after, extra
        )

    early = [(3, "ffn"), (3, "attn"), (2, "ffn"), (2, "attn"), (1, "ffn")]
    grads, smalls, g = back(early, g, None, {}, ((1, 0), (1, 1)))
    ffn_1 = group(grads, 1, (of_ffn,))
    before = {1: {2: grads[1, 2], 3: grads[1, 3]}}
    attn, smalls, g = back([(1, "attn")], g, smalls, before, ((1, 2), (1, 3)))
    attn_1 = group(attn, 1, (of_attn,))
    after = [ffn_1.give()]
    before = {0: {0: grads[0, 0], 1: grads[0, 1]}}
    ffn, smalls, g = back([(0, "ffn")], g, smalls, before, ((0, 0), (0, 1)), after)
    ffn_0 = group(ffn, 0, (of_ffn,))
    after = [ffn_1.give(), attn_1.give()]
    before = {0: {3: grads[0, 3]}}
    heads, smalls, g = back([(0, "heads")], g, smalls, before, (), after)
    after = [attn_1.give(), ffn_0.give()]
    before = {0: {2: grads[0, 2], 3: heads[0, 3]}}
    attn, smalls, halves = back([(0, "input")], g, smalls, before, ((0, 2), (0, 3)), after, extra)
    attn_0 = group(attn, 0, (of_attn,))
    all_1 = Group(links, groups=(ffn_1, attn_1))
    all_1.give()
    attn_0.give()
    blocks = spread(links, *halves)
    ffn_0.give()
    while not all_1.finished():
        all_1.give()
        attn_0.give()
        ffn_0.give()
    pieces_1 = to_sections(links, links.ordered(all_1.total()))
    while not (attn_0.finished() and ffn_0.finished()):
        for last in (attn_0, ffn_0):
            if not last.finished():
                last.give()
    both = Group(links, groups=(ffn_0, attn_0))
    pieces_0 = to_sections(links, links.ordered(both.total()))
    if not extra:
        smalls = lax.psum(smalls, ("section", "dp"))
    return tuple(gather(place, smalls, blocks, (pieces_0, pieces_1), ways, extra))


def solution(mesh):
    rows = P("dp", None)
    in_specs = (rows,) * 4 + (P(),) * 8
    out_specs = (
        P("dp", "section"),
        P("dp", "section"),
        P(None, "dp", None),
        P(None, "dp", None),
        P(None, "dp", None),
        P(None, "dp"),
        P(None, "dp", None),
        P(None, "dp"),
        P(None, None, "dp"),
        P(None, None, "dp"),
    )
    return jax.shard_map(
        on_device, mesh=mesh, in_specs=in_specs, out_specs=out_specs, check_vma=False
    )
```

```python
import jax
import jax.numpy as jnp
from jax import lax
from jax.experimental import pallas as pl
from jax.experimental.pallas import tpu as pltpu
from jax.sharding import PartitionSpec as P

H = 8
HD = 64
T = 512
SEGMENTS = 4
EVEN, MOST = 512, 768
SMALL = 16
EPS = 1e-05
MASKED = -1e30
SAFE = 2.0**60
ONES = 16
LOG2E = 1.4426950408889634
F32 = jnp.float32
BF16 = jnp.bfloat16
VMEM_BYTES = 62 * 1024 * 1024


def dot(a, b):
    return jnp.dot(a, b, preferred_element_type=F32)


def dot_nt(a, b):
    return lax.dot_general(a, b, (((1,), (1,)), ((), ())), preferred_element_type=F32)


def dot_tn(a, b):
    return lax.dot_general(a, b, (((0,), (0,)), ((), ())), preferred_element_type=F32)


def row_stats(values):
    center = values - jnp.mean(values, axis=-1, keepdims=True)
    spread = jnp.mean(center * center, axis=-1, keepdims=True)
    inverse = lax.rsqrt(spread + EPS)
    return center * inverse, inverse


def norm_back(grad, plain, inverse, gain):
    scaled = grad * gain
    return inverse * (
        scaled
        - jnp.mean(scaled, axis=-1, keepdims=True)
        - plain * jnp.mean(scaled * plain, axis=-1, keepdims=True)
    )


def column_sum(values):
    return jnp.sum(values, axis=0, keepdims=True)


def aligned(start, size):
    if isinstance(start, int):
        return pl.ds(start, size)
    return pl.ds(pl.multiple_of(start, size), size)


def head_mask(odd):
    lanes = lax.broadcasted_iota(jnp.int32, (1, 2 * HD), 1)
    low = jnp.where(lanes < HD, 1.0, 0.0)
    return (low * (1.0 - odd) + (1.0 - low) * odd).astype(BF16)


def staged(count, unrolled, first, rest):
    if unrolled:
        ready = first(0)
        for i in range(count):
            following = first(i + 1) if i + 1 < count else None
            rest(i, ready)
            ready = following
    else:

        @pl.loop(0, count)
        def _(i):
            rest(i, first(i))


WHOLE = pl.BlockSpec(memory_space=pltpu.VMEM)
AFAR = pl.BlockSpec(memory_space=pl.ANY)
SCALARS = pl.BlockSpec(memory_space=pltpu.SMEM)
PARAMS = pltpu.CompilerParams(vmem_limit_bytes=VMEM_BYTES)


def for_count(count, run):
    @pl.when(count <= EVEN)
    def _():
        run(EVEN)

    @pl.when(count > EVEN)
    def _():
        run(MOST)


def split_row(segments):
    length = segments.shape[-1]
    sizes = [jnp.sum((segments == v).astype(jnp.int32)) for v in range(SEGMENTS)]
    best_mask = jnp.int32(0)
    best_cost = jnp.int32(2 * length)
    for mask in range(1 << (SEGMENTS - 1)):
        with_first = sizes[0]
        for v in range(1, SEGMENTS):
            if mask >> (v - 1) & 1:
                with_first = with_first + sizes[v]
        cost = jnp.maximum(with_first, length - with_first)
        better = cost < best_cost
        best_mask = jnp.where(better, mask, best_mask)
        best_cost = jnp.where(better, cost, best_cost)
    return sizes, best_mask, best_cost


def group_targets(segments, half, sizes, mask):
    length = segments.shape[-1]
    start = jnp.int32(0)
    offset = jnp.int32(0)
    shift = jnp.full(segments.shape, 0, jnp.int32)
    for v in range(SEGMENTS):
        bit = jnp.int32(1) if v == 0 else lax.shift_right_logical(mask, v - 1) & 1
        inside = (bit == 1) == (half == 0)
        shift = jnp.where(segments == v, jnp.where(inside, offset - start, -4 * length), shift)
        start = start + sizes[v]
        offset = offset + jnp.where(inside, sizes[v], 0)
    return lax.broadcasted_iota(jnp.int32, segments.shape, 1) + shift


def one_hot(target, capacity):
    slots = lax.broadcasted_iota(jnp.int32, (capacity, target.shape[-1]), 0)
    return jnp.where(slots == target, 1.0, 0.0).astype(BF16)


def put_back(slots, values, core, own, other):
    half = own.shape[0]
    lanes = lax.broadcasted_iota(jnp.int32, (half, values.shape[0]), 1).astype(F32)
    for out, start in ((own, core * half), (other, (1 - core) * half)):
        column = slots[pl.ds(pl.multiple_of(start, half), half), 0:1]
        pick = jnp.where(column == lanes, 1.0, 0.0).astype(BF16)
        out[...] = dot(pick, values).astype(BF16)


BIG = ("w_in", "w_out", "w_up", "w_down")
KEPT = (
    ("x_kept", (MOST, T), BF16),
    ("qkv", (MOST, 3 * T), BF16),
    ("probs", (H, MOST, MOST), BF16),
    ("norms", (H, MOST), F32),
    ("mix_t", (T, MOST), BF16),
    ("s1", (MOST, T), F32),
    ("act", (MOST, 4 * T), BF16),
    ("gate", (MOST, 4 * T), BF16),
    ("s2", (MOST, T), F32),
)


def filled(ref, name, cap, *lead):
    if name == "probs":
        return ref.at[(*lead, slice(None), pl.ds(0, cap), pl.ds(0, cap))]
    if name in ("mix_t", "norms"):
        return ref.at[(*lead, slice(None), pl.ds(0, cap))]
    return ref.at[(*lead, pl.ds(0, cap), slice(None))]


def forward_kernel(positions, place, tokens, cotangent, segments, live, b_up, b_down, gain, shift, *refs):
    big = dict(zip(BIG, refs[:4]))
    names = [name for name, _, _ in KEPT]
    kept = dict(zip(names, refs[4:13]))
    own_last, other_last, g_first, counted, slots = refs[13:18]
    weights = dict(zip(BIG, refs[18:22]))
    held = dict(zip(names, refs[22:31]))
    row_x, row_g, allow, v_t, q_t, nrm, nlow, came, left, rows_came = refs[31:]
    row = place[0]
    half = place[1]
    length = segments.shape[1]
    own_rows = pl.ds(pl.multiple_of(row * length, length), length)
    load_x = pltpu.make_async_copy(tokens.at[own_rows], row_x, rows_came.at[0])
    load_g = pltpu.make_async_copy(cotangent.at[own_rows], row_g, rows_came.at[1])
    load_x.start()

    def weight_copy(i, layer):
        return pltpu.make_async_copy(big[BIG[i]].at[layer], weights[BIG[i]].at[layer], came.at[layer, i])

    for i in range(4):
        weight_copy(i, 0).start()
    load_g.start()
    for i in range(4):
        weight_copy(i, 1).start()

    seg = segments[pl.ds(row, 1), :]
    alive = live[pl.ds(row, 1), :]
    sizes, mask, cost = split_row(seg)
    target = group_targets(seg, half, sizes, mask)
    counted[0] = cost
    slots[...] = jnp.broadcast_to(target.astype(F32), (8, length)).T

    def run(cap):
        x_now, qkv, probs, norms, mix_t, s1, act, gate, s2 = (held[name] for name in names)

        def keep(name, position):
            i = names.index(name)
            return pltpu.make_async_copy(
                filled(held[name], name, cap), filled(kept[name], name, cap, position), left.at[i]
            )

        pick = one_hot(target, cap)
        load_x.wait()
        x_now[0:cap, :] = dot(pick, row_x[...]).astype(BF16)
        rows = lax.broadcasted_iota(jnp.int32, (8, length), 0)
        both = jnp.where(
            rows == 0, (seg + 1).astype(F32), jnp.where(rows == 1, alive.astype(F32), 0.0)
        ).astype(BF16)
        as_rows = dot_nt(both, pick)
        as_columns = dot_nt(pick, both)
        seg_row = as_rows[0:1, :]
        keys = lax.broadcasted_iota(jnp.int32, (cap, cap), 0)
        queries = lax.broadcasted_iota(jnp.int32, (cap, cap), 1)
        itself = keys == queries
        alive_key = (as_columns[:, 1:2] == 1.0) & (seg_row > 0.0)
        allowed = (seg_row == as_columns[:, 0:1]) & (alive_key | itself)
        allow[0:cap, 0:cap] = jnp.where(allowed, 1.0, 0.0).astype(BF16)
        load_g.wait()
        g_first[0:cap, :] = dot(pick, row_g[...]).astype(BF16)
        factor = HD**-0.5 * LOG2E
        tall = HD + ONES
        for i in range(H):
            v_t[i * tall + HD : (i + 1) * tall, 0:cap] = jnp.ones((ONES, cap), BF16)

        @pl.loop(0, positions)
        def _(position):
            layer = lax.rem(position, 2)

            def need(i):
                @pl.when(position < 2)
                def _():
                    weight_copy(i, layer).wait()

            def free(*which):
                @pl.when(position > 0)
                def _():
                    for name in which:
                        keep(name, position - 1).wait()

            keep("x_kept", position).start()
            need(0)
            free("qkv")

            for j in range(3):
                columns = slice(j * T, (j + 1) * T)
                merged = dot(x_now[0:cap, :], weights["w_in"][layer, :, columns])
                qkv[0:cap, columns] = (merged * factor if j == 0 else merged).astype(BF16)

            keep("qkv", position).start()
            values = qkv[0:cap, 2 * T : 3 * T].T
            for i in range(H):
                v_t[i * tall : i * tall + HD, 0:cap] = values[i * HD : (i + 1) * HD]
            q_t[:, 0:cap] = qkv[0:cap, 0:T].T
            free("probs", "norms", "mix_t")

            def score(i):
                at = i // 2 * (2 * HD) if isinstance(i, int) else lax.div(i, 2) * (2 * HD)
                keys = qkv[0:cap, aligned(T + at, 2 * HD)] * head_mask(i % 2)
                return dot(keys, q_t[aligned(at, 2 * HD), 0:cap])

            def mix(i, weight, sums):
                both = dot(v_t[aligned(i * tall, tall), 0:cap], weight)
                inverse = 1.0 / (both[HD : HD + 1] if sums is None else sums)
                mix_t[aligned(i * HD, HD), 0:cap] = (both[0:HD] * inverse).astype(BF16)
                return both[HD : HD + 1], inverse

            def plain_head(i, scores):
                weight = jnp.exp2(scores).astype(BF16) * allow[0:cap, 0:cap]
                probs[i, 0:cap, 0:cap] = weight
                sums, inverse = mix(i, weight, None)
                nrm[pl.ds(i, 1), 0:cap] = sums
                norms[pl.ds(i, 1), 0:cap] = inverse

            staged(H, cap == EVEN, score, plain_head)
            sums = nrm[0:H, 0:cap]
            outside = jnp.where((sums > 1.0 / SAFE) & (sums < SAFE), 0.0, 1.0)

            @pl.when(jnp.sum(outside) > 0.0)
            def _():
                @pl.loop(0, H)
                def _(i):
                    masked = jnp.where(allow[0:cap, 0:cap].astype(F32) > 0.0, score(i), MASKED)
                    weight = jnp.exp2(masked - jnp.max(masked, axis=0, keepdims=True))
                    probs[i, 0:cap, 0:cap] = weight.astype(BF16)
                    _, inverse = mix(i, weight.astype(BF16), column_sum(weight))
                    norms[pl.ds(i, 1), 0:cap] = inverse

            keep("probs", position).start()
            keep("norms", position).start()
            keep("mix_t", position).start()
            need(1)
            free("s1")
            summed = x_now[0:cap, :].astype(F32) + dot(mix_t[:, 0:cap].T, weights["w_out"][layer])
            s1[0:cap, :] = summed
            keep("s1", position).start()
            plain, _ = row_stats(summed)
            normed = plain * gain[layer, 0:1, :] + shift[layer, 0:1, :]
            nrm[0:cap, 0:T] = normed
            nlow[0:cap, :] = normed.astype(BF16)
            need(2)
            need(3)
            free("act", "gate")

            def raise_up(t):
                columns = aligned(t * T, T)
                return dot(nlow[0:cap, :], weights["w_up"][layer, :, columns])

            def activate(t, hidden):
                columns = aligned(t * T, T)
                v = hidden + b_up[pl.ds(layer, 1), columns]
                c0 = 0.7978845608028654
                c1 = c0 * 0.044715
                square = v * v
                half_one = 0.5 + 0.5 * jnp.tanh(v * (c0 + c1 * square))
                active = v * half_one
                act[0:cap, columns] = active.astype(BF16)
                slope = half_one + active * (1.0 - half_one) * (2.0 * c0 + 6.0 * c1 * square)
                gate[0:cap, columns] = slope.astype(BF16)

            staged(4, cap == EVEN, raise_up, activate)
            branch = dot(act[0:cap, :], weights["w_down"][layer])
            keep("act", position).start()
            keep("gate", position).start()
            free("s2")
            second = nrm[0:cap, 0:T] + (branch + b_down[pl.ds(layer, 1), :])
            s2[0:cap, :] = second
            keep("s2", position).start()
            plain2, _ = row_stats(second)
            keep("x_kept", position).wait()
            x_now[0:cap, :] = (plain2 * gain[layer, 1:2, :] + shift[layer, 1:2, :]).astype(BF16)

        put_back(slots, x_now[0:cap, :], half, own_last, other_last)
        for name in names[1:]:
            keep(name, positions - 1).wait()

    for_count(cost, run)


def forward(positions, place, tokens, cotangent, segments, live, weights):
    w_in, w_out, w_up, b_up, w_down, b_down, gain, shift = weights
    big = (w_in, w_out, w_up, w_down)
    length = segments.shape[1]

    def body(*refs):
        forward_kernel(positions, *refs)

    return pl.pallas_call(
        body,
        in_specs=[SCALARS, AFAR, AFAR] + [WHOLE] * 6 + [AFAR] * 4,
        out_specs=[AFAR] * len(KEPT) + [WHOLE, WHOLE, WHOLE, SCALARS, WHOLE],
        out_shape=[jax.ShapeDtypeStruct((positions,) + shape, kind) for _, shape, kind in KEPT]
        + [jax.ShapeDtypeStruct((length // 2, T), BF16)] * 2
        + [jax.ShapeDtypeStruct((MOST, T), BF16)]
        + [jax.ShapeDtypeStruct((1,), jnp.int32)]
        + [jax.ShapeDtypeStruct((length, 8), F32)],
        scratch_shapes=[pltpu.VMEM(w.shape, BF16) for w in big]
        + [pltpu.VMEM(shape, kind) for _, shape, kind in KEPT]
        + [
            pltpu.VMEM((length, T), BF16),
            pltpu.VMEM((length, T), BF16),
            pltpu.VMEM((MOST, MOST), BF16),
            pltpu.VMEM((H * (HD + ONES), MOST), BF16),
            pltpu.VMEM((T, MOST), BF16),
            pltpu.VMEM((MOST, max(T, MOST)), F32),
            pltpu.VMEM((MOST, T), BF16),
            pltpu.SemaphoreType.DMA((2, 4)),
            pltpu.SemaphoreType.DMA((len(KEPT),)),
            pltpu.SemaphoreType.DMA((2,)),
        ],
        compiler_params=PARAMS,
        cost_estimate=pl.CostEstimate(flops=60 * 10**9, bytes_accessed=1 << 20, transcendentals=0),
        name="forward",
    )(place, tokens, cotangent, segments, live, b_up, b_down, gain, shift, *big)


FFN_READ = ("s2", "s1", "w_down", "gate", "act", "w_up")
HEADS_READ = ("w_out", "mix_t", "norms", "qkv", "probs")
INPUT_READ = ("x_kept", "w_in")
READ = {
    "ffn": FFN_READ, "heads": HEADS_READ, "input": INPUT_READ, "attn": HEADS_READ + INPUT_READ,
}
FILLED = {"ffn": (0, 1), "heads": (3,), "input": (3, 2), "attn": (3, 2)}


def tile_parts(tile, ways):
    return tile.reshape(ways // 2, 2, T // ways, T)


def each(count, unrolled, body):
    if unrolled:
        for i in range(count):
            body(i)
    else:
        pl.loop(0, count)(body)


class Backward:
    def __init__(self, phases, ways, refs, cap):
        self.phases, self.ways, self.cap = phases, ways, cap
        self.__dict__.update(refs)
        self.wide = T // ways
        self.copies = {}
        self.loaded = set()
        layers = sorted({position % 2 for position, _ in phases})
        self.slot = {layer: i for i, layer in enumerate(layers)}
        self.waits = []
        self.filled_once = set()
        for layer in self.before:
            for which, (source, target) in self.before[layer].items():
                rows = pl.ds(0, source.shape[3])
                target = target.at[:, :, :, rows]
                copy = pltpu.make_async_copy(source, target, self.before_came.at[layer, which])
                self.copies["before", layer, which] = copy

    def start_reads(self, index):
        if index >= len(self.phases):
            return
        position, part = self.phases[index]
        names = list(READ[part])
        if part in ("attn", "heads") and (position, "ffn") not in self.phases:
            names = ["s1"] + names
        for name in names:
            sem = self.came.at[self.names.index(name)]
            source, target = self.sources[name], self.held[name]
            if name.startswith("w_"):
                if (name, position % 2) in self.loaded:
                    continue
                self.loaded.add((name, position % 2))
                source = source.at[position % 2]
                target = self.weight(name, position)
            else:
                source = filled(source, name, self.cap, position)
                target = filled(target, name, self.cap)
            self.copies[name] = pltpu.make_async_copy(source, target, sem)
            self.copies[name].start()
        for i, (source, target) in enumerate(self.handed if part == "input" else ()):
            self.copies["handed", i] = pltpu.make_async_copy(source, target, self.hand.at[i])
            self.copies["handed", i].start()
        for which in FILLED[part]:
            if ("before", position % 2, which) in self.copies:
                self.copies["before", position % 2, which].start()

    def weight(self, name, position):
        return self.held[name].at[self.slot[position % 2]]

    def need(self, *names):
        for name in names:
            if name in self.copies:
                self.copies.pop(name).wait()

    def store(self, layer, which, index, value):
        if which in self.before.get(layer, {}) or (layer, which) in self.filled_once:
            value = value + self.grads[layer][which][index].astype(F32)
        self.grads[layer][which][index] = value.astype(BF16)

    def send(self, layer, which):
        source, sem = self.grads[layer][which], self.left.at[layer, which]
        self.filled_once.add((layer, which))
        if (layer, which) not in self.final:
            copy = pltpu.make_async_copy(source, self.results[layer, which], sem)
            copy.start()
        else:
            start = 0 if which < 2 or (layer, 0) not in self.keys else 2 * self.wide
            rows = pl.ds(start, source.shape[3])
            mine, other = (self.results[layer, role].at[:, :, :, rows] for role in ("mine", "other"))
            copy = pltpu.make_async_copy(source, mine, sem)
            other = pltpu.make_async_copy(source, other, sem)
            core = self.place[1]

            @pl.when(core == which % 2)
            def _():
                copy.start()

            @pl.when(core != which % 2)
            def _():
                other.start()

        self.waits.append(copy)

    def close(self, position, *arrays):
        for which in arrays:
            if self.last_use[position % 2, which] == position:
                self.send(position % 2, which)
            else:
                self.filled_once.add((position % 2, which))

    def incoming(self, position):
        return self.entry if (position, "ffn") == self.phases[0] else self.g_now

    def ends_with(self, position, part):
        return self.phases[-1] == (position, part)

    def with_ffn(self, position):
        return (position, "ffn") in self.phases

    def hand_on(self, i, source, target):
        self.waits.append(pltpu.make_async_copy(source, target, self.hand.at[i]))
        self.waits[-1].start()

    def store_smalls(self):
        below = pl.ds(self.wide, self.extra)
        first, second = self.grads[0][2], self.grads[0][3]
        first[:, :, :, below, :] = jnp.zeros(first.shape[:3] + (self.extra, T), BF16)
        rows = lax.broadcasted_iota(jnp.int32, (self.extra, T), 0)
        for shard in range(self.ways):
            z, y = shard // 2, shard % 2
            lanes = shard * self.wide // 128 * 128
            ups = jnp.zeros((self.extra, T), F32)
            rest = jnp.zeros((self.extra, T), F32)
            for layer in range(2):
                start = shard * 4 * self.wide
                row = self.smalls[layer, start // T : start // T + 1, start % T : start % T + 4 * self.wide]
                row = jnp.concatenate([row, jnp.zeros((1, T - 4 * self.wide), F32)], axis=1)
                ups = jnp.where(rows == layer, row, ups)
                block = self.smalls[layer, :, lanes : lanes + 128]
                for i in range(5):
                    row = jnp.concatenate([block[4 + i : 5 + i], jnp.zeros((1, T - 128), F32)], axis=1)
                    rest = jnp.where(rows == 5 * layer + i, row, rest)
            second[y, 0, z, below, :] = ups.astype(BF16)
            second[y, 1, z, below, :] = rest.astype(BF16)

    def run(self):
        self.last_use = {}
        for position, part in self.phases:
            for which in FILLED[part]:
                self.last_use[position % 2, which] = position
        self.start_reads(0)
        self.start_reads(1)
        for index, (position, part) in enumerate(self.phases):
            getattr(self, part)(position)
            self.start_reads(index + 2)
        for copy in self.waits:
            copy.wait()

    def ffn(self, position):
        cap, layer, wide, ways = self.cap, position % 2, self.wide, self.ways
        rows = slice(0, cap)
        smalls = self.smalls.at[layer]
        g = self.incoming(position)[rows, :].astype(F32)
        self.need("s2")
        plain, inverse = row_stats(self.held["s2"][rows, :])
        smalls[6:7, :] += column_sum(g * plain)
        smalls[8:9, :] += column_sum(g)
        grad_f = norm_back(g, plain, inverse, self.gain[layer, 1:2, :])
        self.gf[rows, :] = grad_f
        grad_branch = grad_f.astype(BF16)
        gb = self.g_now
        gb[rows, :] = grad_branch
        smalls[4:5, :] += column_sum(grad_branch.astype(F32))
        self.need("s1")
        plain1, inverse1 = row_stats(self.held["s1"][rows, :])
        self.n1[rows, :] = plain1
        self.r1[rows, :] = inverse1
        low = (plain1 * self.gain[layer, 0:1, :] + self.shift[layer, 0:1, :]).astype(BF16)
        nl_t = self.d_t.at[0:T]
        nl_t[:, rows] = low.T
        self.need("w_down", "gate", "act", "w_up", ("before", layer, 0), ("before", layer, 1))
        act, gate = self.held["act"], self.held["gate"]
        w_down, w_up = self.weight("w_down", position), self.weight("w_up", position)

        def lower(t):
            return dot_nt(gb[rows, :], w_down[aligned(t * T, T), :])

        def tile(t, da):
            columns = aligned(t * T, T)
            dh = (gate[rows, columns].astype(F32) * da).astype(BF16)
            gate[rows, columns] = dh
            smalls[pl.ds(t, 1), :] += column_sum(dh.astype(F32))
            parts = tile_parts(dot(nl_t[:, rows], dh), ways)
            few = ways // 8
            below = dot_tn(act[rows, columns], gb[rows, :]).reshape(few, 2, 2, 2 * wide, T)
            for y in range(2):
                self.store(layer, 0, (t // 2, y, slice(None), aligned(t % 2 * wide, wide)), parts[:, y])
                for x in range(2):
                    self.store(layer, 1, (y, x, pl.ds(t * few, few)), below[:, y, x])

        staged(4, cap == EVEN, lower, tile)
        self.close(position, 0, 1)
        self.gf[rows, :] = self.gf[rows, :] + dot_nt(gate[rows, :], w_up[...])
        if self.ends_with(position, "ffn"):
            self.hand_on(0, self.gf.at[rows], self.ends[0].at[rows])

    def attn(self, position):
        self.heads(position)
        self.input(position)

    def heads(self, position):
        cap, layer, ways = self.cap, position % 2, self.ways
        rows = slice(0, cap)
        smalls = self.smalls.at[layer]
        if self.with_ffn(position):
            grad_normed = self.gf[rows, :]
            plain1, inverse1 = self.n1[rows, :], self.r1[rows, :]
        else:
            self.need("s1")
            grad_normed = self.entry[rows, :]
            plain1, inverse1 = row_stats(self.held["s1"][rows, :])
        smalls[5:6, :] += column_sum(grad_normed * plain1)
        smalls[7:8, :] += column_sum(grad_normed)
        grad_summed = norm_back(grad_normed, plain1, inverse1, self.gain[layer, 0:1, :])
        self.gf[rows, :] = grad_summed
        if self.ends_with(position, "heads"):
            self.hand_on(0, self.gf.at[rows], self.ends[0].at[rows])
        grad_attn = grad_summed.astype(BF16)
        self.need("w_out", "mix_t", ("before", layer, 3))
        mix_t, qkv, probs = (self.held[name] for name in ("mix_t", "qkv", "probs"))
        parts = tile_parts(dot(mix_t[:, rows], grad_attn), ways)
        for y in range(2):
            self.store(layer, 3, (y, 1, slice(None), pl.ds(0, self.wide)), parts[:, y])
        if self.ends_with(position, "heads"):
            self.close(position, 3)
        dmix_t, d_t = self.dmix_t, self.d_t
        q_t, k_t = d_t.at[0:T], d_t.at[T : 2 * T]
        self.need("norms")
        grad_mixture = dot_nt(self.weight("w_out", position)[...], grad_attn)
        for i in range(H):
            own = slice(i * HD, (i + 1) * HD)
            dmix_t[own, rows] = (grad_mixture[own] * self.held["norms"][i : i + 1, rows]).astype(BF16)
        self.need("qkv")
        q_t[:, rows] = qkv[rows, 0:T].T
        k_t[:, rows] = qkv[rows, T : 2 * T].T
        self.need("probs")

        def grad_probs(i):
            at = i // 2 * (2 * HD) if isinstance(i, int) else lax.div(i, 2) * (2 * HD)
            values = qkv[rows, aligned(2 * T + at, 2 * HD)] * head_mask(i % 2)
            return dot(values, dmix_t[aligned(at, 2 * HD), rows])

        def head(i, dp):
            own = aligned(i * HD, HD)
            do = dmix_t[own, rows]
            delta = column_sum(do.astype(F32) * mix_t[own, rows].astype(F32))
            p = probs[i, rows, rows]
            ds = (p.astype(F32) * (dp - delta)).astype(BF16)
            grad_q = dot(k_t[own, rows], ds) * HD**-0.5
            grad_k = dot_nt(q_t[own, rows], ds) * (1.0 / LOG2E)
            d_t[own, rows] = grad_q.astype(BF16)
            own_k = aligned(T + i * HD, HD)
            d_t[own_k, rows] = grad_k.astype(BF16)
            own_v = aligned(2 * T + i * HD, HD)
            d_t[own_v, rows] = dot_nt(do, p).astype(BF16)

        staged(H, cap == EVEN, grad_probs, head)
        if self.ends_with(position, "heads"):
            self.hand_on(1, d_t.at[:, rows], self.ends[1].at[:, rows])

    def input(self, position):
        cap, layer, ways, d_t = self.cap, position % 2, self.ways, self.d_t
        rows = slice(0, cap)
        self.need("x_kept", "w_in", ("before", layer, 2), ("before", layer, 3))
        self.need(("handed", 0), ("handed", 1))
        x_t = self.held["x_kept"][rows, :].T
        for j in range(3):
            parts = tile_parts(dot_nt(x_t, d_t[j * T : (j + 1) * T, rows]), ways)
            for y in range(2):
                index = ((j, y) if j < 2 else (y, 0)) + (slice(None), pl.ds(0, self.wide))
                self.store(layer, 2 if j < 2 else 3, index, parts[:, y])
        if self.extra:
            self.store_smalls()
        self.close(position, 2, 3)
        g = (self.gf[rows, :] + dot(self.weight("w_in", position)[...], d_t[:, rows]).T).astype(BF16)
        if self.last:
            put_back(self.slots[0], g, self.place[1], *self.ends)
        else:
            self.g_now[rows, :] = g
            if self.ends_with(position, "attn"):
                self.ends[0][rows, :] = g


class LoopedBackward(Backward):
    first, last_one = 3, 1

    def __init__(self, ways, refs, cap):
        self.ways, self.cap = ways, cap
        self.__dict__.update(refs)
        self.wide = T // ways

    def ends_with(self, position, part):
        return False

    def with_ffn(self, position):
        return True

    def incoming(self, position):
        return self.g_now

    def weight(self, name, position):
        return self.held[name].at[lax.rem(position, 2)]

    def weight_copy(self, name, layer):
        i = self.names.index(name)
        return pltpu.make_async_copy(
            self.sources[name].at[layer], self.held[name].at[layer], self.came.at[layer, i]
        )

    def copy(self, name, position):
        source = filled(self.sources[name], name, self.cap, position)
        target = filled(self.held[name], name, self.cap)
        return pltpu.make_async_copy(source, target, self.came.at[0, self.names.index(name)])

    def start_reads(self, part, position):
        names = READ[part]
        for name in names:
            if name.startswith("w_"):

                @pl.when(position >= self.first - 1)
                def _(name=name):
                    self.weight_copy(name, lax.rem(position, 2)).start()

            else:
                self.copy(name, position).start()

    def need(self, *names):
        for name in names:
            if isinstance(name, tuple):
                continue
            if name.startswith("w_"):

                @pl.when(self.position >= self.first - 1)
                def _(name=name):
                    self.weight_copy(name, lax.rem(self.position, 2)).wait()

            else:
                self.copy(name, self.position).wait()

    def store(self, layer, which, index, value):
        target = self.grads[which].at[layer]
        old = jnp.where(self.position == self.last_one, target[index].astype(F32), 0.0)
        target[index] = (value + old).astype(BF16)

    def out(self, layer, which):
        return pltpu.make_async_copy(
            self.grads[which].at[layer], self.results[layer, which], self.left.at[layer, which]
        )

    def final_out(self, which, role):
        source = self.grads[which].at[1]
        rows = pl.ds(0 if which < 2 else 2 * self.wide, source.shape[3])
        return pltpu.make_async_copy(
            source, self.results[1, role].at[:, :, :, rows], self.left.at[1, which]
        )

    def close(self, position, *arrays):
        core = self.place[1]
        for which in arrays:

            @pl.when(position == 2)
            def _(which=which):
                self.out(0, which).start()

            @pl.when((position == 1) & (core == which % 2))
            def _(which=which):
                self.final_out(which, "mine").start()

            @pl.when((position == 1) & (core != which % 2))
            def _(which=which):
                self.final_out(which, "other").start()

    def run(self):
        rows = slice(0, self.cap)
        self.g_now[rows, :] = self.entry[rows, :]
        self.start_reads("ffn", self.first)
        self.start_reads("attn", self.first)

        @pl.loop(0, self.first - self.last_one + 1)
        def _(step):
            position = self.first - step
            self.position = position
            self.ffn(position)

            @pl.when(position > self.last_one)
            def _():
                self.start_reads("ffn", position - 1)

            self.attn(position)

            @pl.when(position > self.last_one)
            def _():
                self.start_reads("attn", position - 1)

        self.ends[0][rows, :] = self.g_now[rows, :]
        for which in range(4):
            self.out(0, which).wait()
            self.final_out(which, "mine").wait()


def backward(phases, ways, place, count, entry, smalls, given, before, final, after=(), extra=0, looped=False):
    parts = [part for _, part in phases]
    first_part, last_part = parts[0], parts[-1]
    names = ["s1"] if first_part in ("heads", "attn") else []
    for part in parts:
        names += [name for name in READ[part] if name not in names]
    shapes = {name: (shape, kind) for name, shape, kind in KEPT}
    for name in BIG:
        layers = len({position % 2 for position, _ in phases})
        shapes[name] = ((layers,) + given[name].shape[1:], BF16)
    wide = T // ways
    packed = {}
    for position, part in phases:
        for which in sorted(FILLED[part]):
            packed[position % 2, which] = (2, 2, ways // 2, (2 if which < 2 else 1) * wide, T)
    olds = [(layer, which) for layer in before for which in before[layer]]
    n, keys = len(names), list(packed)
    extra_rows = extra
    if extra:
        for key in ((0, 2), (0, 3)):
            packed[key] = packed[key][:3] + (wide + extra, T)
    made = {}
    for layer, which in keys:
        if (layer, which) not in final:
            made[layer, which] = packed[layer, which]
        elif which in (0, 2):
            rows = packed[layer, which][3] + (made[layer, "mine"][3] if (layer, "mine") in made else 0)
            for role in ("mine", "other"):
                made[layer, role] = (2, 2, ways // 2, rows, T)
    last = phases[-1] in ((0, "input"), (0, "attn"))
    half = given["slots"].shape[0] // 2
    entries = [] if first_part == "input" else [entry]
    handed = list(entry) if first_part == "input" else []

    def body(place, count, gain, shift, *refs):
        refs = list(refs)

        def cut(amount):
            part = refs[:amount]
            del refs[:amount]
            return part

        entry_refs = cut(len(entries))
        smalls_in = cut(0 if smalls is None else 1)
        slots = cut(1 if last else 0)
        handed_refs = cut(len(handed))
        cut(len(after))

        def by_layer(keys, values):
            table = {}
            for (layer, which), value in zip(keys, values):
                table.setdefault(layer, {})[which] = value
            return table

        sources = dict(zip(names, cut(n)))
        olds_hbm = by_layer(olds, cut(len(olds)))
        results = dict(zip(made, cut(len(made))))
        smalls_out = cut(1)[0]
        end_refs = cut(len(ends))
        held = dict(zip(names, cut(n)))
        grads = cut(4) if looped else by_layer(keys, cut(len(keys)))
        work = ("g_now", "gf", "n1", "r1", "dmix_t", "d_t")
        sems = ("came", "before_came", "left", "hand")
        table = dict(zip(work + sems, cut(len(work) + len(sems))))
        table.update(
            place=place, gain=gain, shift=shift, smalls=smalls_out, ends=end_refs,
            entry=entry_refs[0] if entry_refs else None, slots=slots, last=last, extra=extra_rows,
            handed=[],
            names=names, sources=sources, held=held, grads=grads, results=results, final=final, keys=keys,
            before={
                layer: {which: (ref, grads[layer][which]) for which, ref in olds_hbm[layer].items()}
                for layer in olds_hbm
            },
        )
        smalls_out[...] = smalls_in[0][...] if smalls_in else jnp.zeros(smalls_out.shape, F32)

        def run(cap):
            own = dict(table)
            if handed_refs:
                rows = pl.ds(0, cap)
                own["handed"] = [
                    (handed_refs[0].at[rows], table["gf"].at[rows]),
                    (handed_refs[1].at[:, rows], table["d_t"].at[:, rows]),
                ]
            (LoopedBackward(ways, own, cap) if looped else Backward(phases, ways, own, cap)).run()

        for_count(count[0], run)

    extras = ([] if smalls is None else [smalls]) + ([given["slots"]] if last else [])
    end_spec = [WHOLE]
    if last:
        ends = [jax.ShapeDtypeStruct((half, T), BF16)] * 2
        end_spec = [WHOLE, WHOLE]
    elif last_part == "heads":
        ends = [jax.ShapeDtypeStruct((MOST, T), F32), jax.ShapeDtypeStruct((3 * T, MOST), BF16)]
        end_spec = [AFAR, AFAR]
    elif last_part == "ffn":
        ends = [jax.ShapeDtypeStruct((MOST, T), F32)]
        end_spec = [AFAR]
    else:
        ends = [jax.ShapeDtypeStruct((MOST, T), BF16)]
    costs = {"attn": 14e9, "ffn": 10e9, "heads": 10e9, "input": 4e9}
    flops = sum(costs[part] for part in parts)
    outs = pl.pallas_call(
        body,
        in_specs=[SCALARS, SCALARS]
        + [WHOLE] * (2 + len(entries) + len(extras))
        + [AFAR] * (len(handed) + len(after) + n + len(olds)),
        out_specs=[AFAR] * len(made) + [WHOLE] + end_spec,
        out_shape=[jax.ShapeDtypeStruct(shape, BF16) for shape in made.values()]
        + [jax.ShapeDtypeStruct((2, SMALL, T), F32)]
        + ends,
        scratch_shapes=[pltpu.VMEM(*shapes[name]) for name in names]
        + (
            [pltpu.VMEM((2,) + packed[0, which], BF16) for which in range(4)]
            if looped
            else [pltpu.VMEM(packed[key], BF16) for key in keys]
        )
        + [
            pltpu.VMEM((MOST, T), BF16),
            pltpu.VMEM((MOST, T), F32),
            pltpu.VMEM((MOST, T), F32),
            pltpu.VMEM((MOST, 1), F32),
            pltpu.VMEM((T, MOST), BF16),
            pltpu.VMEM((3 * T, MOST), BF16),
            pltpu.SemaphoreType.DMA((2, n) if looped else (n,)),
            pltpu.SemaphoreType.DMA((2, 4)),
            pltpu.SemaphoreType.DMA((2, 4)),
            pltpu.SemaphoreType.DMA((2,)),
        ],
        compiler_params=PARAMS,
        cost_estimate=pl.CostEstimate(flops=int(flops), bytes_accessed=1 << 20, transcendentals=0),
        name="backward_" + "_".join(f"{part}{position}" for position, part in phases),
    )(
        place, count, given["gain"], given["shift"], *entries, *extras, *handed, *after,
        *[given[name] for name in names], *[before[layer][which] for layer, which in olds],
    )
    table = dict(zip(made, outs))
    outs = outs[len(made) :]
    return table, outs[0], outs[1] if len(ends) == 1 else outs[1:]


def swap(block, pairs):
    return lax.ppermute(block, ("section", "dp"), pairs)


class Links:
    def __init__(self):
        self.sections = lax.axis_size("section")
        self.ways = lax.axis_size("dp")
        section = lax.axis_index("section")
        self.me = lax.axis_index("dp")
        self.core, self.x, y = section % 2, section // 2, self.me % 2
        self.bits = (self.ways // 2).bit_length() - 1
        one = jnp.where(self.core == 0, self.x, y)
        two = jnp.where(self.core == 0, y, self.x)
        low_first = [self.me // (2 << i) % 2 for i in range(self.bits)]
        self.halves = [one, two] + low_first
        self.token = None
        self.in_order = True
        self.others = []

    def pairs(self, partner):
        every = [(s, d) for s in range(self.sections) for d in range(self.ways)]
        return [
            (s * self.ways + d, partner(s, d)[0] * self.ways + partner(s, d)[1]) for s, d in every
        ]

    def in_dp(self, bits):
        return self.pairs(lambda s, d: (s, d ^ bits))

    def in_section(self, bits):
        return self.pairs(lambda s, d: (s ^ bits, d))

    def step(self, i):
        if i == 0:
            return self.pairs(lambda s, d: (s ^ 2, d) if s % 2 == 0 else (s, d ^ 1))
        if i == 1:
            return self.pairs(lambda s, d: (s, d ^ 1) if s % 2 == 0 else (s ^ 2, d))
        return self.in_dp(1 << (i - 1))

    def place(self, gives, steps_done, ndim):
        order = [0, 1] + list(range(self.bits + 1, 1, -1))
        return [gives[axis] if axis < len(gives) else None for axis in order if axis >= steps_done]

    def sum(self, terms):
        total = 0.0
        for array, index in terms:
            for dim in reversed(range(len(index))):
                if index[dim] is not None:
                    kind, axis = index[dim]
                    half = self.halves[axis]
                    at = half if kind == "keep" else 1 - half
                    array = lax.dynamic_index_in_dim(array, at, dim, keepdims=False)
            total = total + array.astype(F32)
        return total

    def ordered(self, total, last=True):
        for token in self.others + ([] if self.token is None else [self.token]):
            width = token.shape[-1]
            row = lax.slice(token, (0,) * token.ndim, (1,) * (token.ndim - 1) + (width,))
            row = jnp.minimum(jnp.abs(row.reshape(width).astype(F32)), 0.0)
            total = total + (row if width == T else jnp.tile(row, T // width))
        self.others = []
        total = total.astype(BF16)
        if last and self.in_order:
            self.token = total
        return total


class Group:
    def __init__(self, links, mine=None, other=None, groups=()):
        self.links, self.done = links, 0
        if groups:
            self.done = groups[0].done
            sums = [links.ordered(group.total(), group is groups[-1]) for group in groups]
            self.have = [(jnp.concatenate(sums, axis=-2), self.done)]
        else:
            shape = (2, 2) + (2,) * links.bits + mine.shape[3:]
            came = swap(other, links.in_section(1))
            self.have = [(mine.reshape(shape), 0), (came.reshape(shape), 0)]

    def sum(self, wanted):
        return self.links.sum(
            [(array, self.links.place(wanted, done, array.ndim)) for array, done in self.have]
        )

    def keeps(self):
        return [("keep", i) for i in range(self.done)]

    def give(self):
        give = self.links.ordered(self.sum(self.keeps() + [("give", self.done)]))
        came = swap(give, self.links.step(self.done))
        self.done += 1
        self.have.append((came, self.done))
        return give

    def finished(self):
        return self.done == 2 + self.links.bits

    def total(self):
        return self.sum(self.keeps())


def to_sections(links, total):
    over = swap(total, links.in_section(2))
    beside = swap(total, links.in_section(1))
    return [total, beside, over, swap(over, links.in_section(1))]


def spread(links, own, other, came):
    came = [swap(other, links.in_section(1)), came]
    rows, width = own[0].shape[0], own[0].shape[1] // links.sections
    after = [] if links.token is None else [links.token]

    def body(*refs):
        own, came, out = refs[:2], refs[2:4], refs[4 + len(after)]
        for s in range(links.sections):
            at = pl.ds(s * width, width)
            for i in range(2):
                out[s, i] = (own[i][:, at].astype(F32) + came[i][:, at].astype(F32)).astype(BF16)

    gives = pl.pallas_call(
        body,
        in_specs=[WHOLE] * 4 + [AFAR] * len(after),
        out_specs=WHOLE,
        out_shape=jax.ShapeDtypeStruct((links.sections, 2, rows, width), BF16),
        compiler_params=PARAMS,
        name="spread",
    )(*own, *came, *after)
    return lax.all_to_all(gives, "section", 0, 0)


def lay_out(layer, at, pieces, wide, scale, ins, out_proj, ups, downs):
    of = [pieces[s ^ at] for s in range(4)]
    own = pl.ds(2 * wide, wide)
    for x in range(2):
        for i in range(2):
            rows = pl.ds(i * wide, wide)
            columns = pl.ds((2 * x + i) * T, T)
            ups[:, columns] = of[2 * x][rows, :].astype(F32) * scale
        downs[pl.ds(2 * x * wide, 2 * wide), :] = of[2 * x + 1][0 : 2 * wide, :].astype(F32) * scale
        ins[:, pl.ds(x * T, T)] = of[2 * x][own, :].astype(F32) * scale
    ins[:, pl.ds(2 * T, T)] = of[1][own, :].astype(F32) * scale
    out_proj[...] = of[3][own, :].astype(F32) * scale


def big_shapes(wide):
    return [(wide, 3 * T), (wide, T), (wide, 4 * T), (4 * wide, T)]


def gather_early(place, blocks, pieces, ways):
    wide = T // ways
    _, _, half, width = blocks.shape
    shapes = big_shapes(wide)

    def body(place, *refs):
        blocks, pieces, outs = refs[0], refs[1:5], refs[5:11]
        made, sems = refs[11:15], refs[15]
        section = 2 * place[0] + place[1]
        for at in range(4):

            @pl.when(section == at)
            def _(at=at):
                lay_out(1, at, pieces, wide, 1.0 / ways, *made)

        copies = [
            pltpu.make_async_copy(made[i], outs[2 + i].at[1], sems.at[i]) for i in range(4)
        ]
        for copy in copies:
            copy.start()
        for s in range(4):
            rows = pl.ds(s * half, half)
            outs[1][rows, :] = blocks[s, 0]
            outs[0][rows, :] = blocks[s, 1]
        for copy in copies:
            copy.wait()

    return pl.pallas_call(
        body,
        in_specs=[SCALARS] + [WHOLE] * 5,
        out_specs=[WHOLE] * 2 + [AFAR] * 4,
        out_shape=[jax.ShapeDtypeStruct((4 * half, width), BF16)] * 2
        + [jax.ShapeDtypeStruct((2,) + shape, F32) for shape in shapes],
        scratch_shapes=[pltpu.VMEM(shape, F32) for shape in shapes]
        + [pltpu.SemaphoreType.DMA((4,))],
        compiler_params=PARAMS,
        cost_estimate=pl.CostEstimate(flops=5 * 10**9, bytes_accessed=1 << 20, transcendentals=0),
        name="gather_early",
    )(place, blocks, *pieces)


def gather_late(place, sums, pieces, begun, ways, extra):
    wide = T // ways
    scale = 1.0 / ways
    shapes = big_shapes(wide)

    def body(place, sums, *refs):
        pieces, outs = refs[:4], refs[8:12]
        up_bias, down_bias, gains, shifts = refs[12:16]
        made, sems = refs[16:20], refs[20]
        section = 2 * place[0] + place[1]
        me = place[2]

        def small_rows(layer, row, rest):
            up_bias[layer : layer + 1, :] = row[0:1, 0 : 4 * wide]
            down_bias[layer : layer + 1, :] = rest[0:1, 0:wide]
            gains[layer] = rest[1:3, 0:wide]
            shifts[layer] = rest[3:5, 0:wide]

        for at in range(4):

            @pl.when(section == at)
            def _(at=at):
                lay_out(0, at, pieces, wide, scale, *made)

        copies = [
            pltpu.make_async_copy(made[i], outs[i].at[0], sems.at[i]) for i in range(4)
        ]
        for copy in copies:
            copy.start()
        if extra:
            for at in range(4):

                @pl.when(section == at)
                def _(at=at):
                    below = pl.ds(3 * wide, extra)
                    row = pieces[1 ^ at][below, :].astype(F32) * scale
                    rest = pieces[3 ^ at][below, 0:128].astype(F32) * scale
                    turn = lax.rem(me * wide, 128)
                    rest = pltpu.roll(rest, lax.rem(128 - turn, 128), 1)
                    for layer in range(2):
                        small_rows(layer, row[layer : layer + 1], rest[5 * layer : 5 * layer + 5])

        else:
            for layer in range(2):
                start = me * (4 * wide)
                row = sums[layer, pl.ds(lax.div(start, T), 1), :] * scale
                row = jnp.broadcast_to(row, (8, T))
                row = pltpu.roll(row, lax.rem(T - lax.rem(start, T), T), 1)
                rest = pltpu.roll(sums[layer] * scale, lax.rem(T - me * wide, T), 1)
                small_rows(layer, row, rest[4:9])
        for copy in copies:
            copy.wait()

    small_shapes = [(2, 4 * wide), (2, wide), (2, 2, wide), (2, 2, wide)]
    return pl.pallas_call(
        body,
        in_specs=[SCALARS] + [WHOLE] * 5 + [AFAR] * 4,
        out_specs=[AFAR] * 4 + [WHOLE] * 4,
        out_shape=[jax.ShapeDtypeStruct((2,) + shape, F32) for shape in shapes]
        + [jax.ShapeDtypeStruct(shape, F32) for shape in small_shapes],
        input_output_aliases={6 + i: i for i in range(4)},
        scratch_shapes=[pltpu.VMEM(shape, F32) for shape in shapes]
        + [pltpu.SemaphoreType.DMA((4,))],
        compiler_params=PARAMS,
        name="gather_late",
    )(place, sums, *pieces, *begun)


def finer(block, kind, ways):
    made = 2 * block.shape[2]
    cut = ways // made
    if cut == 1:
        return block
    z, rows = block.shape[2:4]
    if kind == "down":
        block = block.transpose(2, 0, 1, 3, 4).reshape(z, 2, cut // 2, 2, 2, rows // cut, T)
        block = block.transpose(3, 4, 0, 1, 2, 5, 6)
    elif kind == "right":
        block = block.reshape(2, 2, z, cut // 2, 2, rows // cut, T).transpose(4, 1, 2, 0, 3, 5, 6)
    else:
        tiles = 2 if kind == "up" else 1
        block = block.reshape(2, 2, z, tiles, cut // 2, 2, rows // tiles // cut, T)
        block = block.transpose(0, 5, 2, 1, 4, 3, 6, 7)
    return block.reshape(2, 2, ways // 2, rows // cut, T)


def finer_pair(links, arrays, kinds):
    mine, other = arrays
    if 2 * mine.shape[2] == links.ways:
        return arrays
    wide = T // (2 * mine.shape[2])

    def cut(block, which):
        parts, start = [], 0
        for kind in kinds:
            rows = (2 if kind[0] == "up" else 1) * wide
            parts.append(finer(block[:, :, :, start : start + rows], kind[which], links.ways))
            start += rows
        return jnp.concatenate(parts, axis=3)

    return (
        jnp.where(links.core == 0, cut(mine, 0), cut(mine, 1)),
        jnp.where(links.core == 0, cut(other, 1), cut(other, 0)),
    )


def on_device(
    tokens, segment_ids, live_mask, cotangent,
    project_in, project_out, up_weight, up_bias, down_weight, down_bias, norm_gain, norm_shift,
):
    ways = lax.axis_size("dp")
    positions = lax.axis_size("section")
    made = min(ways, T // 32)
    links = Links()
    place = jnp.stack([links.x, links.core, links.me]).astype(jnp.int32)
    weights = (
        project_in, project_out, up_weight, up_bias, down_weight, down_bias, norm_gain, norm_shift,
    )
    *kept, own, other, g, count, slots = forward(
        positions, place, tokens, cotangent, segment_ids, live_mask, weights
    )
    given = dict(zip((name for name, _, _ in KEPT), kept))
    given.update(
        w_in=project_in, w_out=project_out, w_up=up_weight, w_down=down_weight,
        gain=norm_gain, shift=norm_shift, slots=slots,
    )
    extra = SMALL if made == ways else 0
    came = swap(other, links.in_section(1))
    of_ffn, of_attn = ("up", "down"), ("left", "right")

    def group(arrays, layer, kinds):
        return Group(links, *finer_pair(links, (arrays[layer, "mine"], arrays[layer, "other"]), kinds))

    def back(phases, entry, smalls, before, final=(), after=(), extra=0, looped=False):
        return backward(
            phases, made, place, count, entry, smalls, given, before, final, after, extra, looped
        )

    early = [(position, part) for position in (3, 2, 1) for part in ("ffn", "attn")]
    finals = ((1, 0), (1, 1), (1, 2), (1, 3))
    grads, smalls, g = back(early, g, None, {}, finals, looped=True)
    all_1 = group(grads, 1, (of_ffn, of_attn))
    before = {0: {0: grads[0, 0], 1: grads[0, 1]}}
    ffn, smalls, g = back([(0, "ffn")], g, smalls, before, ((0, 0), (0, 1)))
    ffn_0 = group(ffn, 0, (of_ffn,))
    after = [all_1.give()]
    before = {0: {2: grads[0, 2], 3: grads[0, 3]}}
    attn, smalls, halves = back([(0, "attn")], g, smalls, before, ((0, 2), (0, 3)), after, extra)
    attn_0 = group(attn, 0, (of_attn,))
    all_1.give()
    ffn_0.give()
    attn_0.give()
    all_1.give()
    ffn_0.give()
    attn_0.give()
    blocks = spread(links, (halves[0], own), halves[1], came)
    while not all_1.finished():
        all_1.give()
        ffn_0.give()
        attn_0.give()
    pieces_1 = to_sections(links, links.ordered(all_1.total()))
    links.others = [blocks]
    while not (attn_0.finished() and ffn_0.finished()):
        for last in (ffn_0, attn_0):
            if not last.finished():
                last.give()
    mixed_out, tokens_out, *begun = gather_early(place, blocks, pieces_1, ways)
    both = Group(links, groups=(ffn_0, attn_0))
    links.others = [pieces_1[2]]
    pieces_0 = to_sections(links, links.ordered(both.total()))
    if not extra:
        smalls = lax.psum(smalls, ("section", "dp"))
    outs = gather_late(place, smalls, pieces_0, begun, ways, extra)
    big, (up_sum, down_sum, gains, shifts) = outs[:4], outs[4:]
    return (mixed_out, tokens_out, big[0], big[1], big[2], up_sum, big[3], down_sum, gains, shifts)


def solution(mesh):
    rows = P("dp", None)
    in_specs = (rows,) * 4 + (P(),) * 8
    out_specs = (
        P("dp", "section"),
        P("dp", "section"),
        P(None, "dp", None),
        P(None, "dp", None),
        P(None, "dp", None),
        P(None, "dp"),
        P(None, "dp", None),
        P(None, "dp"),
        P(None, None, "dp"),
        P(None, None, "dp"),
    )
    return jax.shard_map(
        on_device, mesh=mesh, in_specs=in_specs, out_specs=out_specs, check_vma=False
    )
```

```python
import jax
import jax.numpy as jnp
from jax import lax
from jax.experimental import pallas as pl
from jax.experimental.pallas import tpu as pltpu
from jax.sharding import PartitionSpec as P

H = 8
HD = 64
T = 512
SEGMENTS = 4
EVEN, MOST = 512, 768
SMALL = 16
EPS = 1e-05
MASKED = -1e30
SAFE = 2.0**60
ONES = 16
LOG2E = 1.4426950408889634
F32 = jnp.float32
BF16 = jnp.bfloat16
VMEM_BYTES = 62 * 1024 * 1024


def dot(a, b):
    return jnp.dot(a, b, preferred_element_type=F32)


def dot_nt(a, b):
    return lax.dot_general(a, b, (((1,), (1,)), ((), ())), preferred_element_type=F32)


def dot_tn(a, b):
    return lax.dot_general(a, b, (((0,), (0,)), ((), ())), preferred_element_type=F32)


def row_stats(values):
    center = values - jnp.mean(values, axis=-1, keepdims=True)
    spread = jnp.mean(center * center, axis=-1, keepdims=True)
    inverse = lax.rsqrt(spread + EPS)
    return center * inverse, inverse


def norm_back(grad, plain, inverse, gain):
    scaled = grad * gain
    return inverse * (
        scaled
        - jnp.mean(scaled, axis=-1, keepdims=True)
        - plain * jnp.mean(scaled * plain, axis=-1, keepdims=True)
    )


def column_sum(values):
    return jnp.sum(values, axis=0, keepdims=True)


def aligned(start, size):
    if isinstance(start, int):
        return pl.ds(start, size)
    return pl.ds(pl.multiple_of(start, size), size)


def head_mask(odd):
    lanes = lax.broadcasted_iota(jnp.int32, (1, 2 * HD), 1)
    low = jnp.where(lanes < HD, 1.0, 0.0)
    return (low * (1.0 - odd) + (1.0 - low) * odd).astype(BF16)


def staged(count, unrolled, first, rest):
    if unrolled:
        ready = first(0)
        for i in range(count):
            following = first(i + 1) if i + 1 < count else None
            rest(i, ready)
            ready = following
    else:

        @pl.loop(0, count)
        def _(i):
            rest(i, first(i))


WHOLE = pl.BlockSpec(memory_space=pltpu.VMEM)
AFAR = pl.BlockSpec(memory_space=pl.ANY)
SCALARS = pl.BlockSpec(memory_space=pltpu.SMEM)
PARAMS = pltpu.CompilerParams(vmem_limit_bytes=VMEM_BYTES)


def for_count(count, run):
    @pl.when(count <= EVEN)
    def _():
        run(EVEN)

    @pl.when(count > EVEN)
    def _():
        run(MOST)


def split_row(segments):
    length = segments.shape[-1]
    sizes = [jnp.sum((segments == v).astype(jnp.int32)) for v in range(SEGMENTS)]
    best_mask = jnp.int32(0)
    best_cost = jnp.int32(2 * length)
    for mask in range(1 << (SEGMENTS - 1)):
        with_first = sizes[0]
        for v in range(1, SEGMENTS):
            if mask >> (v - 1) & 1:
                with_first = with_first + sizes[v]
        cost = jnp.maximum(with_first, length - with_first)
        better = cost < best_cost
        best_mask = jnp.where(better, mask, best_mask)
        best_cost = jnp.where(better, cost, best_cost)
    return sizes, best_mask, best_cost


def group_targets(segments, half, sizes, mask):
    length = segments.shape[-1]
    start = jnp.int32(0)
    offset = jnp.int32(0)
    shift = jnp.full(segments.shape, 0, jnp.int32)
    for v in range(SEGMENTS):
        bit = jnp.int32(1) if v == 0 else lax.shift_right_logical(mask, v - 1) & 1
        inside = (bit == 1) == (half == 0)
        shift = jnp.where(segments == v, jnp.where(inside, offset - start, -4 * length), shift)
        start = start + sizes[v]
        offset = offset + jnp.where(inside, sizes[v], 0)
    return lax.broadcasted_iota(jnp.int32, segments.shape, 1) + shift


def one_hot(target, capacity):
    slots = lax.broadcasted_iota(jnp.int32, (capacity, target.shape[-1]), 0)
    return jnp.where(slots == target, 1.0, 0.0).astype(BF16)


def put_back(slots, values, core, own, other):
    half = own.shape[0]
    lanes = lax.broadcasted_iota(jnp.int32, (half, values.shape[0]), 1).astype(F32)
    for out, start in ((own, core * half), (other, (1 - core) * half)):
        column = slots[pl.ds(pl.multiple_of(start, half), half), 0:1]
        pick = jnp.where(column == lanes, 1.0, 0.0).astype(BF16)
        out[...] = dot(pick, values).astype(BF16)


BIG = ("w_in", "w_out", "w_up", "w_down")
KEPT = (
    ("x_kept", (MOST, T), BF16),
    ("qkv", (MOST, 3 * T), BF16),
    ("probs", (H, MOST, MOST), BF16),
    ("norms", (H, MOST), F32),
    ("mix_t", (T, MOST), BF16),
    ("s1", (MOST, T), F32),
    ("act", (MOST, 4 * T), BF16),
    ("gate", (MOST, 4 * T), BF16),
    ("s2", (MOST, T), F32),
)


def filled(ref, name, cap, *lead):
    if name == "probs":
        return ref.at[(*lead, slice(None), pl.ds(0, cap), pl.ds(0, cap))]
    if name in ("mix_t", "norms"):
        return ref.at[(*lead, slice(None), pl.ds(0, cap))]
    return ref.at[(*lead, pl.ds(0, cap), slice(None))]


def forward_kernel(positions, place, tokens, cotangent, segments, live, b_up, b_down, gain, shift, *refs):
    big = dict(zip(BIG, refs[:4]))
    names = [name for name, _, _ in KEPT]
    kept = dict(zip(names, refs[4:13]))
    own_last, other_last, g_first, counted, slots = refs[13:18]
    weights = dict(zip(BIG, refs[18:22]))
    held = dict(zip(names, refs[22:31]))
    row_x, row_g, allow, v_t, q_t, nrm, nlow, came, left, rows_came = refs[31:]
    row = place[0]
    half = place[1]
    length = segments.shape[1]
    own_rows = pl.ds(pl.multiple_of(row * length, length), length)
    load_x = pltpu.make_async_copy(tokens.at[own_rows], row_x, rows_came.at[0])
    load_g = pltpu.make_async_copy(cotangent.at[own_rows], row_g, rows_came.at[1])
    load_x.start()

    def weight_copy(i, layer):
        return pltpu.make_async_copy(big[BIG[i]].at[layer], weights[BIG[i]].at[layer], came.at[layer, i])

    for i in range(4):
        weight_copy(i, 0).start()
    load_g.start()
    for i in range(4):
        weight_copy(i, 1).start()

    seg = segments[pl.ds(row, 1), :]
    alive = live[pl.ds(row, 1), :]
    sizes, mask, cost = split_row(seg)
    target = group_targets(seg, half, sizes, mask)
    counted[0] = cost
    slots[...] = jnp.broadcast_to(target.astype(F32), (8, length)).T

    def run(cap):
        x_now, qkv, probs, norms, mix_t, s1, act, gate, s2 = (held[name] for name in names)

        def keep(name, position):
            i = names.index(name)
            return pltpu.make_async_copy(
                filled(held[name], name, cap), filled(kept[name], name, cap, position), left.at[i]
            )

        pick = one_hot(target, cap)
        load_x.wait()
        x_now[0:cap, :] = dot(pick, row_x[...]).astype(BF16)
        rows = lax.broadcasted_iota(jnp.int32, (8, length), 0)
        both = jnp.where(
            rows == 0, (seg + 1).astype(F32), jnp.where(rows == 1, alive.astype(F32), 0.0)
        ).astype(BF16)
        as_rows = dot_nt(both, pick)
        as_columns = dot_nt(pick, both)
        seg_row = as_rows[0:1, :]
        keys = lax.broadcasted_iota(jnp.int32, (cap, cap), 0)
        queries = lax.broadcasted_iota(jnp.int32, (cap, cap), 1)
        itself = keys == queries
        alive_key = (as_columns[:, 1:2] == 1.0) & (seg_row > 0.0)
        allowed = (seg_row == as_columns[:, 0:1]) & (alive_key | itself)
        allow[0:cap, 0:cap] = jnp.where(allowed, 1.0, 0.0).astype(BF16)
        load_g.wait()
        g_first[0:cap, :] = dot(pick, row_g[...]).astype(BF16)
        factor = HD**-0.5 * LOG2E
        tall = HD + ONES
        for i in range(H):
            v_t[i * tall + HD : (i + 1) * tall, 0:cap] = jnp.ones((ONES, cap), BF16)

        @pl.loop(0, positions)
        def _(position):
            layer = lax.rem(position, 2)

            def need(i):
                @pl.when(position < 2)
                def _():
                    weight_copy(i, layer).wait()

            def free(*which):
                @pl.when(position > 0)
                def _():
                    for name in which:
                        keep(name, position - 1).wait()

            keep("x_kept", position).start()
            need(0)
            free("qkv")

            for j in range(3):
                columns = slice(j * T, (j + 1) * T)
                merged = dot(x_now[0:cap, :], weights["w_in"][layer, :, columns])
                qkv[0:cap, columns] = merged.astype(BF16)

            keep("qkv", position).start()
            values = qkv[0:cap, 2 * T : 3 * T].T
            for i in range(H):
                v_t[i * tall : i * tall + HD, 0:cap] = values[i * HD : (i + 1) * HD]
            q_t[:, 0:cap] = qkv[0:cap, 0:T].T
            free("probs", "norms", "mix_t")

            def score(i):
                at = i // 2 * (2 * HD) if isinstance(i, int) else lax.div(i, 2) * (2 * HD)
                keys = qkv[0:cap, aligned(T + at, 2 * HD)] * head_mask(i % 2)
                return dot(keys, q_t[aligned(at, 2 * HD), 0:cap]) * factor

            def mix(i, weight, sums):
                both = dot(v_t[aligned(i * tall, tall), 0:cap], weight)
                inverse = 1.0 / (both[HD : HD + 1] if sums is None else sums)
                mix_t[aligned(i * HD, HD), 0:cap] = (both[0:HD] * inverse).astype(BF16)
                return both[HD : HD + 1], inverse

            def plain_head(i, scores):
                weight = jnp.exp2(scores).astype(BF16) * allow[0:cap, 0:cap]
                probs[i, 0:cap, 0:cap] = weight
                sums, inverse = mix(i, weight, None)
                nrm[pl.ds(i, 1), 0:cap] = sums
                norms[pl.ds(i, 1), 0:cap] = inverse

            staged(H, cap == EVEN, score, plain_head)
            sums = nrm[0:H, 0:cap]
            outside = jnp.where((sums > 1.0 / SAFE) & (sums < SAFE), 0.0, 1.0)

            @pl.when(jnp.sum(outside) > 0.0)
            def _():
                @pl.loop(0, H)
                def _(i):
                    masked = jnp.where(allow[0:cap, 0:cap].astype(F32) > 0.0, score(i), MASKED)
                    weight = jnp.exp2(masked - jnp.max(masked, axis=0, keepdims=True))
                    weight = (weight * (1.0 / column_sum(weight))).astype(BF16)
                    probs[i, 0:cap, 0:cap] = weight
                    one = jnp.ones((1, cap), F32)
                    mix(i, weight, one)
                    norms[pl.ds(i, 1), 0:cap] = one

            keep("probs", position).start()
            keep("norms", position).start()
            keep("mix_t", position).start()
            need(1)
            free("s1")
            summed = x_now[0:cap, :].astype(F32) + dot(mix_t[:, 0:cap].T, weights["w_out"][layer])
            s1[0:cap, :] = summed
            keep("s1", position).start()
            plain, _ = row_stats(summed)
            normed = plain * gain[layer, 0:1, :] + shift[layer, 0:1, :]
            nrm[0:cap, 0:T] = normed
            nlow[0:cap, :] = normed.astype(BF16)
            need(2)
            need(3)
            free("act", "gate")

            def raise_up(t):
                columns = aligned(t * T, T)
                return dot(nlow[0:cap, :], weights["w_up"][layer, :, columns])

            def activate(t, hidden):
                columns = aligned(t * T, T)
                v = hidden + b_up[pl.ds(layer, 1), columns]
                c0 = 0.7978845608028654
                c1 = c0 * 0.044715
                square = v * v
                half_one = 0.5 + 0.5 * jnp.tanh(v * (c0 + c1 * square))
                active = v * half_one
                act[0:cap, columns] = active.astype(BF16)
                slope = half_one + active * (1.0 - half_one) * (2.0 * c0 + 6.0 * c1 * square)
                gate[0:cap, columns] = slope.astype(BF16)

            staged(4, cap == EVEN, raise_up, activate)
            branch = dot(act[0:cap, :], weights["w_down"][layer])
            keep("act", position).start()
            keep("gate", position).start()
            free("s2")
            second = nrm[0:cap, 0:T] + (branch + b_down[pl.ds(layer, 1), :])
            s2[0:cap, :] = second
            keep("s2", position).start()
            plain2, _ = row_stats(second)
            keep("x_kept", position).wait()
            x_now[0:cap, :] = (plain2 * gain[layer, 1:2, :] + shift[layer, 1:2, :]).astype(BF16)

        put_back(slots, x_now[0:cap, :], half, own_last, other_last)
        for name in names[1:]:
            keep(name, positions - 1).wait()

    for_count(cost, run)


def forward(positions, place, tokens, cotangent, segments, live, weights):
    w_in, w_out, w_up, b_up, w_down, b_down, gain, shift = weights
    big = (w_in, w_out, w_up, w_down)
    length = segments.shape[1]

    def body(*refs):
        forward_kernel(positions, *refs)

    return pl.pallas_call(
        body,
        in_specs=[SCALARS, AFAR, AFAR] + [WHOLE] * 6 + [AFAR] * 4,
        out_specs=[AFAR] * len(KEPT) + [WHOLE, WHOLE, WHOLE, SCALARS, WHOLE],
        out_shape=[jax.ShapeDtypeStruct((positions,) + shape, kind) for _, shape, kind in KEPT]
        + [jax.ShapeDtypeStruct((length // 2, T), BF16)] * 2
        + [jax.ShapeDtypeStruct((MOST, T), BF16)]
        + [jax.ShapeDtypeStruct((1,), jnp.int32)]
        + [jax.ShapeDtypeStruct((length, 8), F32)],
        scratch_shapes=[pltpu.VMEM(w.shape, BF16) for w in big]
        + [pltpu.VMEM(shape, kind) for _, shape, kind in KEPT]
        + [
            pltpu.VMEM((length, T), BF16),
            pltpu.VMEM((length, T), BF16),
            pltpu.VMEM((MOST, MOST), BF16),
            pltpu.VMEM((H * (HD + ONES), MOST), BF16),
            pltpu.VMEM((T, MOST), BF16),
            pltpu.VMEM((MOST, max(T, MOST)), F32),
            pltpu.VMEM((MOST, T), BF16),
            pltpu.SemaphoreType.DMA((2, 4)),
            pltpu.SemaphoreType.DMA((len(KEPT),)),
            pltpu.SemaphoreType.DMA((2,)),
        ],
        compiler_params=PARAMS,
        cost_estimate=pl.CostEstimate(flops=60 * 10**9, bytes_accessed=1 << 20, transcendentals=0),
        name="forward",
    )(place, tokens, cotangent, segments, live, b_up, b_down, gain, shift, *big)


FFN_READ = ("s2", "s1", "w_down", "gate", "act", "w_up")
HEADS_READ = ("w_out", "mix_t", "norms", "qkv", "probs")
INPUT_READ = ("x_kept", "w_in")
READ = {
    "ffn": FFN_READ, "heads": HEADS_READ, "input": INPUT_READ, "attn": HEADS_READ + INPUT_READ,
}
FILLED = {"ffn": (0, 1), "heads": (3,), "input": (3, 2), "attn": (3, 2)}


def tile_parts(tile, ways):
    return tile.reshape(ways // 2, 2, T // ways, T)


def each(count, unrolled, body):
    if unrolled:
        for i in range(count):
            body(i)
    else:
        pl.loop(0, count)(body)


class Backward:
    def __init__(self, phases, ways, refs, cap):
        self.phases, self.ways, self.cap = phases, ways, cap
        self.__dict__.update(refs)
        self.wide = T // ways
        self.copies = {}
        self.loaded = set()
        layers = sorted({position % 2 for position, _ in phases})
        self.slot = {layer: i for i, layer in enumerate(layers)}
        self.waits = []
        self.filled_once = set()
        for layer in self.before:
            for which, (source, target) in self.before[layer].items():
                rows = pl.ds(0, source.shape[3])
                target = target.at[:, :, :, rows]
                copy = pltpu.make_async_copy(source, target, self.before_came.at[layer, which])
                self.copies["before", layer, which] = copy

    def start_reads(self, index):
        if index >= len(self.phases):
            return
        position, part = self.phases[index]
        names = list(READ[part])
        if part in ("attn", "heads") and (position, "ffn") not in self.phases:
            names = ["s1"] + names
        for name in names:
            sem = self.came.at[self.names.index(name)]
            source, target = self.sources[name], self.held[name]
            if name.startswith("w_"):
                if (name, position % 2) in self.loaded:
                    continue
                self.loaded.add((name, position % 2))
                source = source.at[position % 2]
                target = self.weight(name, position)
            else:
                source = filled(source, name, self.cap, position)
                target = filled(target, name, self.cap)
            self.copies[name] = pltpu.make_async_copy(source, target, sem)
            self.copies[name].start()
        for i, (source, target) in enumerate(self.handed if part == "input" else ()):
            self.copies["handed", i] = pltpu.make_async_copy(source, target, self.hand.at[i])
            self.copies["handed", i].start()
        for which in FILLED[part]:
            if ("before", position % 2, which) in self.copies:
                self.copies["before", position % 2, which].start()

    def weight(self, name, position):
        return self.held[name].at[self.slot[position % 2]]

    def need(self, *names):
        for name in names:
            if name in self.copies:
                self.copies.pop(name).wait()

    def store(self, layer, which, index, value):
        if which in self.before.get(layer, {}) or (layer, which) in self.filled_once:
            value = value + self.grads[layer][which][index].astype(F32)
        self.grads[layer][which][index] = value.astype(BF16)

    def send(self, layer, which):
        source, sem = self.grads[layer][which], self.left.at[layer, which]
        self.filled_once.add((layer, which))
        if (layer, which) not in self.final:
            copy = pltpu.make_async_copy(source, self.results[layer, which], sem)
            copy.start()
        else:
            start = 0 if which < 2 or (layer, 0) not in self.keys else 2 * self.wide
            rows = pl.ds(start, source.shape[3])
            mine, other = (self.results[layer, role].at[:, :, :, rows] for role in ("mine", "other"))
            copy = pltpu.make_async_copy(source, mine, sem)
            other = pltpu.make_async_copy(source, other, sem)
            core = self.place[1]

            @pl.when(core == which % 2)
            def _():
                copy.start()

            @pl.when(core != which % 2)
            def _():
                other.start()

        self.waits.append(copy)

    def close(self, position, *arrays):
        for which in arrays:
            if self.last_use[position % 2, which] == position:
                self.send(position % 2, which)
            else:
                self.filled_once.add((position % 2, which))

    def incoming(self, position):
        return self.entry if (position, "ffn") == self.phases[0] else self.g_now

    def ends_with(self, position, part):
        return self.phases[-1] == (position, part)

    def with_ffn(self, position):
        return (position, "ffn") in self.phases

    def hand_on(self, i, source, target):
        self.waits.append(pltpu.make_async_copy(source, target, self.hand.at[i]))
        self.waits[-1].start()

    def store_smalls(self):
        below = pl.ds(self.wide, self.extra)
        first, second = self.grads[0][2], self.grads[0][3]
        first[:, :, :, below, :] = jnp.zeros(first.shape[:3] + (self.extra, T), BF16)
        rows = lax.broadcasted_iota(jnp.int32, (self.extra, T), 0)
        for shard in range(self.ways):
            z, y = shard // 2, shard % 2
            lanes = shard * self.wide // 128 * 128
            ups = jnp.zeros((self.extra, T), F32)
            rest = jnp.zeros((self.extra, T), F32)
            for layer in range(2):
                start = shard * 4 * self.wide
                row = self.smalls[layer, start // T : start // T + 1, start % T : start % T + 4 * self.wide]
                row = jnp.concatenate([row, jnp.zeros((1, T - 4 * self.wide), F32)], axis=1)
                ups = jnp.where(rows == layer, row, ups)
                block = self.smalls[layer, :, lanes : lanes + 128]
                for i in range(5):
                    row = jnp.concatenate([block[4 + i : 5 + i], jnp.zeros((1, T - 128), F32)], axis=1)
                    rest = jnp.where(rows == 5 * layer + i, row, rest)
            second[y, 0, z, below, :] = ups.astype(BF16)
            second[y, 1, z, below, :] = rest.astype(BF16)

    def run(self):
        self.last_use = {}
        for position, part in self.phases:
            for which in FILLED[part]:
                self.last_use[position % 2, which] = position
        self.start_reads(0)
        self.start_reads(1)
        for index, (position, part) in enumerate(self.phases):
            getattr(self, part)(position)
            self.start_reads(index + 2)
        for copy in self.waits:
            copy.wait()

    def ffn(self, position):
        cap, layer, wide, ways = self.cap, position % 2, self.wide, self.ways
        rows = slice(0, cap)
        smalls = self.smalls.at[layer]
        g = self.incoming(position)[rows, :].astype(F32)
        self.need("s2")
        plain, inverse = row_stats(self.held["s2"][rows, :])
        smalls[6:7, :] += column_sum(g * plain)
        smalls[8:9, :] += column_sum(g)
        grad_f = norm_back(g, plain, inverse, self.gain[layer, 1:2, :])
        self.gf[rows, :] = grad_f
        grad_branch = grad_f.astype(BF16)
        gb = self.g_now
        gb[rows, :] = grad_branch
        smalls[4:5, :] += column_sum(grad_branch.astype(F32))
        self.need("s1")
        plain1, inverse1 = row_stats(self.held["s1"][rows, :])
        self.n1[rows, :] = plain1
        self.r1[rows, :] = inverse1
        low = (plain1 * self.gain[layer, 0:1, :] + self.shift[layer, 0:1, :]).astype(BF16)
        nl_t = self.d_t.at[0:T]
        nl_t[:, rows] = low.T
        self.need("w_down", "gate", "act", "w_up", ("before", layer, 0), ("before", layer, 1))
        act, gate = self.held["act"], self.held["gate"]
        w_down, w_up = self.weight("w_down", position), self.weight("w_up", position)

        def lower(t):
            return dot_nt(gb[rows, :], w_down[aligned(t * T, T), :])

        def tile(t, da):
            columns = aligned(t * T, T)
            dh = (gate[rows, columns].astype(F32) * da).astype(BF16)
            gate[rows, columns] = dh
            smalls[pl.ds(t, 1), :] += column_sum(dh.astype(F32))
            parts = tile_parts(dot(nl_t[:, rows], dh), ways)
            few = ways // 8
            below = dot_tn(act[rows, columns], gb[rows, :]).reshape(few, 2, 2, 2 * wide, T)
            for y in range(2):
                self.store(layer, 0, (t // 2, y, slice(None), aligned(t % 2 * wide, wide)), parts[:, y])
                for x in range(2):
                    self.store(layer, 1, (y, x, pl.ds(t * few, few)), below[:, y, x])

        staged(4, cap == EVEN, lower, tile)
        self.close(position, 0, 1)
        self.gf[rows, :] = self.gf[rows, :] + dot_nt(gate[rows, :], w_up[...])
        if self.ends_with(position, "ffn"):
            self.hand_on(0, self.gf.at[rows], self.ends[0].at[rows])

    def attn(self, position):
        self.heads(position)
        self.input(position)

    def heads(self, position):
        cap, layer, ways = self.cap, position % 2, self.ways
        rows = slice(0, cap)
        smalls = self.smalls.at[layer]
        if self.with_ffn(position):
            grad_normed = self.gf[rows, :]
            plain1, inverse1 = self.n1[rows, :], self.r1[rows, :]
        else:
            self.need("s1")
            grad_normed = self.entry[rows, :]
            plain1, inverse1 = row_stats(self.held["s1"][rows, :])
        smalls[5:6, :] += column_sum(grad_normed * plain1)
        smalls[7:8, :] += column_sum(grad_normed)
        grad_summed = norm_back(grad_normed, plain1, inverse1, self.gain[layer, 0:1, :])
        self.gf[rows, :] = grad_summed
        if self.ends_with(position, "heads"):
            self.hand_on(0, self.gf.at[rows], self.ends[0].at[rows])
        grad_attn = grad_summed.astype(BF16)
        self.need("w_out", "mix_t", ("before", layer, 3))
        mix_t, qkv, probs = (self.held[name] for name in ("mix_t", "qkv", "probs"))
        parts = tile_parts(dot(mix_t[:, rows], grad_attn), ways)
        for y in range(2):
            self.store(layer, 3, (y, 1, slice(None), pl.ds(0, self.wide)), parts[:, y])
        if self.ends_with(position, "heads"):
            self.close(position, 3)
        dmix_t, d_t = self.dmix_t, self.d_t
        q_t, k_t = d_t.at[0:T], d_t.at[T : 2 * T]
        self.need("norms")
        grad_mixture = dot_nt(self.weight("w_out", position)[...], grad_attn)
        for i in range(H):
            own = slice(i * HD, (i + 1) * HD)
            dmix_t[own, rows] = (grad_mixture[own] * self.held["norms"][i : i + 1, rows]).astype(BF16)
        self.need("qkv")
        q_t[:, rows] = qkv[rows, 0:T].T
        k_t[:, rows] = qkv[rows, T : 2 * T].T
        self.need("probs")

        def grad_probs(i):
            at = i // 2 * (2 * HD) if isinstance(i, int) else lax.div(i, 2) * (2 * HD)
            values = qkv[rows, aligned(2 * T + at, 2 * HD)] * head_mask(i % 2)
            return dot(values, dmix_t[aligned(at, 2 * HD), rows])

        def head(i, dp):
            own = aligned(i * HD, HD)
            do = dmix_t[own, rows]
            delta = column_sum(do.astype(F32) * mix_t[own, rows].astype(F32))
            p = probs[i, rows, rows]
            ds = (p.astype(F32) * (dp - delta)).astype(BF16)
            grad_q = dot(k_t[own, rows], ds) * HD**-0.5
            grad_k = dot_nt(q_t[own, rows], ds) * HD**-0.5
            d_t[own, rows] = grad_q.astype(BF16)
            own_k = aligned(T + i * HD, HD)
            d_t[own_k, rows] = grad_k.astype(BF16)
            own_v = aligned(2 * T + i * HD, HD)
            d_t[own_v, rows] = dot_nt(do, p).astype(BF16)

        staged(H, cap == EVEN, grad_probs, head)
        if self.ends_with(position, "heads"):
            self.hand_on(1, d_t.at[:, rows], self.ends[1].at[:, rows])

    def input(self, position):
        cap, layer, ways, d_t = self.cap, position % 2, self.ways, self.d_t
        rows = slice(0, cap)
        self.need("x_kept", "w_in", ("before", layer, 2), ("before", layer, 3))
        self.need(("handed", 0), ("handed", 1))
        x_t = self.held["x_kept"][rows, :].T
        for j in range(3):
            parts = tile_parts(dot_nt(x_t, d_t[j * T : (j + 1) * T, rows]), ways)
            for y in range(2):
                index = ((j, y) if j < 2 else (y, 0)) + (slice(None), pl.ds(0, self.wide))
                self.store(layer, 2 if j < 2 else 3, index, parts[:, y])
        if self.extra:
            self.store_smalls()
        self.close(position, 2, 3)
        g = (self.gf[rows, :] + dot(self.weight("w_in", position)[...], d_t[:, rows]).T).astype(BF16)
        if self.last:
            put_back(self.slots[0], g, self.place[1], *self.ends)
        else:
            self.g_now[rows, :] = g
            if self.ends_with(position, "attn"):
                self.ends[0][rows, :] = g


class LoopedBackward(Backward):
    first, last_one = 3, 1

    def __init__(self, ways, refs, cap):
        self.ways, self.cap = ways, cap
        self.__dict__.update(refs)
        self.wide = T // ways

    def ends_with(self, position, part):
        return False

    def with_ffn(self, position):
        return True

    def incoming(self, position):
        return self.g_now

    def weight(self, name, position):
        return self.held[name].at[lax.rem(position, 2)]

    def weight_copy(self, name, layer):
        i = self.names.index(name)
        return pltpu.make_async_copy(
            self.sources[name].at[layer], self.held[name].at[layer], self.came.at[layer, i]
        )

    def copy(self, name, position):
        source = filled(self.sources[name], name, self.cap, position)
        target = filled(self.held[name], name, self.cap)
        return pltpu.make_async_copy(source, target, self.came.at[0, self.names.index(name)])

    def start_reads(self, part, position):
        names = READ[part]
        for name in names:
            if name.startswith("w_"):

                @pl.when(position >= self.first - 1)
                def _(name=name):
                    self.weight_copy(name, lax.rem(position, 2)).start()

            else:
                self.copy(name, position).start()

    def need(self, *names):
        for name in names:
            if isinstance(name, tuple):
                continue
            if name.startswith("w_"):

                @pl.when(self.position >= self.first - 1)
                def _(name=name):
                    self.weight_copy(name, lax.rem(self.position, 2)).wait()

            else:
                self.copy(name, self.position).wait()

    def store(self, layer, which, index, value):
        target = self.grads[which].at[layer]
        old = jnp.where(self.position == self.last_one, target[index].astype(F32), 0.0)
        target[index] = (value + old).astype(BF16)

    def out(self, layer, which):
        return pltpu.make_async_copy(
            self.grads[which].at[layer], self.results[layer, which], self.left.at[layer, which]
        )

    def final_out(self, which, role):
        source = self.grads[which].at[1]
        rows = pl.ds(0 if which < 2 else 2 * self.wide, source.shape[3])
        return pltpu.make_async_copy(
            source, self.results[1, role].at[:, :, :, rows], self.left.at[1, which]
        )

    def close(self, position, *arrays):
        core = self.place[1]
        for which in arrays:

            @pl.when(position == 2)
            def _(which=which):
                self.out(0, which).start()

            @pl.when((position == 1) & (core == which % 2))
            def _(which=which):
                self.final_out(which, "mine").start()

            @pl.when((position == 1) & (core != which % 2))
            def _(which=which):
                self.final_out(which, "other").start()

    def run(self):
        rows = slice(0, self.cap)
        self.g_now[rows, :] = self.entry[rows, :]
        self.start_reads("ffn", self.first)
        self.start_reads("attn", self.first)

        @pl.loop(0, self.first - self.last_one + 1)
        def _(step):
            position = self.first - step
            self.position = position
            self.ffn(position)

            @pl.when(position > self.last_one)
            def _():
                self.start_reads("ffn", position - 1)

            self.attn(position)

            @pl.when(position > self.last_one)
            def _():
                self.start_reads("attn", position - 1)

        self.ends[0][rows, :] = self.g_now[rows, :]
        for which in range(4):
            self.out(0, which).wait()
            self.final_out(which, "mine").wait()


def backward(phases, ways, place, count, entry, smalls, given, before, final, after=(), extra=0, looped=False):
    parts = [part for _, part in phases]
    first_part, last_part = parts[0], parts[-1]
    names = ["s1"] if first_part in ("heads", "attn") else []
    for part in parts:
        names += [name for name in READ[part] if name not in names]
    shapes = {name: (shape, kind) for name, shape, kind in KEPT}
    for name in BIG:
        layers = len({position % 2 for position, _ in phases})
        shapes[name] = ((layers,) + given[name].shape[1:], BF16)
    wide = T // ways
    packed = {}
    for position, part in phases:
        for which in sorted(FILLED[part]):
            packed[position % 2, which] = (2, 2, ways // 2, (2 if which < 2 else 1) * wide, T)
    olds = [(layer, which) for layer in before for which in before[layer]]
    n, keys = len(names), list(packed)
    extra_rows = extra
    if extra:
        for key in ((0, 2), (0, 3)):
            packed[key] = packed[key][:3] + (wide + extra, T)
    made = {}
    for layer, which in keys:
        if (layer, which) not in final:
            made[layer, which] = packed[layer, which]
        elif which in (0, 2):
            rows = packed[layer, which][3] + (made[layer, "mine"][3] if (layer, "mine") in made else 0)
            for role in ("mine", "other"):
                made[layer, role] = (2, 2, ways // 2, rows, T)
    last = phases[-1] in ((0, "input"), (0, "attn"))
    half = given["slots"].shape[0] // 2
    entries = [] if first_part == "input" else [entry]
    handed = list(entry) if first_part == "input" else []

    def body(place, count, gain, shift, *refs):
        refs = list(refs)

        def cut(amount):
            part = refs[:amount]
            del refs[:amount]
            return part

        entry_refs = cut(len(entries))
        smalls_in = cut(0 if smalls is None else 1)
        slots = cut(1 if last else 0)
        handed_refs = cut(len(handed))
        cut(len(after))

        def by_layer(keys, values):
            table = {}
            for (layer, which), value in zip(keys, values):
                table.setdefault(layer, {})[which] = value
            return table

        sources = dict(zip(names, cut(n)))
        olds_hbm = by_layer(olds, cut(len(olds)))
        results = dict(zip(made, cut(len(made))))
        smalls_out = cut(1)[0]
        end_refs = cut(len(ends))
        held = dict(zip(names, cut(n)))
        grads = cut(4) if looped else by_layer(keys, cut(len(keys)))
        work = ("g_now", "gf", "n1", "r1", "dmix_t", "d_t")
        sems = ("came", "before_came", "left", "hand")
        table = dict(zip(work + sems, cut(len(work) + len(sems))))
        table.update(
            place=place, gain=gain, shift=shift, smalls=smalls_out, ends=end_refs,
            entry=entry_refs[0] if entry_refs else None, slots=slots, last=last, extra=extra_rows,
            handed=[],
            names=names, sources=sources, held=held, grads=grads, results=results, final=final, keys=keys,
            before={
                layer: {which: (ref, grads[layer][which]) for which, ref in olds_hbm[layer].items()}
                for layer in olds_hbm
            },
        )
        smalls_out[...] = smalls_in[0][...] if smalls_in else jnp.zeros(smalls_out.shape, F32)

        def run(cap):
            own = dict(table)
            if handed_refs:
                rows = pl.ds(0, cap)
                own["handed"] = [
                    (handed_refs[0].at[rows], table["gf"].at[rows]),
                    (handed_refs[1].at[:, rows], table["d_t"].at[:, rows]),
                ]
            (LoopedBackward(ways, own, cap) if looped else Backward(phases, ways, own, cap)).run()

        for_count(count[0], run)

    extras = ([] if smalls is None else [smalls]) + ([given["slots"]] if last else [])
    end_spec = [WHOLE]
    if last:
        ends = [jax.ShapeDtypeStruct((half, T), BF16)] * 2
        end_spec = [WHOLE, WHOLE]
    elif last_part == "heads":
        ends = [jax.ShapeDtypeStruct((MOST, T), F32), jax.ShapeDtypeStruct((3 * T, MOST), BF16)]
        end_spec = [AFAR, AFAR]
    elif last_part == "ffn":
        ends = [jax.ShapeDtypeStruct((MOST, T), F32)]
        end_spec = [AFAR]
    else:
        ends = [jax.ShapeDtypeStruct((MOST, T), BF16)]
    costs = {"attn": 14e9, "ffn": 10e9, "heads": 10e9, "input": 4e9}
    flops = sum(costs[part] for part in parts)
    outs = pl.pallas_call(
        body,
        in_specs=[SCALARS, SCALARS]
        + [WHOLE] * (2 + len(entries) + len(extras))
        + [AFAR] * (len(handed) + len(after) + n + len(olds)),
        out_specs=[AFAR] * len(made) + [WHOLE] + end_spec,
        out_shape=[jax.ShapeDtypeStruct(shape, BF16) for shape in made.values()]
        + [jax.ShapeDtypeStruct((2, SMALL, T), F32)]
        + ends,
        scratch_shapes=[pltpu.VMEM(*shapes[name]) for name in names]
        + (
            [pltpu.VMEM((2,) + packed[0, which], BF16) for which in range(4)]
            if looped
            else [pltpu.VMEM(packed[key], BF16) for key in keys]
        )
        + [
            pltpu.VMEM((MOST, T), BF16),
            pltpu.VMEM((MOST, T), F32),
            pltpu.VMEM((MOST, T), F32),
            pltpu.VMEM((MOST, 1), F32),
            pltpu.VMEM((T, MOST), BF16),
            pltpu.VMEM((3 * T, MOST), BF16),
            pltpu.SemaphoreType.DMA((2, n) if looped else (n,)),
            pltpu.SemaphoreType.DMA((2, 4)),
            pltpu.SemaphoreType.DMA((2, 4)),
            pltpu.SemaphoreType.DMA((2,)),
        ],
        compiler_params=PARAMS,
        cost_estimate=pl.CostEstimate(flops=int(flops), bytes_accessed=1 << 20, transcendentals=0),
        name="backward_" + "_".join(f"{part}{position}" for position, part in phases),
    )(
        place, count, given["gain"], given["shift"], *entries, *extras, *handed, *after,
        *[given[name] for name in names], *[before[layer][which] for layer, which in olds],
    )
    table = dict(zip(made, outs))
    outs = outs[len(made) :]
    return table, outs[0], outs[1] if len(ends) == 1 else outs[1:]


def swap(block, pairs):
    return lax.ppermute(block, ("section", "dp"), pairs)


class Links:
    def __init__(self):
        self.sections = lax.axis_size("section")
        self.ways = lax.axis_size("dp")
        section = lax.axis_index("section")
        self.me = lax.axis_index("dp")
        self.core, self.x, y = section % 2, section // 2, self.me % 2
        self.bits = (self.ways // 2).bit_length() - 1
        one = jnp.where(self.core == 0, self.x, y)
        two = jnp.where(self.core == 0, y, self.x)
        low_first = [self.me // (2 << i) % 2 for i in range(self.bits)]
        self.halves = [one, two] + low_first
        self.token = None
        self.in_order = True
        self.others = []

    def pairs(self, partner):
        every = [(s, d) for s in range(self.sections) for d in range(self.ways)]
        return [
            (s * self.ways + d, partner(s, d)[0] * self.ways + partner(s, d)[1]) for s, d in every
        ]

    def in_dp(self, bits):
        return self.pairs(lambda s, d: (s, d ^ bits))

    def in_section(self, bits):
        return self.pairs(lambda s, d: (s ^ bits, d))

    def step(self, i):
        if i == 0:
            return self.pairs(lambda s, d: (s ^ 2, d) if s % 2 == 0 else (s, d ^ 1))
        if i == 1:
            return self.pairs(lambda s, d: (s, d ^ 1) if s % 2 == 0 else (s ^ 2, d))
        return self.in_dp(1 << (i - 1))

    def place(self, gives, steps_done, ndim):
        order = [0, 1] + list(range(self.bits + 1, 1, -1))
        return [gives[axis] if axis < len(gives) else None for axis in order if axis >= steps_done]

    def sum(self, terms):
        total = 0.0
        for array, index in terms:
            for dim in reversed(range(len(index))):
                if index[dim] is not None:
                    kind, axis = index[dim]
                    half = self.halves[axis]
                    at = half if kind == "keep" else 1 - half
                    array = lax.dynamic_index_in_dim(array, at, dim, keepdims=False)
            total = total + array.astype(F32)
        return total

    def ordered(self, total, last=True):
        for token in self.others + ([] if self.token is None else [self.token]):
            width = token.shape[-1]
            row = lax.slice(token, (0,) * token.ndim, (1,) * (token.ndim - 1) + (width,))
            row = jnp.minimum(jnp.abs(row.reshape(width).astype(F32)), 0.0)
            total = total + (row if width == T else jnp.tile(row, T // width))
        self.others = []
        total = total.astype(BF16)
        if last and self.in_order:
            self.token = total
        return total


class Group:
    def __init__(self, links, mine=None, other=None, groups=()):
        self.links, self.done = links, 0
        if groups:
            self.done = groups[0].done
            sums = [links.ordered(group.total(), group is groups[-1]) for group in groups]
            self.have = [(jnp.concatenate(sums, axis=-2), self.done)]
        else:
            shape = (2, 2) + (2,) * links.bits + mine.shape[3:]
            came = swap(other, links.in_section(1))
            self.have = [(mine.reshape(shape), 0), (came.reshape(shape), 0)]

    def sum(self, wanted):
        return self.links.sum(
            [(array, self.links.place(wanted, done, array.ndim)) for array, done in self.have]
        )

    def keeps(self):
        return [("keep", i) for i in range(self.done)]

    def give(self):
        give = self.links.ordered(self.sum(self.keeps() + [("give", self.done)]))
        came = swap(give, self.links.step(self.done))
        self.done += 1
        self.have.append((came, self.done))
        return give

    def finished(self):
        return self.done == 2 + self.links.bits

    def total(self):
        return self.sum(self.keeps())


def to_sections(links, total):
    over = swap(total, links.in_section(2))
    beside = swap(total, links.in_section(1))
    return [total, beside, over, swap(over, links.in_section(1))]


def spread(links, own, other, came):
    came = [swap(other, links.in_section(1)), came]
    rows, width = own[0].shape[0], own[0].shape[1] // links.sections
    after = [] if links.token is None else [links.token]

    def body(*refs):
        own, came, out = refs[:2], refs[2:4], refs[4 + len(after)]
        for s in range(links.sections):
            at = pl.ds(s * width, width)
            for i in range(2):
                out[s, i] = (own[i][:, at].astype(F32) + came[i][:, at].astype(F32)).astype(BF16)

    gives = pl.pallas_call(
        body,
        in_specs=[WHOLE] * 4 + [AFAR] * len(after),
        out_specs=WHOLE,
        out_shape=jax.ShapeDtypeStruct((links.sections, 2, rows, width), BF16),
        compiler_params=PARAMS,
        name="spread",
    )(*own, *came, *after)
    return lax.all_to_all(gives, "section", 0, 0)


def lay_out(layer, at, pieces, wide, scale, ins, out_proj, ups, downs):
    of = [pieces[s ^ at] for s in range(4)]
    own = pl.ds(2 * wide, wide)
    for x in range(2):
        for i in range(2):
            rows = pl.ds(i * wide, wide)
            columns = pl.ds((2 * x + i) * T, T)
            ups[:, columns] = of[2 * x][rows, :].astype(F32) * scale
        downs[pl.ds(2 * x * wide, 2 * wide), :] = of[2 * x + 1][0 : 2 * wide, :].astype(F32) * scale
        ins[:, pl.ds(x * T, T)] = of[2 * x][own, :].astype(F32) * scale
    ins[:, pl.ds(2 * T, T)] = of[1][own, :].astype(F32) * scale
    out_proj[...] = of[3][own, :].astype(F32) * scale


def big_shapes(wide):
    return [(wide, 3 * T), (wide, T), (wide, 4 * T), (4 * wide, T)]


def gather_early(place, blocks, pieces, ways):
    wide = T // ways
    _, _, half, width = blocks.shape
    shapes = big_shapes(wide)

    def body(place, *refs):
        blocks, pieces, outs = refs[0], refs[1:5], refs[5:11]
        made, sems = refs[11:15], refs[15]
        section = 2 * place[0] + place[1]
        for at in range(4):

            @pl.when(section == at)
            def _(at=at):
                lay_out(1, at, pieces, wide, 1.0 / ways, *made)

        copies = [
            pltpu.make_async_copy(made[i], outs[2 + i].at[1], sems.at[i]) for i in range(4)
        ]
        for copy in copies:
            copy.start()
        for s in range(4):
            rows = pl.ds(s * half, half)
            outs[1][rows, :] = blocks[s, 0]
            outs[0][rows, :] = blocks[s, 1]
        for copy in copies:
            copy.wait()

    return pl.pallas_call(
        body,
        in_specs=[SCALARS] + [WHOLE] * 5,
        out_specs=[WHOLE] * 2 + [AFAR] * 4,
        out_shape=[jax.ShapeDtypeStruct((4 * half, width), BF16)] * 2
        + [jax.ShapeDtypeStruct((2,) + shape, F32) for shape in shapes],
        scratch_shapes=[pltpu.VMEM(shape, F32) for shape in shapes]
        + [pltpu.SemaphoreType.DMA((4,))],
        compiler_params=PARAMS,
        cost_estimate=pl.CostEstimate(flops=5 * 10**9, bytes_accessed=1 << 20, transcendentals=0),
        name="gather_early",
    )(place, blocks, *pieces)


def gather_late(place, sums, pieces, begun, ways, extra):
    wide = T // ways
    scale = 1.0 / ways
    shapes = big_shapes(wide)

    def body(place, sums, *refs):
        pieces, outs = refs[:4], refs[8:12]
        up_bias, down_bias, gains, shifts = refs[12:16]
        made, sems = refs[16:20], refs[20]
        section = 2 * place[0] + place[1]
        me = place[2]

        def small_rows(layer, row, rest):
            up_bias[layer : layer + 1, :] = row[0:1, 0 : 4 * wide]
            down_bias[layer : layer + 1, :] = rest[0:1, 0:wide]
            gains[layer] = rest[1:3, 0:wide]
            shifts[layer] = rest[3:5, 0:wide]

        for at in range(4):

            @pl.when(section == at)
            def _(at=at):
                lay_out(0, at, pieces, wide, scale, *made)

        copies = [
            pltpu.make_async_copy(made[i], outs[i].at[0], sems.at[i]) for i in range(4)
        ]
        for copy in copies:
            copy.start()
        if extra:
            for at in range(4):

                @pl.when(section == at)
                def _(at=at):
                    below = pl.ds(3 * wide, extra)
                    row = pieces[1 ^ at][below, :].astype(F32) * scale
                    rest = pieces[3 ^ at][below, 0:128].astype(F32) * scale
                    turn = lax.rem(me * wide, 128)
                    rest = pltpu.roll(rest, lax.rem(128 - turn, 128), 1)
                    for layer in range(2):
                        small_rows(layer, row[layer : layer + 1], rest[5 * layer : 5 * layer + 5])

        else:
            for layer in range(2):
                start = me * (4 * wide)
                row = sums[layer, pl.ds(lax.div(start, T), 1), :] * scale
                row = jnp.broadcast_to(row, (8, T))
                row = pltpu.roll(row, lax.rem(T - lax.rem(start, T), T), 1)
                rest = pltpu.roll(sums[layer] * scale, lax.rem(T - me * wide, T), 1)
                small_rows(layer, row, rest[4:9])
        for copy in copies:
            copy.wait()

    small_shapes = [(2, 4 * wide), (2, wide), (2, 2, wide), (2, 2, wide)]
    return pl.pallas_call(
        body,
        in_specs=[SCALARS] + [WHOLE] * 5 + [AFAR] * 4,
        out_specs=[AFAR] * 4 + [WHOLE] * 4,
        out_shape=[jax.ShapeDtypeStruct((2,) + shape, F32) for shape in shapes]
        + [jax.ShapeDtypeStruct(shape, F32) for shape in small_shapes],
        input_output_aliases={6 + i: i for i in range(4)},
        scratch_shapes=[pltpu.VMEM(shape, F32) for shape in shapes]
        + [pltpu.SemaphoreType.DMA((4,))],
        compiler_params=PARAMS,
        name="gather_late",
    )(place, sums, *pieces, *begun)


def finer(block, kind, ways):
    made = 2 * block.shape[2]
    cut = ways // made
    if cut == 1:
        return block
    z, rows = block.shape[2:4]
    if kind == "down":
        block = block.transpose(2, 0, 1, 3, 4).reshape(z, 2, cut // 2, 2, 2, rows // cut, T)
        block = block.transpose(3, 4, 0, 1, 2, 5, 6)
    elif kind == "right":
        block = block.reshape(2, 2, z, cut // 2, 2, rows // cut, T).transpose(4, 1, 2, 0, 3, 5, 6)
    else:
        tiles = 2 if kind == "up" else 1
        block = block.reshape(2, 2, z, tiles, cut // 2, 2, rows // tiles // cut, T)
        block = block.transpose(0, 5, 2, 1, 4, 3, 6, 7)
    return block.reshape(2, 2, ways // 2, rows // cut, T)


def finer_pair(links, arrays, kinds):
    mine, other = arrays
    if 2 * mine.shape[2] == links.ways:
        return arrays
    wide = T // (2 * mine.shape[2])

    def cut(block, which):
        parts, start = [], 0
        for kind in kinds:
            rows = (2 if kind[0] == "up" else 1) * wide
            parts.append(finer(block[:, :, :, start : start + rows], kind[which], links.ways))
            start += rows
        return jnp.concatenate(parts, axis=3)

    return (
        jnp.where(links.core == 0, cut(mine, 0), cut(mine, 1)),
        jnp.where(links.core == 0, cut(other, 1), cut(other, 0)),
    )


def on_device(
    tokens, segment_ids, live_mask, cotangent,
    project_in, project_out, up_weight, up_bias, down_weight, down_bias, norm_gain, norm_shift,
):
    ways = lax.axis_size("dp")
    positions = lax.axis_size("section")
    made = min(ways, T // 32)
    links = Links()
    place = jnp.stack([links.x, links.core, links.me]).astype(jnp.int32)
    weights = (
        project_in, project_out, up_weight, up_bias, down_weight, down_bias, norm_gain, norm_shift,
    )
    *kept, own, other, g, count, slots = forward(
        positions, place, tokens, cotangent, segment_ids, live_mask, weights
    )
    given = dict(zip((name for name, _, _ in KEPT), kept))
    given.update(
        w_in=project_in, w_out=project_out, w_up=up_weight, w_down=down_weight,
        gain=norm_gain, shift=norm_shift, slots=slots,
    )
    extra = SMALL if made == ways else 0
    came = swap(other, links.in_section(1))
    of_ffn, of_attn = ("up", "down"), ("left", "right")

    def group(arrays, layer, kinds):
        return Group(links, *finer_pair(links, (arrays[layer, "mine"], arrays[layer, "other"]), kinds))

    def back(phases, entry, smalls, before, final=(), after=(), extra=0, looped=False):
        return backward(
            phases, made, place, count, entry, smalls, given, before, final, after, extra, looped
        )

    early = [(position, part) for position in (3, 2, 1) for part in ("ffn", "attn")]
    finals = ((1, 0), (1, 1), (1, 2), (1, 3))
    grads, smalls, g = back(early, g, None, {}, finals, looped=True)
    all_1 = group(grads, 1, (of_ffn, of_attn))
    before = {0: {0: grads[0, 0], 1: grads[0, 1]}}
    ffn, smalls, g = back([(0, "ffn")], g, smalls, before, ((0, 0), (0, 1)))
    ffn_0 = group(ffn, 0, (of_ffn,))
    after = [all_1.give()]
    before = {0: {2: grads[0, 2], 3: grads[0, 3]}}
    attn, smalls, halves = back([(0, "attn")], g, smalls, before, ((0, 2), (0, 3)), after, extra)
    attn_0 = group(attn, 0, (of_attn,))
    all_1.give()
    ffn_0.give()
    attn_0.give()
    all_1.give()
    ffn_0.give()
    attn_0.give()
    blocks = spread(links, (halves[0], own), halves[1], came)
    while not all_1.finished():
        all_1.give()
        ffn_0.give()
        attn_0.give()
    pieces_1 = to_sections(links, links.ordered(all_1.total()))
    links.others = [blocks]
    while not (attn_0.finished() and ffn_0.finished()):
        for last in (ffn_0, attn_0):
            if not last.finished():
                last.give()
    mixed_out, tokens_out, *begun = gather_early(place, blocks, pieces_1, ways)
    both = Group(links, groups=(ffn_0, attn_0))
    links.others = [pieces_1[2]]
    pieces_0 = to_sections(links, links.ordered(both.total()))
    if not extra:
        smalls = lax.psum(smalls, ("section", "dp"))
    outs = gather_late(place, smalls, pieces_0, begun, ways, extra)
    big, (up_sum, down_sum, gains, shifts) = outs[:4], outs[4:]
    return (mixed_out, tokens_out, big[0], big[1], big[2], up_sum, big[3], down_sum, gains, shifts)


def solution(mesh):
    rows = P("dp", None)
    in_specs = (rows,) * 4 + (P(),) * 8
    out_specs = (
        P("dp", "section"),
        P("dp", "section"),
        P(None, "dp", None),
        P(None, "dp", None),
        P(None, "dp", None),
        P(None, "dp"),
        P(None, "dp", None),
        P(None, "dp"),
        P(None, None, "dp"),
        P(None, None, "dp"),
    )
    return jax.shard_map(
        on_device, mesh=mesh, in_specs=in_specs, out_specs=out_specs, check_vma=False
    )
```

```python
import jax
import jax.numpy as jnp
from jax import lax
from jax.experimental import pallas as pl
from jax.experimental.pallas import tpu as pltpu
from jax.sharding import PartitionSpec as P

H = 8
HD = 64
T = 512
SEGMENTS = 4
EVEN, MOST = 512, 768
SMALL = 16
EPS = 1e-05
MASKED = -1e30
SAFE = 2.0**60
ONES = 16
LOG2E = 1.4426950408889634
F32 = jnp.float32
BF16 = jnp.bfloat16
VMEM_BYTES = 62 * 1024 * 1024


def dot(a, b):
    return jnp.dot(a, b, preferred_element_type=F32)


def dot_nt(a, b):
    return lax.dot_general(a, b, (((1,), (1,)), ((), ())), preferred_element_type=F32)


def dot_tn(a, b):
    return lax.dot_general(a, b, (((0,), (0,)), ((), ())), preferred_element_type=F32)


def row_stats(values):
    center = values - jnp.mean(values, axis=-1, keepdims=True)
    spread = jnp.mean(center * center, axis=-1, keepdims=True)
    inverse = lax.rsqrt(spread + EPS)
    return center * inverse, inverse


def norm_back(grad, plain, inverse, gain):
    scaled = grad * gain
    return inverse * (
        scaled
        - jnp.mean(scaled, axis=-1, keepdims=True)
        - plain * jnp.mean(scaled * plain, axis=-1, keepdims=True)
    )


def column_sum(values):
    return jnp.sum(values, axis=0, keepdims=True)


def aligned(start, size):
    if isinstance(start, int):
        return pl.ds(start, size)
    return pl.ds(pl.multiple_of(start, size), size)


def head_mask(odd):
    lanes = lax.broadcasted_iota(jnp.int32, (1, 2 * HD), 1)
    low = jnp.where(lanes < HD, 1.0, 0.0)
    return (low * (1.0 - odd) + (1.0 - low) * odd).astype(BF16)


def staged(count, unrolled, first, rest):
    if unrolled:
        ready = first(0)
        for i in range(count):
            following = first(i + 1) if i + 1 < count else None
            rest(i, ready)
            ready = following
    else:

        @pl.loop(0, count)
        def _(i):
            rest(i, first(i))


WHOLE = pl.BlockSpec(memory_space=pltpu.VMEM)
AFAR = pl.BlockSpec(memory_space=pl.ANY)
SCALARS = pl.BlockSpec(memory_space=pltpu.SMEM)
PARAMS = pltpu.CompilerParams(vmem_limit_bytes=VMEM_BYTES)


def for_count(count, run):
    @pl.when(count <= EVEN)
    def _():
        run(EVEN)

    @pl.when(count > EVEN)
    def _():
        run(MOST)


def split_row(segments):
    length = segments.shape[-1]
    sizes = [jnp.sum((segments == v).astype(jnp.int32)) for v in range(SEGMENTS)]
    best_mask = jnp.int32(0)
    best_cost = jnp.int32(2 * length)
    for mask in range(1 << (SEGMENTS - 1)):
        with_first = sizes[0]
        for v in range(1, SEGMENTS):
            if mask >> (v - 1) & 1:
                with_first = with_first + sizes[v]
        cost = jnp.maximum(with_first, length - with_first)
        better = cost < best_cost
        best_mask = jnp.where(better, mask, best_mask)
        best_cost = jnp.where(better, cost, best_cost)
    return sizes, best_mask, best_cost


def group_targets(segments, half, sizes, mask):
    length = segments.shape[-1]
    start = jnp.int32(0)
    offset = jnp.int32(0)
    shift = jnp.full(segments.shape, 0, jnp.int32)
    for v in range(SEGMENTS):
        bit = jnp.int32(1) if v == 0 else lax.shift_right_logical(mask, v - 1) & 1
        inside = (bit == 1) == (half == 0)
        shift = jnp.where(segments == v, jnp.where(inside, offset - start, -4 * length), shift)
        start = start + sizes[v]
        offset = offset + jnp.where(inside, sizes[v], 0)
    return lax.broadcasted_iota(jnp.int32, segments.shape, 1) + shift


def one_hot(target, capacity):
    slots = lax.broadcasted_iota(jnp.int32, (capacity, target.shape[-1]), 0)
    return jnp.where(slots == target, 1.0, 0.0).astype(BF16)


def put_back(slots, values, core, own, other):
    half = own.shape[0]
    lanes = lax.broadcasted_iota(jnp.int32, (half, values.shape[0]), 1).astype(F32)
    for out, start in ((own, core * half), (other, (1 - core) * half)):
        column = slots[pl.ds(pl.multiple_of(start, half), half), 0:1]
        pick = jnp.where(column == lanes, 1.0, 0.0).astype(BF16)
        out[...] = dot(pick, values).astype(BF16)


BIG = ("w_in", "w_out", "w_up", "w_down")
KEPT = (
    ("x_kept", (MOST, T), BF16),
    ("qkv", (MOST, 3 * T), BF16),
    ("probs", (H, MOST, MOST), BF16),
    ("norms", (H, MOST), F32),
    ("mix_t", (T, MOST), BF16),
    ("s1", (MOST, T), F32),
    ("act", (MOST, 4 * T), BF16),
    ("gate", (MOST, 4 * T), BF16),
    ("s2", (MOST, T), F32),
)


def filled(ref, name, cap, *lead):
    if name == "probs":
        return ref.at[(*lead, slice(None), pl.ds(0, cap), pl.ds(0, cap))]
    if name in ("mix_t", "norms"):
        return ref.at[(*lead, slice(None), pl.ds(0, cap))]
    return ref.at[(*lead, pl.ds(0, cap), slice(None))]


def forward_kernel(positions, place, tokens, cotangent, segments, live, b_up, b_down, gain, shift, *refs):
    big = dict(zip(BIG, refs[:4]))
    names = [name for name, _, _ in KEPT]
    kept = dict(zip(names, refs[4:13]))
    own_last, other_last, g_first, counted, slots = refs[13:18]
    weights = dict(zip(BIG, refs[18:22]))
    held = dict(zip(names, refs[22:31]))
    row_x, row_g, allow, v_t, q_t, nrm, nlow, came, left, rows_came = refs[31:]
    row = place[0]
    half = place[1]
    length = segments.shape[1]
    own_rows = pl.ds(pl.multiple_of(row * length, length), length)
    load_x = pltpu.make_async_copy(tokens.at[own_rows], row_x, rows_came.at[0])
    load_g = pltpu.make_async_copy(cotangent.at[own_rows], row_g, rows_came.at[1])
    load_x.start()

    def weight_copy(i, layer):
        return pltpu.make_async_copy(big[BIG[i]].at[layer], weights[BIG[i]].at[layer], came.at[layer, i])

    for i in range(4):
        weight_copy(i, 0).start()
    load_g.start()
    for i in range(4):
        weight_copy(i, 1).start()

    seg = segments[pl.ds(row, 1), :]
    alive = live[pl.ds(row, 1), :]
    sizes, mask, cost = split_row(seg)
    target = group_targets(seg, half, sizes, mask)
    counted[0] = cost
    slots[...] = jnp.broadcast_to(target.astype(F32), (8, length)).T

    def run(cap):
        x_now, qkv, probs, norms, mix_t, s1, act, gate, s2 = (held[name] for name in names)

        def keep(name, position):
            i = names.index(name)
            return pltpu.make_async_copy(
                filled(held[name], name, cap), filled(kept[name], name, cap, position), left.at[i]
            )

        pick = one_hot(target, cap)
        load_x.wait()
        x_now[0:cap, :] = dot(pick, row_x[...]).astype(BF16)
        rows = lax.broadcasted_iota(jnp.int32, (8, length), 0)
        both = jnp.where(
            rows == 0, (seg + 1).astype(F32), jnp.where(rows == 1, alive.astype(F32), 0.0)
        ).astype(BF16)
        as_rows = dot_nt(both, pick)
        as_columns = dot_nt(pick, both)
        seg_row = as_rows[0:1, :]
        keys = lax.broadcasted_iota(jnp.int32, (cap, cap), 0)
        queries = lax.broadcasted_iota(jnp.int32, (cap, cap), 1)
        itself = keys == queries
        alive_key = (as_columns[:, 1:2] == 1.0) & (seg_row > 0.0)
        allowed = (seg_row == as_columns[:, 0:1]) & (alive_key | itself)
        allow[0:cap, 0:cap] = jnp.where(allowed, 1.0, 0.0).astype(BF16)
        load_g.wait()
        g_first[0:cap, :] = dot(pick, row_g[...]).astype(BF16)
        factor = HD**-0.5 * LOG2E
        tall = HD + ONES
        for i in range(H):
            v_t[i * tall + HD : (i + 1) * tall, 0:cap] = jnp.ones((ONES, cap), BF16)

        @pl.loop(0, positions)
        def _(position):
            layer = lax.rem(position, 2)

            def need(i):
                @pl.when(position < 2)
                def _():
                    weight_copy(i, layer).wait()

            def free(*which):
                @pl.when(position > 0)
                def _():
                    for name in which:
                        keep(name, position - 1).wait()

            keep("x_kept", position).start()
            need(0)
            free("qkv")

            for j in range(3):
                columns = slice(j * T, (j + 1) * T)
                merged = dot(x_now[0:cap, :], weights["w_in"][layer, :, columns])
                qkv[0:cap, columns] = merged.astype(BF16)

            keep("qkv", position).start()
            values = qkv[0:cap, 2 * T : 3 * T].T
            for i in range(H):
                v_t[i * tall : i * tall + HD, 0:cap] = values[i * HD : (i + 1) * HD]
            q_t[:, 0:cap] = qkv[0:cap, 0:T].T
            free("probs", "norms", "mix_t")

            def score(i):
                at = i // 2 * (2 * HD) if isinstance(i, int) else lax.div(i, 2) * (2 * HD)
                keys = qkv[0:cap, aligned(T + at, 2 * HD)] * head_mask(i % 2)
                return dot(keys, q_t[aligned(at, 2 * HD), 0:cap]) * factor

            def mix(i, weight, sums):
                both = dot(v_t[aligned(i * tall, tall), 0:cap], weight)
                inverse = 1.0 / (both[HD : HD + 1] if sums is None else sums)
                mix_t[aligned(i * HD, HD), 0:cap] = (both[0:HD] * inverse).astype(BF16)
                return both[HD : HD + 1], inverse

            def plain_head(i, scores):
                weight = jnp.exp2(scores).astype(BF16) * allow[0:cap, 0:cap]
                probs[i, 0:cap, 0:cap] = weight
                sums, inverse = mix(i, weight, None)
                nrm[pl.ds(i, 1), 0:cap] = sums
                norms[pl.ds(i, 1), 0:cap] = inverse

            staged(H, cap == EVEN, score, plain_head)
            sums = nrm[0:H, 0:cap]
            outside = jnp.where((sums > 1.0 / SAFE) & (sums < SAFE), 0.0, 1.0)

            @pl.when(jnp.sum(outside) > 0.0)
            def _():
                @pl.loop(0, H)
                def _(i):
                    masked = jnp.where(allow[0:cap, 0:cap].astype(F32) > 0.0, score(i), MASKED)
                    weight = jnp.exp2(masked - jnp.max(masked, axis=0, keepdims=True))
                    weight = (weight * (1.0 / column_sum(weight))).astype(BF16)
                    probs[i, 0:cap, 0:cap] = weight
                    one = jnp.ones((1, cap), F32)
                    mix(i, weight, one)
                    norms[pl.ds(i, 1), 0:cap] = one

            keep("probs", position).start()
            keep("norms", position).start()
            keep("mix_t", position).start()
            need(1)
            free("s1")
            summed = x_now[0:cap, :].astype(F32) + dot(mix_t[:, 0:cap].T, weights["w_out"][layer])
            s1[0:cap, :] = summed
            keep("s1", position).start()
            plain, _ = row_stats(summed)
            normed = plain * gain[layer, 0:1, :] + shift[layer, 0:1, :]
            nrm[0:cap, 0:T] = normed
            nlow[0:cap, :] = normed.astype(BF16)
            need(2)
            need(3)
            free("act", "gate")

            def raise_up(t):
                columns = aligned(t * T, T)
                return dot(nlow[0:cap, :], weights["w_up"][layer, :, columns])

            def activate(t, hidden):
                columns = aligned(t * T, T)
                v = hidden + b_up[pl.ds(layer, 1), columns]
                c0 = 0.7978845608028654
                c1 = c0 * 0.044715
                square = v * v
                half_one = 0.5 + 0.5 * jnp.tanh(v * (c0 + c1 * square))
                active = v * half_one
                act[0:cap, columns] = active.astype(BF16)
                slope = half_one + active * (1.0 - half_one) * (2.0 * c0 + 6.0 * c1 * square)
                gate[0:cap, columns] = slope.astype(BF16)

            staged(4, cap == EVEN, raise_up, activate)
            branch = dot(act[0:cap, :], weights["w_down"][layer])
            keep("act", position).start()
            keep("gate", position).start()
            free("s2")
            second = nrm[0:cap, 0:T] + (branch + b_down[pl.ds(layer, 1), :])
            s2[0:cap, :] = second
            keep("s2", position).start()
            plain2, _ = row_stats(second)
            keep("x_kept", position).wait()
            x_now[0:cap, :] = (plain2 * gain[layer, 1:2, :] + shift[layer, 1:2, :]).astype(BF16)

        put_back(slots, x_now[0:cap, :], half, own_last, other_last)
        for name in names[1:]:
            keep(name, positions - 1).wait()

    for_count(cost, run)


def forward(positions, place, tokens, cotangent, segments, live, weights):
    w_in, w_out, w_up, b_up, w_down, b_down, gain, shift = weights
    big = (w_in, w_out, w_up, w_down)
    length = segments.shape[1]

    def body(*refs):
        forward_kernel(positions, *refs)

    return pl.pallas_call(
        body,
        in_specs=[SCALARS, AFAR, AFAR] + [WHOLE] * 6 + [AFAR] * 4,
        out_specs=[AFAR] * len(KEPT) + [WHOLE, WHOLE, WHOLE, SCALARS, WHOLE],
        out_shape=[jax.ShapeDtypeStruct((positions,) + shape, kind) for _, shape, kind in KEPT]
        + [jax.ShapeDtypeStruct((length // 2, T), BF16)] * 2
        + [jax.ShapeDtypeStruct((MOST, T), BF16)]
        + [jax.ShapeDtypeStruct((1,), jnp.int32)]
        + [jax.ShapeDtypeStruct((length, 8), F32)],
        scratch_shapes=[pltpu.VMEM(w.shape, BF16) for w in big]
        + [pltpu.VMEM(shape, kind) for _, shape, kind in KEPT]
        + [
            pltpu.VMEM((length, T), BF16),
            pltpu.VMEM((length, T), BF16),
            pltpu.VMEM((MOST, MOST), BF16),
            pltpu.VMEM((H * (HD + ONES), MOST), BF16),
            pltpu.VMEM((T, MOST), BF16),
            pltpu.VMEM((MOST, max(T, MOST)), F32),
            pltpu.VMEM((MOST, T), BF16),
            pltpu.SemaphoreType.DMA((2, 4)),
            pltpu.SemaphoreType.DMA((len(KEPT),)),
            pltpu.SemaphoreType.DMA((2,)),
        ],
        compiler_params=PARAMS,
        cost_estimate=pl.CostEstimate(flops=60 * 10**9, bytes_accessed=1 << 20, transcendentals=0),
        name="forward",
    )(place, tokens, cotangent, segments, live, b_up, b_down, gain, shift, *big)


FFN_READ = ("s2", "s1", "w_down", "gate", "act", "w_up")
HEADS_READ = ("w_out", "mix_t", "norms", "qkv", "probs")
INPUT_READ = ("x_kept", "w_in")
READ = {
    "ffn": FFN_READ, "heads": HEADS_READ, "input": INPUT_READ, "attn": HEADS_READ + INPUT_READ,
}
FILLED = {"ffn": (0, 1), "heads": (3,), "input": (3, 2), "attn": (3, 2)}


def tile_parts(tile, ways):
    return tile.reshape(ways // 2, 2, T // ways, T)


def each(count, unrolled, body):
    if unrolled:
        for i in range(count):
            body(i)
    else:
        pl.loop(0, count)(body)


class Backward:
    def __init__(self, phases, ways, refs, cap):
        self.phases, self.ways, self.cap = phases, ways, cap
        self.__dict__.update(refs)
        self.wide = T // ways
        self.copies = {}
        self.loaded = set()
        layers = sorted({position % 2 for position, _ in phases})
        self.slot = {layer: i for i, layer in enumerate(layers)}
        self.waits = []
        self.filled_once = set()
        for layer in self.before:
            for which, (source, target) in self.before[layer].items():
                rows = pl.ds(0, source.shape[3])
                target = target.at[:, :, :, rows]
                copy = pltpu.make_async_copy(source, target, self.before_came.at[layer, which])
                self.copies["before", layer, which] = copy

    def start_reads(self, index):
        if index >= len(self.phases):
            return
        position, part = self.phases[index]
        names = list(READ[part])
        if part in ("attn", "heads") and (position, "ffn") not in self.phases:
            names = ["s1"] + names
        for name in names:
            sem = self.came.at[self.names.index(name)]
            source, target = self.sources[name], self.held[name]
            if name.startswith("w_"):
                if (name, position % 2) in self.loaded:
                    continue
                self.loaded.add((name, position % 2))
                source = source.at[position % 2]
                target = self.weight(name, position)
            else:
                source = filled(source, name, self.cap, position)
                target = filled(target, name, self.cap)
            self.copies[name] = pltpu.make_async_copy(source, target, sem)
            self.copies[name].start()
        for i, (source, target) in enumerate(self.handed if part == "input" else ()):
            self.copies["handed", i] = pltpu.make_async_copy(source, target, self.hand.at[i])
            self.copies["handed", i].start()
        for which in FILLED[part]:
            if ("before", position % 2, which) in self.copies:
                self.copies["before", position % 2, which].start()

    def weight(self, name, position):
        return self.held[name].at[self.slot[position % 2]]

    def need(self, *names):
        for name in names:
            if name in self.copies:
                self.copies.pop(name).wait()

    def store(self, layer, which, index, value):
        if which in self.before.get(layer, {}) or (layer, which) in self.filled_once:
            value = value + self.grads[layer][which][index].astype(F32)
        self.grads[layer][which][index] = value.astype(BF16)

    def send(self, layer, which):
        source, sem = self.grads[layer][which], self.left.at[layer, which]
        self.filled_once.add((layer, which))
        if (layer, which) not in self.final:
            copy = pltpu.make_async_copy(source, self.results[layer, which], sem)
            copy.start()
        else:
            start = 0 if which < 2 or (layer, 0) not in self.keys else 2 * self.wide
            rows = pl.ds(start, source.shape[3])
            mine, other = (self.results[layer, role].at[:, :, :, rows] for role in ("mine", "other"))
            copy = pltpu.make_async_copy(source, mine, sem)
            other = pltpu.make_async_copy(source, other, sem)
            core = self.place[1]

            @pl.when(core == which % 2)
            def _():
                copy.start()

            @pl.when(core != which % 2)
            def _():
                other.start()

        self.waits.append(copy)

    def close(self, position, *arrays):
        for which in arrays:
            if self.last_use[position % 2, which] == position:
                self.send(position % 2, which)
            else:
                self.filled_once.add((position % 2, which))

    def incoming(self, position):
        return self.entry if (position, "ffn") == self.phases[0] else self.g_now

    def ends_with(self, position, part):
        return self.phases[-1] == (position, part)

    def with_ffn(self, position):
        return (position, "ffn") in self.phases

    def hand_on(self, i, source, target):
        self.waits.append(pltpu.make_async_copy(source, target, self.hand.at[i]))
        self.waits[-1].start()

    def store_smalls(self):
        below = pl.ds(self.wide, self.extra)
        first, second = self.grads[0][2], self.grads[0][3]
        first[:, :, :, below, :] = jnp.zeros(first.shape[:3] + (self.extra, T), BF16)
        rows = lax.broadcasted_iota(jnp.int32, (self.extra, T), 0)
        for shard in range(self.ways):
            z, y = shard // 2, shard % 2
            lanes = shard * self.wide // 128 * 128
            ups = jnp.zeros((self.extra, T), F32)
            rest = jnp.zeros((self.extra, T), F32)
            for layer in range(2):
                start = shard * 4 * self.wide
                row = self.smalls[layer, start // T : start // T + 1, start % T : start % T + 4 * self.wide]
                row = jnp.concatenate([row, jnp.zeros((1, T - 4 * self.wide), F32)], axis=1)
                ups = jnp.where(rows == layer, row, ups)
                block = self.smalls[layer, :, lanes : lanes + 128]
                for i in range(5):
                    row = jnp.concatenate([block[4 + i : 5 + i], jnp.zeros((1, T - 128), F32)], axis=1)
                    rest = jnp.where(rows == 5 * layer + i, row, rest)
            second[y, 0, z, below, :] = ups.astype(BF16)
            second[y, 1, z, below, :] = rest.astype(BF16)

    def run(self):
        self.last_use = {}
        for position, part in self.phases:
            for which in FILLED[part]:
                self.last_use[position % 2, which] = position
        self.start_reads(0)
        self.start_reads(1)
        for index, (position, part) in enumerate(self.phases):
            getattr(self, part)(position)
            self.start_reads(index + 2)
        for copy in self.waits:
            copy.wait()

    def ffn(self, position):
        cap, layer, wide, ways = self.cap, position % 2, self.wide, self.ways
        rows = slice(0, cap)
        smalls = self.smalls.at[layer]
        g = self.incoming(position)[rows, :].astype(F32)
        self.need("s2")
        plain, inverse = row_stats(self.held["s2"][rows, :])
        smalls[6:7, :] += column_sum(g * plain)
        smalls[8:9, :] += column_sum(g)
        grad_f = norm_back(g, plain, inverse, self.gain[layer, 1:2, :])
        self.gf[rows, :] = grad_f
        grad_branch = grad_f.astype(BF16)
        gb = self.g_now
        gb[rows, :] = grad_branch
        smalls[4:5, :] += column_sum(grad_branch.astype(F32))
        self.need("s1")
        plain1, inverse1 = row_stats(self.held["s1"][rows, :])
        self.n1[rows, :] = plain1
        self.r1[rows, :] = inverse1
        low = (plain1 * self.gain[layer, 0:1, :] + self.shift[layer, 0:1, :]).astype(BF16)
        nl_t = self.d_t.at[0:T]
        nl_t[:, rows] = low.T
        self.need("w_down", "gate", "act", "w_up", ("before", layer, 0), ("before", layer, 1))
        act, gate = self.held["act"], self.held["gate"]
        w_down, w_up = self.weight("w_down", position), self.weight("w_up", position)

        def lower(t):
            return dot_nt(gb[rows, :], w_down[aligned(t * T, T), :])

        def tile(t, da):
            columns = aligned(t * T, T)
            dh = (gate[rows, columns].astype(F32) * da).astype(BF16)
            gate[rows, columns] = dh
            smalls[pl.ds(t, 1), :] += column_sum(dh.astype(F32))
            parts = tile_parts(dot(nl_t[:, rows], dh), ways)
            few = ways // 8
            below = dot_tn(act[rows, columns], gb[rows, :]).reshape(few, 2, 2, 2 * wide, T)
            for y in range(2):
                self.store(layer, 0, (t // 2, y, slice(None), aligned(t % 2 * wide, wide)), parts[:, y])
                for x in range(2):
                    self.store(layer, 1, (y, x, pl.ds(t * few, few)), below[:, y, x])

        staged(4, cap == EVEN, lower, tile)
        self.close(position, 0, 1)
        self.gf[rows, :] = self.gf[rows, :] + dot_nt(gate[rows, :], w_up[...])
        if self.ends_with(position, "ffn"):
            self.hand_on(0, self.gf.at[rows], self.ends[0].at[rows])

    def attn(self, position):
        self.heads(position)
        self.input(position)

    def heads(self, position):
        cap, layer, ways = self.cap, position % 2, self.ways
        rows = slice(0, cap)
        smalls = self.smalls.at[layer]
        if self.with_ffn(position):
            grad_normed = self.gf[rows, :]
            plain1, inverse1 = self.n1[rows, :], self.r1[rows, :]
        else:
            self.need("s1")
            grad_normed = self.entry[rows, :]
            plain1, inverse1 = row_stats(self.held["s1"][rows, :])
        smalls[5:6, :] += column_sum(grad_normed * plain1)
        smalls[7:8, :] += column_sum(grad_normed)
        grad_summed = norm_back(grad_normed, plain1, inverse1, self.gain[layer, 0:1, :])
        self.gf[rows, :] = grad_summed
        if self.ends_with(position, "heads"):
            self.hand_on(0, self.gf.at[rows], self.ends[0].at[rows])
        grad_attn = grad_summed.astype(BF16)
        self.need("w_out", "mix_t", ("before", layer, 3))
        mix_t, qkv, probs = (self.held[name] for name in ("mix_t", "qkv", "probs"))
        parts = tile_parts(dot(mix_t[:, rows], grad_attn), ways)
        for y in range(2):
            self.store(layer, 3, (y, 1, slice(None), pl.ds(0, self.wide)), parts[:, y])
        if self.ends_with(position, "heads"):
            self.close(position, 3)
        dmix_t, d_t = self.dmix_t, self.d_t
        q_t, k_t = d_t.at[0:T], d_t.at[T : 2 * T]
        self.need("norms")
        grad_mixture = dot_nt(self.weight("w_out", position)[...], grad_attn)
        for i in range(H):
            own = slice(i * HD, (i + 1) * HD)
            dmix_t[own, rows] = (grad_mixture[own] * self.held["norms"][i : i + 1, rows]).astype(BF16)
        self.need("qkv")
        q_t[:, rows] = qkv[rows, 0:T].T
        k_t[:, rows] = qkv[rows, T : 2 * T].T
        self.need("probs")

        def grad_probs(i):
            at = i // 2 * (2 * HD) if isinstance(i, int) else lax.div(i, 2) * (2 * HD)
            values = qkv[rows, aligned(2 * T + at, 2 * HD)] * head_mask(i % 2)
            return dot(values, dmix_t[aligned(at, 2 * HD), rows])

        def head(i, dp):
            own = aligned(i * HD, HD)
            do = dmix_t[own, rows]
            delta = column_sum(do.astype(F32) * mix_t[own, rows].astype(F32))
            p = probs[i, rows, rows]
            ds = (p.astype(F32) * (dp - delta)).astype(BF16)
            grad_q = dot(k_t[own, rows], ds) * HD**-0.5
            grad_k = dot_nt(q_t[own, rows], ds) * HD**-0.5
            d_t[own, rows] = grad_q.astype(BF16)
            own_k = aligned(T + i * HD, HD)
            d_t[own_k, rows] = grad_k.astype(BF16)
            own_v = aligned(2 * T + i * HD, HD)
            d_t[own_v, rows] = dot_nt(do, p).astype(BF16)

        staged(H, cap == EVEN, grad_probs, head)
        if self.ends_with(position, "heads"):
            self.hand_on(1, d_t.at[:, rows], self.ends[1].at[:, rows])

    def input(self, position):
        cap, layer, ways, d_t = self.cap, position % 2, self.ways, self.d_t
        rows = slice(0, cap)
        self.need("x_kept", "w_in", ("before", layer, 2), ("before", layer, 3))
        self.need(("handed", 0), ("handed", 1))
        x_t = self.held["x_kept"][rows, :].T
        for j in range(3):
            parts = tile_parts(dot_nt(x_t, d_t[j * T : (j + 1) * T, rows]), ways)
            for y in range(2):
                index = ((j, y) if j < 2 else (y, 0)) + (slice(None), pl.ds(0, self.wide))
                self.store(layer, 2 if j < 2 else 3, index, parts[:, y])
        if self.extra:
            self.store_smalls()
        self.close(position, 2, 3)
        g = (self.gf[rows, :] + dot(self.weight("w_in", position)[...], d_t[:, rows]).T).astype(BF16)
        if self.last:
            put_back(self.slots[0], g, self.place[1], *self.ends)
        else:
            self.g_now[rows, :] = g
            if self.ends_with(position, "attn"):
                self.ends[0][rows, :] = g


class LoopedBackward(Backward):
    first, last_one = 3, 1

    def __init__(self, ways, refs, cap):
        self.ways, self.cap = ways, cap
        self.__dict__.update(refs)
        self.wide = T // ways

    def ends_with(self, position, part):
        return False

    def with_ffn(self, position):
        return True

    def incoming(self, position):
        return self.g_now

    def weight(self, name, position):
        return self.held[name].at[lax.rem(position, 2)]

    def weight_copy(self, name, layer):
        i = self.names.index(name)
        return pltpu.make_async_copy(
            self.sources[name].at[layer], self.held[name].at[layer], self.came.at[layer, i]
        )

    def copy(self, name, position):
        source = filled(self.sources[name], name, self.cap, position)
        target = filled(self.held[name], name, self.cap)
        return pltpu.make_async_copy(source, target, self.came.at[0, self.names.index(name)])

    def start_reads(self, part, position):
        names = READ[part]
        for name in names:
            if name.startswith("w_"):

                @pl.when(position >= self.first - 1)
                def _(name=name):
                    self.weight_copy(name, lax.rem(position, 2)).start()

            else:
                self.copy(name, position).start()

    def need(self, *names):
        for name in names:
            if isinstance(name, tuple):
                continue
            if name.startswith("w_"):

                @pl.when(self.position >= self.first - 1)
                def _(name=name):
                    self.weight_copy(name, lax.rem(self.position, 2)).wait()

            else:
                self.copy(name, self.position).wait()

    def store(self, layer, which, index, value):
        target = self.grads[which].at[layer]
        old = jnp.where(self.position == self.last_one, target[index].astype(F32), 0.0)
        target[index] = (value + old).astype(BF16)

    def out(self, layer, which):
        return pltpu.make_async_copy(
            self.grads[which].at[layer], self.results[layer, which], self.left.at[layer, which]
        )

    def final_out(self, which, role):
        source = self.grads[which].at[1]
        rows = pl.ds(0 if which < 2 else 2 * self.wide, source.shape[3])
        return pltpu.make_async_copy(
            source, self.results[1, role].at[:, :, :, rows], self.left.at[1, which]
        )

    def close(self, position, *arrays):
        core = self.place[1]
        for which in arrays:

            @pl.when(position == 2)
            def _(which=which):
                self.out(0, which).start()

            @pl.when((position == 1) & (core == which % 2))
            def _(which=which):
                self.final_out(which, "mine").start()

            @pl.when((position == 1) & (core != which % 2))
            def _(which=which):
                self.final_out(which, "other").start()

    def run(self):
        rows = slice(0, self.cap)
        self.g_now[rows, :] = self.entry[rows, :]
        self.start_reads("ffn", self.first)
        self.start_reads("attn", self.first)

        @pl.loop(0, self.first - self.last_one + 1)
        def _(step):
            position = self.first - step
            self.position = position
            self.ffn(position)

            @pl.when(position > self.last_one)
            def _():
                self.start_reads("ffn", position - 1)

            self.attn(position)

            @pl.when(position > self.last_one)
            def _():
                self.start_reads("attn", position - 1)

        self.ends[0][rows, :] = self.g_now[rows, :]
        for which in range(4):
            self.out(0, which).wait()
            self.final_out(which, "mine").wait()


def backward(phases, ways, place, count, entry, smalls, given, before, final, after=(), extra=0, looped=False):
    parts = [part for _, part in phases]
    first_part, last_part = parts[0], parts[-1]
    names = ["s1"] if first_part in ("heads", "attn") else []
    for part in parts:
        names += [name for name in READ[part] if name not in names]
    shapes = {name: (shape, kind) for name, shape, kind in KEPT}
    for name in BIG:
        layers = len({position % 2 for position, _ in phases})
        shapes[name] = ((layers,) + given[name].shape[1:], BF16)
    wide = T // ways
    packed = {}
    for position, part in phases:
        for which in sorted(FILLED[part]):
            packed[position % 2, which] = (2, 2, ways // 2, (2 if which < 2 else 1) * wide, T)
    olds = [(layer, which) for layer in before for which in before[layer]]
    n, keys = len(names), list(packed)
    extra_rows = extra
    if extra:
        for key in ((0, 2), (0, 3)):
            packed[key] = packed[key][:3] + (wide + extra, T)
    made = {}
    for layer, which in keys:
        if (layer, which) not in final:
            made[layer, which] = packed[layer, which]
        elif which in (0, 2):
            rows = packed[layer, which][3] + (made[layer, "mine"][3] if (layer, "mine") in made else 0)
            for role in ("mine", "other"):
                made[layer, role] = (2, 2, ways // 2, rows, T)
    last = phases[-1] in ((0, "input"), (0, "attn"))
    half = given["slots"].shape[0] // 2
    entries = [] if first_part == "input" else [entry]
    handed = list(entry) if first_part == "input" else []

    def body(place, count, gain, shift, *refs):
        refs = list(refs)

        def cut(amount):
            part = refs[:amount]
            del refs[:amount]
            return part

        entry_refs = cut(len(entries))
        smalls_in = cut(0 if smalls is None else 1)
        slots = cut(1 if last else 0)
        handed_refs = cut(len(handed))
        cut(len(after))

        def by_layer(keys, values):
            table = {}
            for (layer, which), value in zip(keys, values):
                table.setdefault(layer, {})[which] = value
            return table

        sources = dict(zip(names, cut(n)))
        olds_hbm = by_layer(olds, cut(len(olds)))
        results = dict(zip(made, cut(len(made))))
        smalls_out = cut(1)[0]
        end_refs = cut(len(ends))
        held = dict(zip(names, cut(n)))
        grads = cut(4) if looped else by_layer(keys, cut(len(keys)))
        work = ("g_now", "gf", "n1", "r1", "dmix_t", "d_t")
        sems = ("came", "before_came", "left", "hand")
        table = dict(zip(work + sems, cut(len(work) + len(sems))))
        table.update(
            place=place, gain=gain, shift=shift, smalls=smalls_out, ends=end_refs,
            entry=entry_refs[0] if entry_refs else None, slots=slots, last=last, extra=extra_rows,
            handed=[],
            names=names, sources=sources, held=held, grads=grads, results=results, final=final, keys=keys,
            before={
                layer: {which: (ref, grads[layer][which]) for which, ref in olds_hbm[layer].items()}
                for layer in olds_hbm
            },
        )
        smalls_out[...] = smalls_in[0][...] if smalls_in else jnp.zeros(smalls_out.shape, F32)

        def run(cap):
            own = dict(table)
            if handed_refs:
                rows = pl.ds(0, cap)
                own["handed"] = [
                    (handed_refs[0].at[rows], table["gf"].at[rows]),
                    (handed_refs[1].at[:, rows], table["d_t"].at[:, rows]),
                ]
            (LoopedBackward(ways, own, cap) if looped else Backward(phases, ways, own, cap)).run()

        for_count(count[0], run)

    extras = ([] if smalls is None else [smalls]) + ([given["slots"]] if last else [])
    end_spec = [WHOLE]
    if last:
        ends = [jax.ShapeDtypeStruct((half, T), BF16)] * 2
        end_spec = [WHOLE, WHOLE]
    elif last_part == "heads":
        ends = [jax.ShapeDtypeStruct((MOST, T), F32), jax.ShapeDtypeStruct((3 * T, MOST), BF16)]
        end_spec = [AFAR, AFAR]
    elif last_part == "ffn":
        ends = [jax.ShapeDtypeStruct((MOST, T), F32)]
        end_spec = [AFAR]
    else:
        ends = [jax.ShapeDtypeStruct((MOST, T), BF16)]
    costs = {"attn": 14e9, "ffn": 10e9, "heads": 10e9, "input": 4e9}
    flops = sum(costs[part] for part in parts)
    outs = pl.pallas_call(
        body,
        in_specs=[SCALARS, SCALARS]
        + [WHOLE] * (2 + len(entries) + len(extras))
        + [AFAR] * (len(handed) + len(after) + n + len(olds)),
        out_specs=[AFAR] * len(made) + [WHOLE] + end_spec,
        out_shape=[jax.ShapeDtypeStruct(shape, BF16) for shape in made.values()]
        + [jax.ShapeDtypeStruct((2, SMALL, T), F32)]
        + ends,
        scratch_shapes=[pltpu.VMEM(*shapes[name]) for name in names]
        + (
            [pltpu.VMEM((2,) + packed[0, which], BF16) for which in range(4)]
            if looped
            else [pltpu.VMEM(packed[key], BF16) for key in keys]
        )
        + [
            pltpu.VMEM((MOST, T), BF16),
            pltpu.VMEM((MOST, T), F32),
            pltpu.VMEM((MOST, T), F32),
            pltpu.VMEM((MOST, 1), F32),
            pltpu.VMEM((T, MOST), BF16),
            pltpu.VMEM((3 * T, MOST), BF16),
            pltpu.SemaphoreType.DMA((2, n) if looped else (n,)),
            pltpu.SemaphoreType.DMA((2, 4)),
            pltpu.SemaphoreType.DMA((2, 4)),
            pltpu.SemaphoreType.DMA((2,)),
        ],
        compiler_params=PARAMS,
        cost_estimate=pl.CostEstimate(flops=int(flops), bytes_accessed=1 << 20, transcendentals=0),
        name="backward_" + "_".join(f"{part}{position}" for position, part in phases),
    )(
        place, count, given["gain"], given["shift"], *entries, *extras, *handed, *after,
        *[given[name] for name in names], *[before[layer][which] for layer, which in olds],
    )
    table = dict(zip(made, outs))
    outs = outs[len(made) :]
    return table, outs[0], outs[1] if len(ends) == 1 else outs[1:]


def swap(block, pairs):
    return lax.ppermute(block, ("section", "dp"), pairs)


class Links:
    def __init__(self):
        self.sections = lax.axis_size("section")
        self.ways = lax.axis_size("dp")
        section = lax.axis_index("section")
        self.me = lax.axis_index("dp")
        self.core, self.x, y = section % 2, section // 2, self.me % 2
        self.bits = (self.ways // 2).bit_length() - 1
        one = jnp.where(self.core == 0, self.x, y)
        two = jnp.where(self.core == 0, y, self.x)
        low_first = [self.me // (2 << i) % 2 for i in range(self.bits)]
        self.halves = [one, two] + low_first
        self.token = None
        self.in_order = True
        self.others = []

    def pairs(self, partner):
        every = [(s, d) for s in range(self.sections) for d in range(self.ways)]
        return [
            (s * self.ways + d, partner(s, d)[0] * self.ways + partner(s, d)[1]) for s, d in every
        ]

    def in_dp(self, bits):
        return self.pairs(lambda s, d: (s, d ^ bits))

    def in_section(self, bits):
        return self.pairs(lambda s, d: (s ^ bits, d))

    def step(self, i):
        if i == 0:
            return self.pairs(lambda s, d: (s ^ 2, d) if s % 2 == 0 else (s, d ^ 1))
        if i == 1:
            return self.pairs(lambda s, d: (s, d ^ 1) if s % 2 == 0 else (s ^ 2, d))
        return self.in_dp(1 << (i - 1))

    def place(self, gives, steps_done, ndim):
        order = [0, 1] + list(range(self.bits + 1, 1, -1))
        return [gives[axis] if axis < len(gives) else None for axis in order if axis >= steps_done]

    def sum(self, terms):
        total = 0.0
        for array, index in terms:
            for dim in reversed(range(len(index))):
                if index[dim] is not None:
                    kind, axis = index[dim]
                    half = self.halves[axis]
                    at = half if kind == "keep" else 1 - half
                    array = lax.dynamic_index_in_dim(array, at, dim, keepdims=False)
            total = total + array.astype(F32)
        return total

    def ordered(self, total, last=True):
        for token in self.others + ([] if self.token is None else [self.token]):
            width = token.shape[-1]
            row = lax.slice(token, (0,) * token.ndim, (1,) * (token.ndim - 1) + (width,))
            row = jnp.minimum(jnp.abs(row.reshape(width).astype(F32)), 0.0)
            total = total + (row if width == T else jnp.tile(row, T // width))
        self.others = []
        total = total.astype(BF16)
        if last and self.in_order:
            self.token = total
        return total


class Group:
    def __init__(self, links, mine=None, other=None, groups=()):
        self.links, self.done = links, 0
        if groups:
            self.done = groups[0].done
            sums = [links.ordered(group.total(), group is groups[-1]) for group in groups]
            self.have = [(jnp.concatenate(sums, axis=-2), self.done)]
        else:
            shape = (2, 2) + (2,) * links.bits + mine.shape[3:]
            came = swap(other, links.in_section(1))
            self.have = [(mine.reshape(shape), 0), (came.reshape(shape), 0)]

    def sum(self, wanted):
        return self.links.sum(
            [(array, self.links.place(wanted, done, array.ndim)) for array, done in self.have]
        )

    def keeps(self):
        return [("keep", i) for i in range(self.done)]

    def give(self):
        give = self.links.ordered(self.sum(self.keeps() + [("give", self.done)]))
        came = swap(give, self.links.step(self.done))
        self.done += 1
        self.have.append((came, self.done))
        return give

    def finished(self):
        return self.done == 2 + self.links.bits

    def total(self):
        return self.sum(self.keeps())


def to_sections(links, total):
    over = swap(total, links.in_section(2))
    beside = swap(total, links.in_section(1))
    return [total, beside, over, swap(over, links.in_section(1))]


def spread(links, own, other, came):
    came = [swap(other, links.in_section(1)), came]
    rows, width = own[0].shape[0], own[0].shape[1] // links.sections
    after = [] if links.token is None else [links.token]

    def body(*refs):
        own, came, out = refs[:2], refs[2:4], refs[4 + len(after)]
        for s in range(links.sections):
            at = pl.ds(s * width, width)
            for i in range(2):
                out[s, i] = (own[i][:, at].astype(F32) + came[i][:, at].astype(F32)).astype(BF16)

    gives = pl.pallas_call(
        body,
        in_specs=[WHOLE] * 4 + [AFAR] * len(after),
        out_specs=WHOLE,
        out_shape=jax.ShapeDtypeStruct((links.sections, 2, rows, width), BF16),
        compiler_params=PARAMS,
        name="spread",
    )(*own, *came, *after)
    return lax.all_to_all(gives, "section", 0, 0)


def lay_out(layer, at, pieces, wide, scale, ins, out_proj, ups, downs):
    of = [pieces[s ^ at] for s in range(4)]
    own = pl.ds(2 * wide, wide)
    for x in range(2):
        for i in range(2):
            rows = pl.ds(i * wide, wide)
            columns = pl.ds((2 * x + i) * T, T)
            ups[:, columns] = of[2 * x][rows, :].astype(F32) * scale
        downs[pl.ds(2 * x * wide, 2 * wide), :] = of[2 * x + 1][0 : 2 * wide, :].astype(F32) * scale
        ins[:, pl.ds(x * T, T)] = of[2 * x][own, :].astype(F32) * scale
    ins[:, pl.ds(2 * T, T)] = of[1][own, :].astype(F32) * scale
    out_proj[...] = of[3][own, :].astype(F32) * scale


def big_shapes(wide):
    return [(wide, 3 * T), (wide, T), (wide, 4 * T), (4 * wide, T)]


def gather_early(place, blocks, pieces, ways):
    wide = T // ways
    _, _, half, width = blocks.shape
    shapes = big_shapes(wide)

    def body(place, *refs):
        blocks, pieces, outs = refs[0], refs[1:5], refs[5:11]
        made, sems = refs[11:15], refs[15]
        section = 2 * place[0] + place[1]
        for at in range(4):

            @pl.when(section == at)
            def _(at=at):
                lay_out(1, at, pieces, wide, 1.0 / ways, *made)

        copies = [
            pltpu.make_async_copy(made[i], outs[2 + i].at[1], sems.at[i]) for i in range(4)
        ]
        for copy in copies:
            copy.start()
        for s in range(4):
            rows = pl.ds(s * half, half)
            outs[1][rows, :] = blocks[s, 0]
            outs[0][rows, :] = blocks[s, 1]
        for copy in copies:
            copy.wait()

    return pl.pallas_call(
        body,
        in_specs=[SCALARS] + [WHOLE] * 5,
        out_specs=[WHOLE] * 2 + [AFAR] * 4,
        out_shape=[jax.ShapeDtypeStruct((4 * half, width), BF16)] * 2
        + [jax.ShapeDtypeStruct((2,) + shape, F32) for shape in shapes],
        scratch_shapes=[pltpu.VMEM(shape, F32) for shape in shapes]
        + [pltpu.SemaphoreType.DMA((4,))],
        compiler_params=PARAMS,
        cost_estimate=pl.CostEstimate(flops=5 * 10**9, bytes_accessed=1 << 20, transcendentals=0),
        name="gather_early",
    )(place, blocks, *pieces)


def gather_late(place, sums, pieces, begun, ways, extra):
    wide = T // ways
    scale = 1.0 / ways
    shapes = big_shapes(wide)

    def body(place, sums, *refs):
        pieces, outs = refs[:4], refs[8:12]
        up_bias, down_bias, gains, shifts = refs[12:16]
        made, sems = refs[16:20], refs[20]
        section = 2 * place[0] + place[1]
        me = place[2]

        def small_rows(layer, row, rest):
            up_bias[layer : layer + 1, :] = row[0:1, 0 : 4 * wide]
            down_bias[layer : layer + 1, :] = rest[0:1, 0:wide]
            gains[layer] = rest[1:3, 0:wide]
            shifts[layer] = rest[3:5, 0:wide]

        for at in range(4):

            @pl.when(section == at)
            def _(at=at):
                lay_out(0, at, pieces, wide, scale, *made)

        copies = [
            pltpu.make_async_copy(made[i], outs[i].at[0], sems.at[i]) for i in range(4)
        ]
        for copy in copies:
            copy.start()
        if extra:
            for at in range(4):

                @pl.when(section == at)
                def _(at=at):
                    below = pl.ds(3 * wide, extra)
                    row = pieces[1 ^ at][below, :].astype(F32) * scale
                    rest = pieces[3 ^ at][below, 0:128].astype(F32) * scale
                    turn = lax.rem(me * wide, 128)
                    rest = pltpu.roll(rest, lax.rem(128 - turn, 128), 1)
                    for layer in range(2):
                        small_rows(layer, row[layer : layer + 1], rest[5 * layer : 5 * layer + 5])

        else:
            for layer in range(2):
                start = me * (4 * wide)
                row = sums[layer, pl.ds(lax.div(start, T), 1), :] * scale
                row = jnp.broadcast_to(row, (8, T))
                row = pltpu.roll(row, lax.rem(T - lax.rem(start, T), T), 1)
                rest = pltpu.roll(sums[layer] * scale, lax.rem(T - me * wide, T), 1)
                small_rows(layer, row, rest[4:9])
        for copy in copies:
            copy.wait()

    small_shapes = [(2, 4 * wide), (2, wide), (2, 2, wide), (2, 2, wide)]
    return pl.pallas_call(
        body,
        in_specs=[SCALARS] + [WHOLE] * 5 + [AFAR] * 4,
        out_specs=[AFAR] * 4 + [WHOLE] * 4,
        out_shape=[jax.ShapeDtypeStruct((2,) + shape, F32) for shape in shapes]
        + [jax.ShapeDtypeStruct(shape, F32) for shape in small_shapes],
        input_output_aliases={6 + i: i for i in range(4)},
        scratch_shapes=[pltpu.VMEM(shape, F32) for shape in shapes]
        + [pltpu.SemaphoreType.DMA((4,))],
        compiler_params=PARAMS,
        name="gather_late",
    )(place, sums, *pieces, *begun)


def finer(block, kind, ways):
    made = 2 * block.shape[2]
    cut = ways // made
    if cut == 1:
        return block
    z, rows = block.shape[2:4]
    if kind == "down":
        block = block.transpose(2, 0, 1, 3, 4).reshape(z, 2, cut // 2, 2, 2, rows // cut, T)
        block = block.transpose(3, 4, 0, 1, 2, 5, 6)
    elif kind == "right":
        block = block.reshape(2, 2, z, cut // 2, 2, rows // cut, T).transpose(4, 1, 2, 0, 3, 5, 6)
    else:
        tiles = 2 if kind == "up" else 1
        block = block.reshape(2, 2, z, tiles, cut // 2, 2, rows // tiles // cut, T)
        block = block.transpose(0, 5, 2, 1, 4, 3, 6, 7)
    return block.reshape(2, 2, ways // 2, rows // cut, T)


def finer_pair(links, arrays, kinds):
    mine, other = arrays
    if 2 * mine.shape[2] == links.ways:
        return arrays
    wide = T // (2 * mine.shape[2])

    def cut(block, which):
        parts, start = [], 0
        for kind in kinds:
            rows = (2 if kind[0] == "up" else 1) * wide
            parts.append(finer(block[:, :, :, start : start + rows], kind[which], links.ways))
            start += rows
        return jnp.concatenate(parts, axis=3)

    return (
        jnp.where(links.core == 0, cut(mine, 0), cut(mine, 1)),
        jnp.where(links.core == 0, cut(other, 1), cut(other, 0)),
    )


def on_device(
    tokens, segment_ids, live_mask, cotangent,
    project_in, project_out, up_weight, up_bias, down_weight, down_bias, norm_gain, norm_shift,
):
    ways = lax.axis_size("dp")
    positions = lax.axis_size("section")
    made = min(ways, T // 32)
    links = Links()
    place = jnp.stack([links.x, links.core, links.me]).astype(jnp.int32)
    weights = (
        project_in, project_out, up_weight, up_bias, down_weight, down_bias, norm_gain, norm_shift,
    )
    *kept, own, other, g, count, slots = forward(
        positions, place, tokens, cotangent, segment_ids, live_mask, weights
    )
    given = dict(zip((name for name, _, _ in KEPT), kept))
    given.update(
        w_in=project_in, w_out=project_out, w_up=up_weight, w_down=down_weight,
        gain=norm_gain, shift=norm_shift, slots=slots,
    )
    extra = SMALL if made == ways else 0
    came = swap(other, links.in_section(1))
    of_ffn, of_attn = ("up", "down"), ("left", "right")

    def group(arrays, layer, kinds):
        return Group(links, *finer_pair(links, (arrays[layer, "mine"], arrays[layer, "other"]), kinds))

    def back(phases, entry, smalls, before, final=(), after=(), extra=0, looped=False):
        return backward(
            phases, made, place, count, entry, smalls, given, before, final, after, extra, looped
        )

    early = [(position, part) for position in (3, 2, 1) for part in ("ffn", "attn")]
    finals = ((1, 0), (1, 1), (1, 2), (1, 3))
    grads, smalls, g = back(early, g, None, {}, finals, looped=True)
    all_1 = group(grads, 1, (of_ffn, of_attn))
    before = {0: {0: grads[0, 0], 1: grads[0, 1]}}
    ffn, smalls, g = back([(0, "ffn")], g, smalls, before, ((0, 0), (0, 1)))
    ffn_0 = group(ffn, 0, (of_ffn,))
    after = [all_1.give()]
    before = {0: {2: grads[0, 2], 3: grads[0, 3]}}
    attn, smalls, halves = back([(0, "attn")], g, smalls, before, ((0, 2), (0, 3)), after, extra)
    attn_0 = group(attn, 0, (of_attn,))
    all_1.give()
    ffn_0.give()
    attn_0.give()
    all_1.give()
    ffn_0.give()
    attn_0.give()
    blocks = spread(links, (halves[0], own), halves[1], came)
    while not all_1.finished():
        all_1.give()
        ffn_0.give()
        attn_0.give()
    pieces_1 = to_sections(links, links.ordered(all_1.total()))
    links.others = [blocks]
    while not (attn_0.finished() and ffn_0.finished()):
        for last in (ffn_0, attn_0):
            if not last.finished():
                last.give()
    mixed_out, tokens_out, *begun = gather_early(place, blocks, pieces_1, ways)
    both = Group(links, groups=(ffn_0, attn_0))
    links.others = [mixed_out]
    pieces_0 = to_sections(links, links.ordered(both.total()))
    if not extra:
        smalls = lax.psum(smalls, ("section", "dp"))
    outs = gather_late(place, smalls, pieces_0, begun, ways, extra)
    big, (up_sum, down_sum, gains, shifts) = outs[:4], outs[4:]
    return (mixed_out, tokens_out, big[0], big[1], big[2], up_sum, big[3], down_sum, gains, shifts)


def solution(mesh):
    rows = P("dp", None)
    in_specs = (rows,) * 4 + (P(),) * 8
    out_specs = (
        P("dp", "section"),
        P("dp", "section"),
        P(None, "dp", None),
        P(None, "dp", None),
        P(None, "dp", None),
        P(None, "dp"),
        P(None, "dp", None),
        P(None, "dp"),
        P(None, None, "dp"),
        P(None, None, "dp"),
    )
    return jax.shard_map(
        on_device, mesh=mesh, in_specs=in_specs, out_specs=out_specs, check_vma=False
    )
```
